32 devices in a mesh: fsdp: 4 (over z), ctx: 4 (over x, core), tp: 2 (over y).
Axes of the slice: x: 2, y: 2, z: 4, core: 2. Of those that a mesh axis runs over, the one named last changes fastest.
Arguments:
- inputs: bfloat16 [8192, 1536], P(('fsdp', 'ctx')), may hold values from -6 to 6
- cotangent: bfloat16 [8192, 1536], P(('fsdp', 'ctx', 'tp')), may hold values from -6 to 6
- routes: int32 [8192, 8], P(('fsdp', 'ctx')), may hold values from 0 to 31, all different within a row; in each aligned block of 256 rows (0 to 255, 256 to 511, ...) at most 96 rows name the same one
- segment_ids: int32 [4, 2048], P('fsdp'), may hold values from 0 to 12, as said below
- parents: int32 [4, 13], P('fsdp'), may hold values from 0 to 11, as said below
- w_qkv: float32 [1536, 2560], P(('fsdp', 'ctx'), 'tp'), may hold values from -0.15625 to 0.15625
- w_out: float32 [1536, 1536], P('tp', ('fsdp', 'ctx')), may hold values from -1.25 to 1.25
- w_router: float32 [1536, 32], P(('fsdp', 'ctx')), may hold values from -0.15625 to 0.15625
- w_gate_up: float32 [32, 1536, 1024], P(('fsdp', 'tp'), 'ctx'), may hold values from -0.15625 to 0.15625
- w_down: float32 [32, 512, 1536], P(('fsdp', 'tp'), None, 'ctx'), may hold values from -0.25 to 0.25
- gain_attn: float32 [1536], P(('fsdp', 'ctx')), may hold values from 0.5 to 1.5
- gain_moe: float32 [1536], P(('fsdp', 'ctx')), may hold values from 0.5 to 1.5
- row_qkv: float32 [1536], replicated, may hold values from 27 to 9830, as said below
- col_qkv: float32 [2560], replicated, may hold values from 163 to 1638
- row_out: float32 [1536], replicated, may hold values from 163 to 1638
- col_out: float32 [1536], replicated, may hold values from 27 to 9830, as said below
- row_router: float32 [1536], replicated, may hold values from 27 to 9830, as said below
- col_router: float32 [32], replicated, may hold values from 163 to 1638
- row_gate_up: float32 [32, 1536], replicated, may hold values from 27 to 9830, as said below
- col_gate_up: float32 [32, 1024], replicated, may hold values from 27 to 9830, as said below
- row_down: float32 [32, 512], replicated, may hold values from 1 to 491, as said below
- col_down: float32 [32, 1536], replicated, may hold values from 1 to 491, as said below
- second_attn: float32 [1536], P(('fsdp', 'ctx')), may hold values from 27 to 9830, as said below
- second_moe: float32 [1536], P(('fsdp', 'ctx')), may hold values from 27 to 9830, as said below
Outputs:
- layer_out: bfloat16 [8192, 1536], P(('fsdp', 'ctx', 'tp'))
- grad_inputs: float32 [8192, 1536], P(('fsdp', 'ctx'))
- aux_loss: float32 [], replicated
- grad_qkv: float32 [1536, 2560], P(('fsdp', 'ctx'), 'tp')
- grad_out: float32 [1536, 1536], P('tp', ('fsdp', 'ctx'))
- grad_router: float32 [1536, 32], P(('fsdp', 'ctx'))
- grad_gate_up: float32 [32, 1536, 1024], P(('fsdp', 'tp'), 'ctx')
- grad_down: float32 [32, 512, 1536], P(('fsdp', 'tp'), None, 'ctx')
- grad_gain_attn: float32 [1536], P(('fsdp', 'ctx'))
- grad_gain_moe: float32 [1536], P(('fsdp', 'ctx'))
- new_qkv: float32 [1536, 2560], P(('fsdp', 'ctx'), 'tp')
- new_out: float32 [1536, 1536], P('tp', ('fsdp', 'ctx'))
- new_router: float32 [1536, 32], P(('fsdp', 'ctx'))
- new_gate_up: float32 [32, 1536, 1024], P(('fsdp', 'tp'), 'ctx')
- new_down: float32 [32, 512, 1536], P(('fsdp', 'tp'), None, 'ctx')
- new_gain_attn: float32 [1536], P(('fsdp', 'ctx'))
- new_gain_moe: float32 [1536], P(('fsdp', 'ctx'))
- copy_qkv: bfloat16 [1536, 2560], P(('fsdp', 'ctx'), 'tp')
- copy_out: bfloat16 [1536, 1536], P('tp', ('fsdp', 'ctx'))
- copy_router: bfloat16 [1536, 32], P(('fsdp', 'ctx'))
- copy_gate_up: bfloat16 [32, 1536, 1024], P(('fsdp', 'tp'), 'ctx')
- copy_down: bfloat16 [32, 512, 1536], P(('fsdp', 'tp'), None, 'ctx')
- copy_gain_attn: bfloat16 [1536], P(('fsdp', 'ctx'))
- copy_gain_moe: bfloat16 [1536], P(('fsdp', 'ctx'))
- row_qkv_new: float32 [1536], replicated
- col_qkv_new: float32 [2560], replicated
- row_out_new: float32 [1536], replicated
- col_out_new: float32 [1536], replicated
- row_router_new: float32 [1536], replicated
- col_router_new: float32 [32], replicated
- row_gate_up_new: float32 [32, 1536], replicated
- col_gate_up_new: float32 [32, 1024], replicated
- row_down_new: float32 [32, 512], replicated
- col_down_new: float32 [32, 1536], replicated
- second_attn_new: float32 [1536], P(('fsdp', 'ctx'))
- second_moe_new: float32 [1536], P(('fsdp', 'ctx'))
- update_rms: float32 [7], replicated
The draws below stay inside these ranges and needn't reach their ends.
Inputs may be any that keep to these rules, and one draw needn't show every extreme that they name: `segment_ids`: in each tree the segment number never falls along the tokens; segment 0 holds exactly the first 819 tokens, and every segment holds at least one token. parents[r, 0] = 0; for s >= 1 the parent of segment s is smaller than s; the parent of segment 13 - 1 is 11. `routes`: within each aligned block of 256 rows no expert is named by more than 96 rows. `row_qkv`: positive. `col_out`: positive. `row_router`: positive. `row_gate_up`: positive. `col_gate_up`: positive. `row_down`: positive. `col_down`: positive. `second_attn`: positive. `second_moe`: positive.
All inputs are finite; a program needn't handle non-finite values.
Results may differ from the reference program's by a relative error of at most 0.015.
The reference program's roundings to bfloat16 on the way count: a program that leaves them out, or rounds other values in their place, can miss the bound.
Values may be sent and summed in bfloat16 or wider, within the bound.
No kernel may reach another device: no remote copies, remote signals or barrier semaphores. Data moves between devices by JAX's collectives and lax.ppermute only.
A program may use at most 320 MiB of HBM per device.

```python
import math
import jax
import jax.numpy as jnp
import numpy as np
from jax import lax

D = 1536
HEADS = 24
KV_HEADS = 8
HEAD = 64
FFE = 512
TOPK = 8
EXPERTS = 32
NSEG = 13
TOK_DEV = 512
TREES = 4
TREE = 2048
TOKENS = 8192
TRUNK = 819
MROWS = 256
CAP = 96
QKVW = 2560
N_TP = 2


def segment_tree(tree_key):
    room_after = TREE - TRUNK - 1
    shuffled = jax.random.permutation(tree_key, room_after)
    cut_points = shuffled[:NSEG - 2] + TRUNK + 1
    positions = jnp.arange(TREE, dtype=jnp.int32)
    later = jnp.sum((positions[:, None] >= cut_points[None, :]).astype(jnp.int32), axis=1)
    segment = jnp.where(positions < TRUNK, 0, 1 + later)
    return segment.astype(jnp.int32)


def draw_segment_ids(key, part):
    tree_keys = jax.random.split(jax.random.fold_in(key, 11), TREES)
    return jax.vmap(segment_tree)(tree_keys)


def draw_parents(key, part):
    seg_labels = jnp.arange(NSEG, dtype=jnp.int32)
    chosen_parent = jax.random.randint(jax.random.fold_in(key, 23), (TREES, NSEG), 0, jnp.maximum(seg_labels, 1))
    chosen_parent = jnp.where(seg_labels[None, :] == NSEG - 1, NSEG - 2, chosen_parent)
    return chosen_parent.astype(jnp.int32)


def moment_state(key, shape, spread, level):
    low_end = math.log(TOKENS * level / 50.0)
    high_end = math.log(TOKENS * level / 5.0)
    base = jnp.exp(jax.random.uniform(key, shape, jnp.float32, low_end, high_end))
    count = shape[0]
    place = jnp.arange(count, dtype=jnp.float32) / float(max(count - 1, 1))
    factor = jnp.exp((place - 0.5) * math.log(spread))
    factor = factor.reshape((count,) + (1,) * (len(shape) - 1))
    return base * factor


def pick_spread():
    spread = 10.0
    return spread


def draw_row_qkv(key, part):
    return moment_state(jax.random.fold_in(key, 101), (D,), pick_spread(), 1.0)


def draw_col_out(key, part):
    return moment_state(jax.random.fold_in(key, 102), (D,), pick_spread(), 1.0)


def draw_row_router(key, part):
    return moment_state(jax.random.fold_in(key, 103), (D,), pick_spread(), 1.0)


def draw_row_gate_up(key, part):
    return moment_state(jax.random.fold_in(key, 104), (EXPERTS, D), pick_spread(), 1.0)


def draw_col_gate_up(key, part):
    return moment_state(jax.random.fold_in(key, 105), (EXPERTS, 2 * FFE), pick_spread(), 1.0)


def draw_row_down(key, part):
    return moment_state(jax.random.fold_in(key, 106), (EXPERTS, FFE), pick_spread(), 0.05)


def draw_col_down(key, part):
    return moment_state(jax.random.fold_in(key, 107), (EXPERTS, D), pick_spread(), 0.05)


def draw_second_attn(key, part):
    return moment_state(jax.random.fold_in(key, 108), (D,), pick_spread(), 1.0)


def draw_second_moe(key, part):
    return moment_state(jax.random.fold_in(key, 109), (D,), pick_spread(), 1.0)


def block_scale(rng, shape, shards, smallest, top_value):
    factor_of = 1.0
    for dim, parts in shards:
        steps = jax.random.uniform(jax.random.fold_in(jax.random.fold_in(rng, 6), dim), (parts,), jnp.float32, smallest / len(shards), top_value / len(shards))
        factor_of = factor_of * jnp.repeat(jnp.exp(steps), shape[dim] // parts).reshape((-1,) + (1,) * (len(shape) - 1 - dim))
    return factor_of


def deal_out(rng, own, number, rows, amount, top, most, skew):
    ranking = jax.random.permutation(rng, amount)
    heavy_load, common = load_shares(amount, rows * top, most, skew, True), load_shares(amount, rows * top, most, skew, False)
    places = jnp.arange(amount)

    def named(sizes, turn):
        used = int((sizes > 0).sum())
        fixed = max(1, used // 4)
        passed = fixed + (places - fixed + turn * (used - fixed)) % max(1, amount - fixed)
        return jnp.zeros((amount,), jnp.int32).at[ranking[jnp.where(places < fixed, places, passed)]].set(jnp.asarray(sizes, jnp.int32))

    sizes = jnp.where(number % 4 == 0, named(heavy_load, number // 4), named(common, number - number // 4 - 1))
    mixed = jax.random.permutation(jax.random.fold_in(own, 3), amount)
    giver, sink = mixed[0:amount // 2 * 2:2], mixed[1:amount // 2 * 2:2]
    margin = jnp.minimum(sizes[giver] - 1, most - sizes[sink]) // 2
    margin = jnp.where((giver == ranking[0]) | (sink == ranking[0]) | (sizes[sink] == 0), 0, jnp.maximum(margin, 0))
    passed = jax.random.randint(jax.random.fold_in(own, 4), (amount // 2,), 0, 1 << 20) % (margin + 1)
    sizes = sizes.at[giver].add(-passed).at[sink].add(passed)
    items = jnp.searchsorted(jnp.cumsum(sizes), jnp.arange(rows * top), side="right").astype(jnp.int32)
    listing = items.reshape(top, rows).T
    listing = listing[jax.random.permutation(jax.random.fold_in(own, 1), rows)]
    turn = jax.random.randint(jax.random.fold_in(own, 2), (rows, 1), 0, top)
    return jnp.take_along_axis(listing, (jnp.arange(top)[None, :] + turn) % top, axis=1)


def load_shares(number_of, total, most, slope, full):
    loads = [(1 << 20) // math.isqrt(rank ** slope) + 1 for rank in range(1, number_of + 1)]
    largest = most if full else min(most, max(-(-total // number_of), total * loads[0] // sum(loads)))
    least = 1 if total - largest >= number_of - 1 else 0
    given, rest = [largest] + [least] * (number_of - 1), total - largest - least * (number_of - 1)
    while rest > 0:
        free = [i for i in range(1, number_of) if given[i] < largest] or [i for i in range(1, number_of) if given[i] < most]
        whole, budget = sum([loads[i] for i in free]), rest
        for i in free:
            more = min(most - given[i], max(1, budget * loads[i] // whole), rest)
            given[i] = given[i] + more
            rest = rest - more
    return np.array(given)


def centred(stream_key, extent, deviation, limit, shards=(), held_as=jnp.bfloat16):
    result = jax.random.normal(stream_key, extent, jnp.float32) * deviation
    if len(shards) > 0:
        result = block_scale(stream_key, extent, shards, -0.22, 0.18) * result
    return jnp.clip(result, min=-limit, max=limit).astype(held_as)


def setup_inputs(seed: int = 0) -> dict:
    key_list = jax.random.split(jax.random.key(seed), 25)
    inputs = centred(key_list[0], (TOKENS, D), 1.0, 6.0, ((0, 16),))
    cotangent = centred(key_list[1], (TOKENS, D), 1.0, 6.0, ((0, 32),))
    routes_keys = jax.random.split(jax.random.fold_in(key_list[2], 1), TOKENS // MROWS)
    routes_turns = jax.random.permutation(jax.random.fold_in(key_list[2], 3), TOKENS // MROWS)
    routes = jax.vmap(lambda own, number: deal_out(jax.random.fold_in(key_list[2], 2), own, number, MROWS, EXPERTS, TOPK, CAP, 1))(routes_keys, routes_turns).reshape((TOKENS, TOPK))
    segment_ids = draw_segment_ids(jax.random.fold_in(key_list[24], 71), 0)
    parents = draw_parents(jax.random.fold_in(key_list[24], 71), 0)
    w_qkv = centred(key_list[5], (D, QKVW), D ** -0.5, 0.15625, ((0, 16), (1, 2)), jnp.float32)
    w_out = centred(key_list[6], (HEADS * HEAD, D), (HEADS * HEAD * 8 // TOK_DEV) ** -0.5, 1.25, ((0, 2), (1, 16)), jnp.float32)
    w_router = centred(key_list[7], (D, EXPERTS), D ** -0.5, 0.15625, ((0, 16),), jnp.float32)
    w_gate_up = centred(key_list[8], (EXPERTS, D, 2 * FFE), D ** -0.5, 0.15625, ((0, 8), (1, 4)), jnp.float32)
    w_down = centred(key_list[9], (EXPERTS, FFE, D), FFE ** -0.5, 0.25, ((0, 8), (2, 4)), jnp.float32)
    gain_attn = jnp.clip(1.0 + 0.1 * jax.random.normal(key_list[10], (D,), jnp.float32), 0.5, 1.5)
    gain_moe = jnp.clip(1.0 + 0.1 * jax.random.normal(key_list[11], (D,), jnp.float32), 0.5, 1.5)
    row_qkv = draw_row_qkv(jax.random.fold_in(key_list[24], 71), 0)
    col_qkv = jnp.clip(jnp.exp(jax.random.uniform(key_list[13], (QKVW,), jnp.float32, math.log(163.0), math.log(1638.0))), 163.0, 1638.0)
    row_out = jnp.clip(jnp.exp(jax.random.uniform(key_list[14], (HEADS * HEAD,), jnp.float32, math.log(163.0), math.log(1638.0))), 163.0, 1638.0)
    col_out = draw_col_out(jax.random.fold_in(key_list[24], 71), 0)
    row_router = draw_row_router(jax.random.fold_in(key_list[24], 71), 0)
    col_router = jnp.clip(jnp.exp(jax.random.uniform(key_list[17], (EXPERTS,), jnp.float32, math.log(163.0), math.log(1638.0))), 163.0, 1638.0)
    row_gate_up = draw_row_gate_up(jax.random.fold_in(key_list[24], 71), 0)
    col_gate_up = draw_col_gate_up(jax.random.fold_in(key_list[24], 71), 0)
    row_down = draw_row_down(jax.random.fold_in(key_list[24], 71), 0)
    col_down = draw_col_down(jax.random.fold_in(key_list[24], 71), 0)
    second_attn = draw_second_attn(jax.random.fold_in(key_list[24], 71), 0)
    second_moe = draw_second_moe(jax.random.fold_in(key_list[24], 71), 0)
    return dict(inputs=inputs, cotangent=cotangent, routes=routes, segment_ids=segment_ids, parents=parents, w_qkv=w_qkv, w_out=w_out, w_router=w_router, w_gate_up=w_gate_up, w_down=w_down, gain_attn=gain_attn, gain_moe=gain_moe, row_qkv=row_qkv, col_qkv=col_qkv, row_out=row_out, col_out=col_out, row_router=row_router, col_router=col_router, row_gate_up=row_gate_up, col_gate_up=col_gate_up, row_down=row_down, col_down=col_down, second_attn=second_attn, second_moe=second_moe)


norm_eps = 1e-05
decay = 0.5
floor_sq = 1e-30
rate = 0.25
clip_rms = 0.05
aux_weight = 1.0
highest = lax.Precision.HIGHEST

@jax.custom_vjp
def low(v):
    return lax.optimization_barrier(v.astype(jnp.bfloat16)).astype(jnp.float32)

@jax.custom_vjp
def low_back(v):
    return v

def low_keep(v):
    return (low(v), None)

def low_pass(kept, grad):
    return (grad,)

def back_keep(v):
    return (v, None)

def back_low(kept, grad):
    return (low(grad),)
low.defvjp(low_keep, low_pass)
low_back.defvjp(back_keep, back_low)

def rms_norm(values, gain):
    return values * lax.rsqrt(lax.optimization_barrier(jnp.mean(values * values, axis=-1, keepdims=True)) + norm_eps) * gain

def ancestry(parent_row):
    seg_labels = jnp.arange(NSEG, dtype=jnp.int32)
    table = jnp.maximum((seg_labels[:, None] == seg_labels[None, :]).astype(jnp.float32), (parent_row[:, None] == seg_labels[None, :]).astype(jnp.float32))
    for sweep in range(NSEG.bit_length()):
        table = lax.optimization_barrier(jnp.max(table[:, :, None] * table[None, :, :], axis=1))
    return table

def tree_attention(operands):
    query, keys, values, segments, table = operands
    group_size = HEADS // KV_HEADS
    keys_full = jnp.repeat(keys, group_size, axis=1)
    values_full = jnp.repeat(values, group_size, axis=1)
    seg_labels = jnp.arange(NSEG, dtype=jnp.int32)
    seg_hot = (segments[:, None] == seg_labels[None, :]).astype(jnp.float32)
    reach = jnp.dot(jnp.dot(seg_hot, table, precision=highest), seg_hot.T, precision=highest)
    positions = jnp.arange(TREE, dtype=jnp.int32)
    allowed = (reach > 0.5) & (positions[None, :] <= positions[:, None])
    block = min(512, TREE)
    scale = HEAD ** (-0.5)

    def attend(start):
        query_block = lax.dynamic_slice_in_dim(query, start, block, 0)
        mask_block = lax.dynamic_slice_in_dim(allowed, start, block, 0)
        scores = low_back(jnp.einsum('qhd,khd->hqk', query_block, keys_full, precision=highest) * scale)
        weights_low = low(jax.nn.softmax(jnp.where(mask_block[None], scores, -1e+30), axis=-1))
        return jnp.einsum('hqk,khd->qhd', weights_low, values_full, precision=highest)
    starts = jnp.arange(TREE // block, dtype=jnp.int32) * block
    blocks = lax.map(jax.checkpoint(attend), starts)
    return blocks.reshape(TREE, HEADS, HEAD)

def reference(inputs, cotangent, routes, segment_ids, parents, w_qkv, w_out, w_router, w_gate_up, w_down, gain_attn, gain_moe, row_qkv, col_qkv, row_out, col_out, row_router, col_router, row_gate_up, col_gate_up, row_down, col_down, second_attn, second_moe):
    labels = jnp.arange(EXPERTS, dtype=jnp.int32)
    route_hot = (routes[..., None] == labels).astype(jnp.float32)
    fraction = lax.optimization_barrier(jnp.sum(route_hot, axis=(0, 1))) / (TOKENS * TOPK)
    tables = jax.vmap(ancestry)(parents)
    block_count = TOKENS // MROWS
    slot_count = block_count * CAP
    flat_routes = routes.reshape(block_count, MROWS * TOPK)
    flat_hot = (flat_routes[..., None] == labels).astype(jnp.int32)
    rank_all = jnp.cumsum(flat_hot, axis=1) - flat_hot
    slot_rank = lax.optimization_barrier(jnp.sum(rank_all * flat_hot, axis=-1))
    block_ids = jnp.arange(block_count, dtype=jnp.int32)[:, None]
    dest = (flat_routes * slot_count + block_ids * CAP + slot_rank).reshape(-1).astype(jnp.int32)
    slot_ids = jnp.arange(TOKENS * TOPK, dtype=jnp.int32)
    slot_table = jnp.zeros((EXPERTS * slot_count,), jnp.int32).at[dest].set(slot_ids).reshape(EXPERTS, slot_count)
    slot_fill = jnp.zeros((EXPERTS * slot_count,), jnp.float32).at[dest].set(1.0).reshape(EXPERTS, slot_count)
    tokens_of = (slot_table // TOPK).astype(jnp.int32)
    q_heads = HEADS // N_TP
    kv_local = KV_HEADS // N_TP

    def forward(inputs_f32, weights):
        qkv_w, out_w, router_w, gate_up_w, down_w, gain_one, gain_two = weights
        qkv_low = low(qkv_w)
        out_low = low(out_w)
        router_low = low(router_w)
        gate_up_low = low(gate_up_w)
        down_low = low(down_w)
        act1 = low(rms_norm(inputs_f32, low(gain_one)))
        qkv = low_back(low(jnp.dot(act1, qkv_low, precision=highest)))
        grouped = qkv.reshape(TOKENS, N_TP, q_heads + 2 * kv_local, HEAD)
        query = grouped[:, :, :q_heads].reshape(TREES, TREE, HEADS, HEAD)
        keys = grouped[:, :, q_heads:q_heads + kv_local].reshape(TREES, TREE, KV_HEADS, HEAD)
        values = grouped[:, :, q_heads + kv_local:].reshape(TREES, TREE, KV_HEADS, HEAD)
        attended = lax.map(jax.checkpoint(tree_attention), (query, keys, values, segment_ids, tables))
        attended = low_back(low(attended.reshape(TOKENS, HEADS * HEAD)))
        attn = low_back(jnp.dot(attended, out_low, precision=highest))
        x_one = inputs_f32 + attn
        act2 = low(rms_norm(x_one, low(gain_two)))
        logits = low_back(jnp.dot(act2, router_low, precision=highest))
        router_probs = jax.nn.softmax(logits, axis=-1)
        aux = EXPERTS * jnp.sum(fraction * lax.optimization_barrier(jnp.mean(router_probs, axis=0)))
        chosen = jnp.take_along_axis(logits, routes, axis=1)
        combine = jax.nn.softmax(chosen, axis=-1)
        slot_weights = combine.reshape(-1)[slot_table] * slot_fill

        def expert(operands):
            rows_of, gate_up_e, down_e = operands
            rows = low_back(act2[rows_of])
            gate_up = low_back(jnp.dot(rows, gate_up_e, precision=highest))
            hidden = low(jax.nn.silu(gate_up[:, :FFE]) * gate_up[:, FFE:])
            return low_back(low(jnp.dot(hidden, down_e, precision=highest)))
        outs = lax.map(jax.checkpoint(expert), (tokens_of, gate_up_low, down_low))
        moe = jnp.zeros((TOKENS, D), jnp.float32).at[tokens_of.reshape(-1)].add((slot_weights[..., None] * outs).reshape(-1, D))
        return (x_one + moe, aux)
    weights = (w_qkv, w_out, w_router, w_gate_up, w_down, gain_attn, gain_moe)
    (layer_f32, aux_loss), back = jax.vjp(forward, inputs.astype(jnp.float32), weights)
    grad_inputs, grads = back((cotangent.astype(jnp.float32), jnp.asarray(aux_weight * TOKENS, jnp.float32)))
    g_qkv, g_out, g_router, g_gate_up, g_down, g_gain1, g_gain2 = grads

    def factored(grad, row_old, col_old):
        squared = grad * grad + floor_sq
        row_new = decay * row_old + (1.0 - decay) * lax.optimization_barrier(jnp.mean(squared, axis=-1))
        col_new = decay * col_old + (1.0 - decay) * lax.optimization_barrier(jnp.mean(squared, axis=-2))
        second = row_new[..., :, None] * col_new[..., None, :] / lax.optimization_barrier(jnp.mean(row_new, axis=-1))[..., None, None]
        return (row_new, col_new, grad * lax.rsqrt(second))

    def unfactored(grad, second_old):
        second_new = decay * second_old + (1.0 - decay) * (grad * grad + floor_sq)
        return (second_new, grad * lax.rsqrt(second_new))

    def applied(weight, change):
        rms = jnp.sqrt(jnp.mean(change * change))
        weight_rms = jnp.sqrt(jnp.mean(weight * weight))
        return (weight - rate * weight_rms * change / jnp.maximum(clip_rms, rms), rms)
    rq, cq, change_qkv = factored(g_qkv, row_qkv, col_qkv)
    ro, co, change_out = factored(g_out, row_out, col_out)
    rr, cr, change_router = factored(g_router, row_router, col_router)
    rg, cg, change_gate_up = factored(g_gate_up, row_gate_up, col_gate_up)
    rd, cd, change_down = factored(g_down, row_down, col_down)
    sa, change_gain1 = unfactored(g_gain1, second_attn)
    sm, change_gain2 = unfactored(g_gain2, second_moe)
    new_qkv, rms_qkv = applied(w_qkv, change_qkv)
    new_out, rms_out = applied(w_out, change_out)
    new_router, rms_router = applied(w_router, change_router)
    new_gate_up, rms_gate_up = applied(w_gate_up, change_gate_up)
    new_down, rms_down = applied(w_down, change_down)
    new_gain1, rms_gain1 = applied(gain_attn, change_gain1)
    new_gain2, rms_gain2 = applied(gain_moe, change_gain2)
    update_rms = jnp.stack([rms_qkv, rms_out, rms_router, rms_gate_up, rms_down, rms_gain1, rms_gain2])
    return (layer_f32.astype(jnp.bfloat16), grad_inputs, aux_loss, g_qkv, g_out, g_router, g_gate_up, g_down, g_gain1, g_gain2, new_qkv, new_out, new_router, new_gate_up, new_down, new_gain1, new_gain2, new_qkv.astype(jnp.bfloat16), new_out.astype(jnp.bfloat16), new_router.astype(jnp.bfloat16), new_gate_up.astype(jnp.bfloat16), new_down.astype(jnp.bfloat16), new_gain1.astype(jnp.bfloat16), new_gain2.astype(jnp.bfloat16), rq, cq, ro, co, rr, cr, rg, cg, rd, cd, sa, sm, update_rms)
```

```python
import jax
import jax.numpy as jnp
from jax import lax
from jax.sharding import PartitionSpec as P

D = 1536
HEADS = 24
KV_HEADS = 8
HEAD = 64
FFE = 512
TOPK = 8
EXPERTS = 32
NSEG = 13

norm_eps = 1e-05
decay = 0.5
floor_sq = 1e-30
rate = 0.25
clip_rms = 0.05
aux_weight = 1.0
bf16 = jnp.bfloat16
f32 = jnp.float32
EVERY = ("fsdp", "ctx", "tp")


def dot(spec, left, right):
    return jnp.einsum(spec, left, right, preferred_element_type=f32)


def exchange(values, axes):
    return lax.all_to_all(values, axes, split_axis=0, concat_axis=0, tiled=True)


def share(vector, count):
    return exchange(jnp.broadcast_to(vector[None], (count,) + vector.shape), EVERY)


def inv_rms(values):
    return lax.rsqrt(jnp.mean(values * values, axis=-1, keepdims=True) + norm_eps)


def norm_backward(values, inv, gain, d_out):
    normed = values * inv
    scaled = d_out * gain
    d_values = inv * (scaled - normed * jnp.mean(scaled * normed, axis=-1, keepdims=True))
    return d_values, normed


def ancestry(parent_row):
    seg_labels = jnp.arange(NSEG, dtype=jnp.int32)
    table = jnp.maximum(
        (seg_labels[:, None] == seg_labels[None, :]).astype(f32),
        (parent_row[:, None] == seg_labels[None, :]).astype(f32),
    )
    for sweep in range(NSEG.bit_length()):
        table = jnp.max(table[:, :, None] * table[None, :, :], axis=1)
    return table


def attention_forward(query, key, value, allowed, blocks):
    rows = query.shape[0] // blocks
    outs, logs = [], []
    for b in range(blocks):
        seen = (b + 1) * rows
        mine = slice(b * rows, seen)
        scores = dot("qgd,kd->gqk", query[mine], key[:seen]) * HEAD ** (-0.5)
        masked = jnp.where(allowed[None, mine, :seen], scores, -1e30)
        row_max = jnp.max(masked, axis=-1, keepdims=True)
        exp_scores = jnp.exp(masked - row_max)
        row_total = jnp.sum(exp_scores, axis=-1, keepdims=True)
        prob_low = (exp_scores / row_total).astype(bf16)
        logs.append(row_max + jnp.log(row_total))
        outs.append(dot("gqk,kd->qgd", prob_low, value[:seen]))
    return jnp.concatenate(outs, axis=0).astype(bf16), logs


def attention_backward(query, key, value, allowed, logs, d_out):
    blocks = len(logs)
    rows = query.shape[0] // blocks
    scale = HEAD ** (-0.5)
    d_key = jnp.zeros(key.shape, f32)
    d_value = jnp.zeros(key.shape, f32)
    d_queries = []
    for b in range(blocks):
        seen = (b + 1) * rows
        mine = slice(b * rows, seen)
        scores = dot("qgd,kd->gqk", query[mine], key[:seen]) * scale
        masked = jnp.where(allowed[None, mine, :seen], scores, -1e30)
        prob_full = jnp.exp(masked - logs[b])
        d_prob = dot("qgd,kd->gqk", d_out[mine], value[:seen])
        delta = jnp.sum(prob_full * d_prob, axis=-1, keepdims=True)
        d_scores = (prob_full * (d_prob - delta)).astype(bf16)
        d_queries.append(dot("gqk,kd->qgd", d_scores, key[:seen]) * scale)
        d_key = d_key.at[:seen].add(dot("gqk,qgd->kd", d_scores, query[mine]) * scale)
        d_value = d_value.at[:seen].add(dot("gqk,qgd->kd", prob_full.astype(bf16), d_out[mine]))
    return jnp.concatenate(d_queries, axis=0), d_key, d_value


def per_device(
    inputs,
    cotangent,
    routes,
    segment_ids,
    parents,
    w_qkv,
    w_out,
    w_router,
    w_gate_up,
    w_down,
    gain_attn,
    gain_moe,
    row_qkv,
    col_qkv,
    row_out,
    col_out,
    row_router,
    col_router,
    row_gate_up,
    col_gate_up,
    row_down,
    col_down,
    second_attn,
    second_moe,
):
    tp_count = lax.axis_size("tp")
    ctx_count = lax.axis_size("ctx")
    fsdp_count = lax.axis_size("fsdp")
    count = tp_count * ctx_count * fsdp_count
    tp_index = lax.axis_index("tp")
    ctx_index = lax.axis_index("ctx")
    fsdp_index = lax.axis_index("fsdp")
    flat_index = fsdp_index * ctx_count + ctx_index
    owner_index = fsdp_index * tp_count + tp_index
    keep_once = (tp_index == 0).astype(f32)
    tok_rows = inputs.shape[0]
    half_rows = tok_rows // tp_count
    tree_len = segment_ids.shape[1]
    tokens_all = tok_rows * fsdp_count * ctx_count
    capacity = half_rows * TOPK * 3 // (2 * EXPERTS)
    groups = fsdp_count * tp_count
    local_experts = EXPERTS // groups
    q_own = HEADS // (tp_count * ctx_count)
    kv_own = KV_HEADS // (tp_count * ctx_count)
    group_size = HEADS // KV_HEADS
    q_cols = q_own * HEAD
    kv_cols = kv_own * HEAD
    own_cols = q_cols + 2 * kv_cols
    dense_rows = w_qkv.shape[0]
    qkv_cols = w_qkv.shape[1]
    dense_parts = fsdp_count * ctx_count
    ctx_rows = w_gate_up.shape[1]
    labels = jnp.arange(EXPERTS, dtype=jnp.int32)

    def by_ctx(columns):
        q_end = ctx_count * q_cols
        k_end = q_end + ctx_count * kv_cols
        lead = columns.shape[:-1]
        return jnp.concatenate(
            [
                columns[..., :q_end].reshape(lead + (ctx_count, q_cols)),
                columns[..., q_end:k_end].reshape(lead + (ctx_count, kv_cols)),
                columns[..., k_end:].reshape(lead + (ctx_count, kv_cols)),
            ],
            axis=-1,
        )

    def from_ctx(columns):
        lead = columns.shape[:-2]
        return jnp.concatenate(
            [
                columns[..., :q_cols].reshape(lead + (-1,)),
                columns[..., q_cols : q_cols + kv_cols].reshape(lead + (-1,)),
                columns[..., q_cols + kv_cols :].reshape(lead + (-1,)),
            ],
            axis=-1,
        )

    w_qkv_low = w_qkv.astype(bf16)
    w_grouped = by_ctx(w_qkv_low)
    extras = jnp.concatenate(
        [gain_attn.astype(bf16)[:, None], gain_moe.astype(bf16)[:, None], w_router.astype(bf16)],
        axis=1,
    )
    w_send = jnp.concatenate(
        [
            jnp.moveaxis(w_grouped, 1, 0),
            jnp.broadcast_to(extras[None], (ctx_count,) + extras.shape),
        ],
        axis=-1,
    )
    w_send = jnp.broadcast_to(w_send[None], (fsdp_count,) + w_send.shape)
    w_got = exchange(w_send.reshape((dense_parts,) + w_send.shape[2:]), ("fsdp", "ctx"))
    w_got = w_got.reshape(D, own_cols + 2 + EXPERTS)
    tree_inputs = lax.all_gather(inputs, "ctx", axis=0, tiled=True).astype(f32)
    w_own = w_got[:, :own_cols]
    gain_one = w_got[:, own_cols].astype(f32)
    gain_two = w_got[:, own_cols + 1].astype(f32)
    router_full = w_got[:, own_cols + 2 :]

    my_routes = lax.dynamic_slice_in_dim(routes, tp_index * half_rows, half_rows, 0)
    hit = jnp.sum((my_routes[..., None] == labels).astype(f32), axis=1)
    master_sums = jnp.stack(
        [
            jnp.sum(w_qkv * w_qkv),
            jnp.sum(w_out * w_out),
            keep_once * jnp.sum(w_router * w_router),
            jnp.sum(w_gate_up * w_gate_up),
            jnp.sum(w_down * w_down),
            keep_once * jnp.sum(gain_attn * gain_attn),
            keep_once * jnp.sum(gain_moe * gain_moe),
        ]
    )
    early = jnp.sum(share(jnp.concatenate([jnp.sum(hit, axis=0), master_sums]), count), axis=0)
    fraction = early[:EXPERTS] / (tokens_all * TOPK)
    master_totals = early[EXPERTS:]
    before = (
        jnp.arange(half_rows, dtype=jnp.int32)[:, None]
        < jnp.arange(half_rows, dtype=jnp.int32)[None, :]
    ).astype(bf16)
    rank = dot("te,tu->eu", hit.astype(bf16), before)
    rank = jnp.where(hit.T > 0.5, rank, -1.0)
    ranks = exchange(rank.reshape(groups, local_experts, half_rows), ("fsdp", "tp"))
    grad_rows = lax.all_gather(cotangent, ("fsdp", "tp"), axis=0, tiled=True)
    grad_rows = grad_rows.reshape(groups, half_rows, D)
    gate_up_all = lax.all_gather(w_gate_up.astype(bf16), "ctx", axis=1, tiled=True)
    down_all = lax.all_gather(w_down.astype(bf16), "ctx", axis=2, tiled=True)
    out_t = lax.all_gather(w_out.astype(bf16).T, ("tp", "fsdp", "ctx"), axis=0, tiled=True)
    out_t = out_t.reshape(tp_count, D, w_out.shape[0])
    qkv_full = lax.all_gather(
        w_grouped.reshape(dense_rows, qkv_cols), ("tp", "fsdp", "ctx"), axis=0, tiled=True
    ).reshape(tp_count, D, qkv_cols)

    act1 = (tree_inputs * inv_rms(tree_inputs) * gain_one).astype(bf16)
    qkv = dot("td,dc->tc", act1, w_own).astype(bf16)
    query = qkv[:, :q_cols].reshape(tree_len, kv_own, group_size, HEAD)
    keys = qkv[:, q_cols : q_cols + kv_cols].reshape(tree_len, kv_own, HEAD)
    values = qkv[:, q_cols + kv_cols :].reshape(tree_len, kv_own, HEAD)
    seg_hot = (segment_ids[0][:, None] == jnp.arange(NSEG, dtype=jnp.int32)).astype(bf16)
    reach = dot("qs,ks->qk", dot("qs,su->qu", seg_hot, ancestry(parents[0]).astype(bf16)).astype(bf16), seg_hot)
    positions = jnp.arange(tree_len, dtype=jnp.int32)
    allowed = (reach > 0.5) & (positions[None, :] <= positions[:, None])
    blocks = 4
    outs, logs = [], []
    for h in range(kv_own):
        out_h, log_h = attention_forward(query[:, h], keys[:, h], values[:, h], allowed, blocks)
        outs.append(out_h)
        logs.append(log_h)
    attended_own = jnp.concatenate(outs, axis=1).reshape(tree_len, q_cols)
    attended = exchange(attended_own, ("ctx", "tp")).reshape(ctx_count, tp_count, half_rows, q_cols)
    attended = attended.transpose(2, 1, 0, 3).reshape(half_rows, tp_count, ctx_count * q_cols)
    inputs_half = lax.dynamic_slice_in_dim(inputs, tp_index * half_rows, half_rows, 0).astype(f32)
    x_one = inputs_half + dot("rtk,tdk->rd", attended, out_t)

    inv_two = inv_rms(x_one)
    act2 = (x_one * inv_two * gain_two).astype(bf16)
    rows = lax.all_gather(act2, ("fsdp", "tp"), axis=0, tiled=True).reshape(groups, half_rows, D)
    logits = dot("td,de->te", act2, router_full)
    router_probs = jax.nn.softmax(logits, axis=-1)
    combine = jax.nn.softmax(jnp.where(hit > 0.5, logits, -jnp.inf), axis=-1)
    weights = exchange(combine.T.reshape(groups, local_experts, half_rows), ("fsdp", "tp"))

    slots = jnp.arange(capacity, dtype=f32)
    chosen = ranks[:, :, None, :] == slots[None, None, :, None]
    pick = chosen.astype(bf16)
    slot_weight = jnp.sum(jnp.where(chosen, weights[:, :, None, :], 0.0), axis=-1)
    x_e = dot("sert,std->serd", pick, rows).astype(bf16)
    c_e = dot("sert,std->serd", pick, grad_rows)
    gate_up = dot("serd,edf->serf", x_e, gate_up_all)
    gate = gate_up[..., :FFE]
    up = gate_up[..., FFE:]
    sig = jax.nn.sigmoid(gate)
    hidden = (gate * sig * up).astype(bf16)
    expert_out = dot("serf,efd->serd", hidden, down_all).astype(bf16)
    d_slot_out = jnp.sum(c_e * expert_out.astype(f32), axis=-1)
    d_slot = (slot_weight[..., None] * c_e).astype(bf16)
    d_hidden = dot("serd,efd->serf", d_slot, down_all)
    g_down_local = dot("serf,serd->efd", hidden, d_slot)
    d_gate = d_hidden * up * sig * (1.0 + gate * (1.0 - sig))
    d_up = d_hidden * gate * sig
    d_gate_up = jnp.concatenate([d_gate, d_up], axis=-1).astype(bf16)
    d_row = dot("serf,edf->serd", d_gate_up, gate_up_all).astype(bf16)
    g_gate_up_local = dot("serd,serf->edf", x_e, d_gate_up)
    d_sum = dot("sert,serd->std", pick, d_row).astype(bf16)
    weighted = (slot_weight[..., None] * expert_out.astype(f32)).astype(bf16)
    moe_sum = dot("sert,serd->std", pick, weighted).astype(bf16)
    d_combine_own = jnp.sum(jnp.where(chosen, d_slot_out[..., None], 0.0), axis=2)
    d_combine = exchange(d_combine_own, ("fsdp", "tp")).reshape(EXPERTS, half_rows).T
    d_act2 = lax.psum_scatter(
        d_sum.reshape(groups * half_rows, D), ("fsdp", "tp"), scatter_dimension=0, tiled=True
    ).astype(f32)
    moe = lax.psum_scatter(
        moe_sum.reshape(groups * half_rows, D), ("fsdp", "tp"), scatter_dimension=0, tiled=True
    ).astype(f32)
    layer_out = (x_one + moe).astype(bf16)
    g_gate_up = lax.psum_scatter(
        g_gate_up_local.astype(bf16), "ctx", scatter_dimension=1, tiled=True
    ).astype(f32)
    g_down = lax.psum_scatter(
        g_down_local.astype(bf16), "ctx", scatter_dimension=2, tiled=True
    ).astype(f32)

    aux_grad = aux_weight * EXPERTS * fraction
    d_logits = combine * (d_combine - jnp.sum(combine * d_combine, axis=-1, keepdims=True))
    d_logits = d_logits + router_probs * (
        aux_grad - jnp.sum(router_probs * aux_grad, axis=-1, keepdims=True)
    )
    d_logits = d_logits.astype(bf16)
    d_act2 = d_act2 + dot("te,de->td", d_logits, router_full)
    d_half, normed_two = norm_backward(x_one, inv_two, gain_two, d_act2)
    d_x1_half = cotangent.astype(f32) + d_half
    d_x1_low = d_x1_half.astype(bf16)
    g_small = jnp.concatenate(
        [dot("te,td->ed", d_logits, act2), jnp.sum(d_act2 * normed_two, axis=0)[None]], axis=0
    )
    g_small = jnp.moveaxis(g_small.reshape(EXPERTS + 1, dense_parts, dense_rows), 1, 0)
    g_small = jnp.broadcast_to(g_small[:, None], (dense_parts, tp_count) + g_small.shape[1:])
    g_small = exchange(g_small.reshape((count,) + g_small.shape[2:]), EVERY)
    g_small = jnp.sum(g_small, axis=0)
    g_router = g_small[:EXPERTS].T
    g_gain2 = g_small[EXPERTS]

    d_attended = dot("rd,tdk->rtk", d_x1_low, out_t).astype(bf16)
    d_attended = d_attended.reshape(half_rows, tp_count, ctx_count, q_cols).transpose(2, 1, 0, 3)
    d_attended = exchange(d_attended.reshape(tree_len, q_cols), ("ctx", "tp"))
    d_attended = d_attended.reshape(tree_len, kv_own, group_size, HEAD)
    d_q, d_k, d_v = [], [], []
    for h in range(kv_own):
        dq_h, dk_h, dv_h = attention_backward(
            query[:, h], keys[:, h], values[:, h], allowed, logs[h], d_attended[:, h]
        )
        d_q.append(dq_h.reshape(tree_len, -1))
        d_k.append(dk_h)
        d_v.append(dv_h)
    d_qkv = jnp.concatenate(d_q + d_k + d_v, axis=1).astype(bf16)
    g_qkv_part = dot("td,tc->dc", act1, d_qkv).astype(bf16)
    g_qkv_got = exchange(g_qkv_part.reshape(dense_parts, dense_rows, own_cols), ("fsdp", "ctx"))
    g_qkv_got = g_qkv_got.reshape(fsdp_count, ctx_count, dense_rows, own_cols).astype(f32)
    g_qkv = from_ctx(jnp.moveaxis(jnp.sum(g_qkv_got, axis=0), 0, 1))
    d_qkv_send = jnp.broadcast_to(
        d_qkv.reshape(ctx_count, 1, tok_rows, own_cols), (ctx_count, tp_count, tok_rows, own_cols)
    )
    d_qkv_all = exchange(d_qkv_send.reshape(-1, tok_rows, own_cols), ("ctx", "tp"))
    d_qkv_all = d_qkv_all.reshape(ctx_count, tp_count, tok_rows, own_cols)
    d_qkv_all = d_qkv_all.transpose(2, 1, 0, 3).reshape(tok_rows, tp_count, qkv_cols)
    d_act1 = dot("rtc,tdc->rd", d_qkv_all, qkv_full)
    own_inputs = inputs.astype(f32)
    d_inputs_attn, _ = norm_backward(own_inputs, inv_rms(own_inputs), gain_one, d_act1)
    d_x1 = lax.all_gather(d_x1_half, "tp", axis=0, tiled=True)
    grad_inputs = d_x1 + d_inputs_attn

    attended_t = attended.transpose(1, 0, 2)
    attended_pair = exchange(attended_t, "tp").reshape(tok_rows, -1)
    d_x1_pair = d_x1.astype(bf16)
    g_out_part = dot("td,tq->dq", d_x1_pair, attended_pair).astype(bf16)
    g_out_got = exchange(g_out_part.reshape(dense_parts, dense_rows, -1), ("fsdp", "ctx"))
    g_out = jnp.sum(g_out_got.astype(f32), axis=0).T

    sq_out = g_out * g_out
    sq_router = g_router * g_router
    out_rows = w_out.shape[0]
    first = jnp.concatenate(
        [
            jnp.sum(sq_out, axis=1),
            jnp.sum(sq_out, axis=0),
            jnp.sum(sq_router, axis=1),
            jnp.sum(sq_router, axis=0),
            jnp.sum(router_probs, axis=0),
        ]
    )
    first = share(first, count).reshape(dense_parts, tp_count, -1)
    at = [out_rows, out_rows + dense_rows, out_rows + 2 * dense_rows]
    at.append(at[-1] + EXPERTS)
    tot_row_out = jnp.sum(first[..., : at[0]], axis=0).reshape(-1)
    tot_col_out = jnp.sum(first[..., at[0] : at[1]], axis=1).reshape(-1)
    tot_row_router = first[:, 0, at[1] : at[2]].reshape(-1)
    tot_col_router = jnp.sum(first[:, 0, at[2] : at[3]], axis=0)
    prob_totals = jnp.sum(first[..., at[3] :], axis=(0, 1))

    sq_gate_up = g_gate_up * g_gate_up
    sq_down = g_down * g_down
    expert_parts = jnp.concatenate(
        [
            jnp.sum(sq_gate_up, axis=2),
            jnp.sum(sq_down, axis=1),
            jnp.sum(sq_gate_up, axis=1),
            jnp.sum(sq_down, axis=2),
        ],
        axis=1,
    )
    expert_got = share(expert_parts, count).reshape(
        fsdp_count, ctx_count, tp_count, local_experts, -1
    )
    split_rows = expert_got[..., : 2 * ctx_rows].transpose(0, 2, 3, 1, 4)
    summed = jnp.sum(expert_got[..., 2 * ctx_rows :], axis=1).reshape(EXPERTS, -1)
    tot_row_gu = split_rows[..., :ctx_rows].reshape(EXPERTS, D)
    tot_col_down = split_rows[..., ctx_rows:].reshape(EXPERTS, D)
    tot_col_gu = summed[:, : 2 * FFE]
    tot_row_down = summed[:, 2 * FFE :]

    sq_qkv = g_qkv * g_qkv
    gain_part = jnp.sum(g_qkv * w_qkv_low.astype(f32), axis=1) / gain_attn.astype(bf16).astype(f32)
    second = jnp.concatenate([jnp.sum(sq_qkv, axis=1), gain_part, jnp.sum(sq_qkv, axis=0)])
    second = share(second, count).reshape(dense_parts, tp_count, -1)
    tot_row_qkv = jnp.sum(second[..., :dense_rows], axis=1).reshape(-1)
    g_gain1_all = jnp.sum(second[..., dense_rows : 2 * dense_rows], axis=1)
    g_gain1 = lax.dynamic_index_in_dim(g_gain1_all, flat_index, 0, keepdims=False)
    tot_col_qkv = jnp.sum(second[..., 2 * dense_rows :], axis=0).reshape(-1)

    qkv_width = (HEADS + 2 * KV_HEADS) * HEAD
    row_qkv_new = decay * row_qkv + (1.0 - decay) * (tot_row_qkv / qkv_width + floor_sq)
    col_qkv_new = decay * col_qkv + (1.0 - decay) * (tot_col_qkv / D + floor_sq)
    row_out_new = decay * row_out + (1.0 - decay) * (tot_row_out / D + floor_sq)
    col_out_new = decay * col_out + (1.0 - decay) * (tot_col_out / (HEADS * HEAD) + floor_sq)
    row_router_new = decay * row_router + (1.0 - decay) * (tot_row_router / EXPERTS + floor_sq)
    col_router_new = decay * col_router + (1.0 - decay) * (tot_col_router / D + floor_sq)
    row_gu_new = decay * row_gate_up + (1.0 - decay) * (tot_row_gu / (2 * FFE) + floor_sq)
    col_gu_new = decay * col_gate_up + (1.0 - decay) * (tot_col_gu / D + floor_sq)
    row_down_new = decay * row_down + (1.0 - decay) * (tot_row_down / D + floor_sq)
    col_down_new = decay * col_down + (1.0 - decay) * (tot_col_down / FFE + floor_sq)
    aux_loss = EXPERTS * jnp.sum(fraction * prob_totals / tokens_all)

    expert_start = owner_index * local_experts
    rows_here = lax.dynamic_slice_in_dim(row_qkv_new, flat_index * dense_rows, dense_rows, 0)
    cols_here = lax.dynamic_slice_in_dim(col_qkv_new, tp_index * qkv_cols, qkv_cols, 0)
    change_qkv = g_qkv * lax.rsqrt(rows_here[:, None] * cols_here[None, :] / jnp.mean(row_qkv_new))
    rows_here = lax.dynamic_slice_in_dim(row_out_new, tp_index * out_rows, out_rows, 0)
    cols_here = lax.dynamic_slice_in_dim(col_out_new, flat_index * dense_rows, dense_rows, 0)
    change_out = g_out * lax.rsqrt(rows_here[:, None] * cols_here[None, :] / jnp.mean(row_out_new))
    rows_here = lax.dynamic_slice_in_dim(row_router_new, flat_index * dense_rows, dense_rows, 0)
    change_router = g_router * lax.rsqrt(
        rows_here[:, None] * col_router_new[None, :] / jnp.mean(row_router_new)
    )
    start_pair = (
        jnp.asarray(expert_start, jnp.int32),
        jnp.asarray(ctx_index * ctx_rows, jnp.int32),
    )
    zero_start = jnp.asarray(0, jnp.int32)
    rows_gu = lax.dynamic_slice(row_gu_new, start_pair, (local_experts, ctx_rows))
    cols_gu = lax.dynamic_slice(col_gu_new, (start_pair[0], zero_start), (local_experts, 2 * FFE))
    mean_gu = lax.dynamic_slice_in_dim(
        jnp.mean(row_gu_new, axis=-1), expert_start, local_experts, 0
    )
    change_gate_up = g_gate_up * lax.rsqrt(
        rows_gu[:, :, None] * cols_gu[:, None, :] / mean_gu[:, None, None]
    )
    rows_dn = lax.dynamic_slice(row_down_new, (start_pair[0], zero_start), (local_experts, FFE))
    cols_dn = lax.dynamic_slice(col_down_new, start_pair, (local_experts, ctx_rows))
    mean_dn = lax.dynamic_slice_in_dim(
        jnp.mean(row_down_new, axis=-1), expert_start, local_experts, 0
    )
    change_down = g_down * lax.rsqrt(
        rows_dn[:, :, None] * cols_dn[:, None, :] / mean_dn[:, None, None]
    )
    second_attn_new = decay * second_attn + (1.0 - decay) * (g_gain1 * g_gain1 + floor_sq)
    second_moe_new = decay * second_moe + (1.0 - decay) * (g_gain2 * g_gain2 + floor_sq)
    change_gain1 = g_gain1 * lax.rsqrt(second_attn_new)
    change_gain2 = g_gain2 * lax.rsqrt(second_moe_new)
    square_sums = jnp.stack(
        [
            jnp.sum(change_qkv * change_qkv),
            jnp.sum(change_out * change_out),
            keep_once * jnp.sum(change_router * change_router),
            jnp.sum(change_gate_up * change_gate_up),
            jnp.sum(change_down * change_down),
            keep_once * jnp.sum(change_gain1 * change_gain1),
            keep_once * jnp.sum(change_gain2 * change_gain2),
        ]
    )
    square_totals = jnp.sum(share(square_sums, count), axis=0)
    entries = jnp.array(
        [
            D * qkv_width,
            HEADS * HEAD * D,
            D * EXPERTS,
            EXPERTS * D * 2 * FFE,
            EXPERTS * FFE * D,
            D,
            D,
        ],
        f32,
    )
    update_rms = jnp.sqrt(square_totals / entries)
    weight_rms = jnp.sqrt(master_totals / entries)
    step_scale = rate * weight_rms / jnp.maximum(clip_rms, update_rms)
    new_qkv = w_qkv - step_scale[0] * change_qkv
    new_out = w_out - step_scale[1] * change_out
    new_router = w_router - step_scale[2] * change_router
    new_gate_up = w_gate_up - step_scale[3] * change_gate_up
    new_down = w_down - step_scale[4] * change_down
    new_gain1 = gain_attn - step_scale[5] * change_gain1
    new_gain2 = gain_moe - step_scale[6] * change_gain2
    return (
        layer_out,
        grad_inputs,
        aux_loss,
        g_qkv,
        g_out,
        g_router,
        g_gate_up,
        g_down,
        g_gain1,
        g_gain2,
        new_qkv,
        new_out,
        new_router,
        new_gate_up,
        new_down,
        new_gain1,
        new_gain2,
        new_qkv.astype(bf16),
        new_out.astype(bf16),
        new_router.astype(bf16),
        new_gate_up.astype(bf16),
        new_down.astype(bf16),
        new_gain1.astype(bf16),
        new_gain2.astype(bf16),
        row_qkv_new,
        col_qkv_new,
        row_out_new,
        col_out_new,
        row_router_new,
        col_router_new,
        row_gu_new,
        col_gu_new,
        row_down_new,
        col_down_new,
        second_attn_new,
        second_moe_new,
        update_rms,
    )


def solution(mesh):
    placed = (
        P(("fsdp", "ctx"), None),
        P(("fsdp", "ctx", "tp"), None),
        P(("fsdp", "ctx"), None),
        P("fsdp", None),
        P("fsdp", None),
        P(("fsdp", "ctx"), "tp"),
        P("tp", ("fsdp", "ctx")),
        P(("fsdp", "ctx"), None),
        P(("fsdp", "tp"), "ctx", None),
        P(("fsdp", "tp"), None, "ctx"),
        P(("fsdp", "ctx")),
        P(("fsdp", "ctx")),
        P(),
        P(),
        P(),
        P(),
        P(),
        P(),
        P(),
        P(),
        P(),
        P(),
        P(("fsdp", "ctx")),
        P(("fsdp", "ctx")),
    )
    return jax.shard_map(
        per_device,
        mesh=mesh,
        in_specs=placed,
        out_specs=(
            P(("fsdp", "ctx", "tp"), None),
            P(("fsdp", "ctx"), None),
            P(),
            P(("fsdp", "ctx"), "tp"),
            P("tp", ("fsdp", "ctx")),
            P(("fsdp", "ctx"), None),
            P(("fsdp", "tp"), "ctx", None),
            P(("fsdp", "tp"), None, "ctx"),
            P(("fsdp", "ctx")),
            P(("fsdp", "ctx")),
            P(("fsdp", "ctx"), "tp"),
            P("tp", ("fsdp", "ctx")),
            P(("fsdp", "ctx"), None),
            P(("fsdp", "tp"), "ctx", None),
            P(("fsdp", "tp"), None, "ctx"),
            P(("fsdp", "ctx")),
            P(("fsdp", "ctx")),
            P(("fsdp", "ctx"), "tp"),
            P("tp", ("fsdp", "ctx")),
            P(("fsdp", "ctx"), None),
            P(("fsdp", "tp"), "ctx", None),
            P(("fsdp", "tp"), None, "ctx"),
            P(("fsdp", "ctx")),
            P(("fsdp", "ctx")),
            P(),
            P(),
            P(),
            P(),
            P(),
            P(),
            P(),
            P(),
            P(),
            P(),
            P(("fsdp", "ctx")),
            P(("fsdp", "ctx")),
            P(),
        ),
        check_vma=False,
    )
```

```python
import functools

import jax
import jax.numpy as jnp
from jax import lax
from jax.experimental import pallas as pl
from jax.experimental.pallas import tpu as pltpu
from jax.sharding import PartitionSpec as P

D = 1536
HEADS = 24
KV_HEADS = 8
HEAD = 64
FFE = 512
TOPK = 8
EXPERTS = 32
NSEG = 13

norm_eps = 1e-05
decay = 0.5
floor_sq = 1e-30
rate = 0.25
clip_rms = 0.05
aux_weight = 1.0
bf16 = jnp.bfloat16
f32 = jnp.float32
EVERY = ("fsdp", "ctx", "tp")
NT = (((1,), (1,)), ((), ()))
NN = (((1,), (0,)), ((), ()))
TN = (((0,), (0,)), ((), ()))


def dot(spec, left, right):
    return jnp.einsum(spec, left, right, preferred_element_type=f32)


def exchange(values, axes):
    return lax.all_to_all(values, axes, split_axis=0, concat_axis=0, tiled=True)


def share(vector, count):
    return exchange(jnp.broadcast_to(vector[None], (count,) + vector.shape), EVERY)


def inv_rms(values):
    return lax.rsqrt(jnp.mean(values * values, axis=-1, keepdims=True) + norm_eps)


def norm_backward(values, inv, gain, d_out):
    normed = values * inv
    scaled = d_out * gain
    d_values = inv * (scaled - normed * jnp.mean(scaled * normed, axis=-1, keepdims=True))
    return d_values, normed


def ancestry(parent_row):
    seg_labels = jnp.arange(NSEG, dtype=jnp.int32)
    table = jnp.maximum(
        (seg_labels[:, None] == seg_labels[None, :]).astype(f32),
        (parent_row[:, None] == seg_labels[None, :]).astype(f32),
    )
    for sweep in range(NSEG.bit_length()):
        table = jnp.max(table[:, :, None] * table[None, :, :], axis=1)
    return table


def partner(values, axis, bits, count):
    return lax.ppermute(values, axis, [(i, i ^ bits) for i in range(count)])


def after(values, *others):
    return lax.optimization_barrier((values,) + others)[0]


def xor_order(values, axis, index):
    shape = values.shape
    bit = 1
    while bit < shape[axis]:
        halves = values.reshape(shape[:axis] + (-1, 2, bit) + shape[axis + 1 :])
        swapped = jnp.flip(halves, axis + 1)
        values = jnp.where((index // bit) % 2 == 1, swapped, halves).reshape(shape)
        bit *= 2
    return values


def in_order(mine, other, bit, axis):
    first = jnp.where(bit == 0, mine, other)
    second = jnp.where(bit == 0, other, mine)
    return jnp.stack([first, second], axis=axis)


def mm(left, right, dims):
    return lax.dot_general(left, right, dims, preferred_element_type=f32)


def forward_kernel(q_ref, k_ref, vt_ref, out_ref, log_ref, acc_ref, top_ref, sum_ref):
    step = pl.program_id(0)
    heads, rows, wide = q_ref.shape
    query = q_ref[...].reshape(heads * rows, wide)
    acc_ref[...] = jnp.zeros_like(acc_ref)
    top_ref[...] = jnp.full(top_ref.shape, -3e38, f32)
    sum_ref[...] = jnp.zeros_like(sum_ref)

    def chunk(j, diagonal):
        at = pl.ds(pl.multiple_of(j * rows, rows), rows)
        scores = mm(k_ref[at, :], query, NT)
        if diagonal:
            key_at = lax.broadcasted_iota(jnp.int32, (rows, rows), 0)
            query_at = lax.broadcasted_iota(jnp.int32, (rows, rows), 1)
            later = jnp.where(key_at > query_at, -1e30, 0.0)
            scores = scores + jnp.concatenate([later] * heads, axis=1)
        top_old = top_ref[...]
        top = jnp.maximum(top_old, jnp.max(scores, axis=0, keepdims=True))
        probs = jnp.exp(scores - top)
        shrink = jnp.exp(top_old - top)
        sum_ref[...] = sum_ref[...] * shrink + jnp.sum(probs, axis=0, keepdims=True)
        acc_ref[...] = acc_ref[...] * shrink + mm(vt_ref[:, at], probs.astype(bf16), NN)
        top_ref[...] = top

    chunk(step, True)

    @pl.loop(0, step)
    def _(j):
        chunk(j, False)

    total = sum_ref[...]
    log_ref[...] = (top_ref[...] + jnp.log(total))[None]
    out = (acc_ref[...] / total).T.astype(bf16)
    out_ref[...] = out.reshape(heads, rows, HEAD)


def attention_forward(query, key, value_t, rows):
    heads, length, wide = query.shape
    steps = length // rows
    return pl.pallas_call(
        forward_kernel,
        out_shape=(
            jax.ShapeDtypeStruct((heads, length, HEAD), bf16),
            jax.ShapeDtypeStruct((steps, 1, heads * rows), f32),
        ),
        grid=(steps,),
        in_specs=[
            pl.BlockSpec((heads, rows, wide), lambda i: (0, i, 0)),
            pl.BlockSpec((length, wide), lambda i: (0, 0)),
            pl.BlockSpec((HEAD, length), lambda i: (0, 0)),
        ],
        out_specs=(
            pl.BlockSpec((heads, rows, HEAD), lambda i: (0, i, 0)),
            pl.BlockSpec((1, 1, heads * rows), lambda i: (i, 0, 0)),
        ),
        scratch_shapes=[
            pltpu.VMEM((HEAD, heads * rows), f32),
            pltpu.VMEM((1, heads * rows), f32),
            pltpu.VMEM((1, heads * rows), f32),
        ],
        compiler_params=pltpu.CompilerParams(vmem_limit_bytes=40 * 2**20),
        cost_estimate=pl.CostEstimate(
            flops=3 * heads * length * length * 128, bytes_accessed=8 * 2**20, transcendentals=0
        ),
    )(query, key, value_t)


def backward_kernel(
    q_ref, k_ref, kt_ref, v_ref, do_ref, log_ref, delta_ref, dq_ref, dk_ref, dv_ref, acc_ref
):
    step = pl.program_id(0)
    heads, rows, wide = q_ref.shape
    query = q_ref[...].reshape(heads * rows, wide)
    d_out = do_ref[...].reshape(heads * rows, HEAD)
    logs = log_ref[0]
    delta = delta_ref[0]

    @pl.when(step == 0)
    def _():
        dk_ref[...] = jnp.zeros_like(dk_ref)
        dv_ref[...] = jnp.zeros_like(dv_ref)

    acc_ref[...] = jnp.zeros_like(acc_ref)

    def chunk(j, diagonal):
        at = pl.ds(pl.multiple_of(j * rows, rows), rows)
        scores = mm(k_ref[at, :], query, NT)
        if diagonal:
            key_at = lax.broadcasted_iota(jnp.int32, (rows, rows), 0)
            query_at = lax.broadcasted_iota(jnp.int32, (rows, rows), 1)
            later = jnp.where(key_at > query_at, -1e30, 0.0)
            scores = scores + jnp.concatenate([later] * heads, axis=1)
        probs = jnp.exp(scores - logs)
        d_probs = mm(v_ref[at, :], d_out, NT)
        d_scores = (probs * (d_probs - delta)).astype(bf16)
        dv_ref[at, :] += mm(probs.astype(bf16), d_out, NN)
        dk_ref[at, :] += mm(d_scores, query, NN)
        acc_ref[...] += mm(kt_ref[:, at], d_scores, NN)

    chunk(step, True)

    @pl.loop(0, step)
    def _(j):
        chunk(j, False)

    out = (acc_ref[...] * HEAD ** (-0.5)).T.astype(bf16)
    dq_ref[...] = out.reshape(heads, rows, HEAD)


def attention_backward(query, key, key_t, value, d_out, logs, delta):
    heads, length, wide = query.shape
    steps = logs.shape[0]
    rows = length // steps
    return pl.pallas_call(
        backward_kernel,
        out_shape=(
            jax.ShapeDtypeStruct((heads, length, HEAD), bf16),
            jax.ShapeDtypeStruct((length, wide), f32),
            jax.ShapeDtypeStruct((length, HEAD), f32),
        ),
        grid=(steps,),
        in_specs=[
            pl.BlockSpec((heads, rows, wide), lambda i: (0, i, 0)),
            pl.BlockSpec((length, wide), lambda i: (0, 0)),
            pl.BlockSpec((HEAD, length), lambda i: (0, 0)),
            pl.BlockSpec((length, HEAD), lambda i: (0, 0)),
            pl.BlockSpec((heads, rows, HEAD), lambda i: (0, i, 0)),
            pl.BlockSpec((1, 1, heads * rows), lambda i: (i, 0, 0)),
            pl.BlockSpec((1, 1, heads * rows), lambda i: (i, 0, 0)),
        ],
        out_specs=(
            pl.BlockSpec((heads, rows, HEAD), lambda i: (0, i, 0)),
            pl.BlockSpec((length, wide), lambda i: (0, 0)),
            pl.BlockSpec((length, HEAD), lambda i: (0, 0)),
        ),
        scratch_shapes=[pltpu.VMEM((HEAD, heads * rows), f32)],
        compiler_params=pltpu.CompilerParams(vmem_limit_bytes=40 * 2**20),
        cost_estimate=pl.CostEstimate(
            flops=8 * heads * length * length * 128, bytes_accessed=8 * 2**20, transcendentals=0
        ),
    )(query, key, key_t, value, d_out, logs, delta)


def slot_kernel(sources, *refs):
    row_refs, cot_refs = refs[:sources], refs[sources : 2 * sources]
    rank_ref, weight_ref, gu_ref, down_ref = refs[2 * sources : 2 * sources + 4]
    x_ref, hid_ref, ds_ref, dgu_ref, dcomb_ref = refs[2 * sources + 4 : 2 * sources + 9]
    moe_refs = refs[2 * sources + 9 : 3 * sources + 9]
    dsum_refs = refs[3 * sources + 9 : 4 * sources + 9]
    moe_acc, dsum_acc = refs[4 * sources + 9 :]
    expert = pl.program_id(0)
    tokens, width = row_refs[0].shape
    cap = x_ref.shape[1] // sources

    @pl.when(expert == 0)
    def _():
        moe_acc[...] = jnp.zeros_like(moe_acc)
        dsum_acc[...] = jnp.zeros_like(dsum_acc)

    slots = lax.broadcasted_iota(jnp.int32, (cap, tokens), 0).astype(f32)
    chosen, picks, cots, slot_weights = [], [], [], []
    for s in range(sources):
        hit = rank_ref[0, s : s + 1, :] == slots
        pick = jnp.where(hit, 1.0, 0.0).astype(bf16)
        chosen.append(hit)
        picks.append(pick)
        x_ref[0, s * cap : (s + 1) * cap, :] = mm(pick, row_refs[s][...], NN).astype(bf16)
        cots.append(mm(pick, cot_refs[s][...], NN))
        slot_weights.append(
            jnp.sum(jnp.where(hit, weight_ref[0, s : s + 1, :], 0.0), axis=1, keepdims=True)
        )
    x_rows = x_ref[0]
    cot = jnp.concatenate(cots, axis=0)
    slot_weight = jnp.concatenate(slot_weights, axis=0)
    gate_up = mm(x_rows, gu_ref[0], NN)
    gate = gate_up[:, :FFE]
    up = gate_up[:, FFE:]
    sig = 1.0 / (1.0 + jnp.exp(-gate))
    silu = gate * sig
    hidden = (silu * up).astype(bf16)
    hid_ref[0] = hidden
    expert_out = mm(hidden, down_ref[0], NN).astype(bf16).astype(f32)
    d_slot = (slot_weight * cot).astype(bf16)
    ds_ref[0] = d_slot
    d_comb = jnp.sum(cot * expert_out, axis=1, keepdims=True)
    weighted = (slot_weight * expert_out).astype(bf16)
    d_hidden = mm(d_slot, down_ref[0], NT)
    d_gate = (d_hidden * up * sig * (1.0 + gate * (1.0 - sig))).astype(bf16)
    d_up = (d_hidden * silu).astype(bf16)
    dgu_ref[0, :, :FFE] = d_gate
    dgu_ref[0, :, FFE:] = d_up
    d_row = mm(dgu_ref[0], gu_ref[0], NT).astype(bf16)
    for s in range(sources):
        part = slice(s * cap, (s + 1) * cap)
        moe_acc[s] += mm(picks[s], weighted[part], TN)
        dsum_acc[s] += mm(picks[s], d_row[part], TN)
        dcomb_ref[0, s : s + 1, :] = jnp.sum(
            jnp.where(chosen[s], d_comb[part], 0.0), axis=0, keepdims=True
        )

    @pl.when(expert == pl.num_programs(0) - 1)
    def _():
        for s in range(sources):
            moe_refs[s][...] = moe_acc[s].astype(bf16)
            dsum_refs[s][...] = dsum_acc[s].astype(bf16)


def expert_slot(rows, cots, ranks, weights, gate_up, down, cap):
    sources = len(rows)
    tokens, width = rows[0].shape
    experts = gate_up.shape[0]
    held = sources * cap
    each = lambda *shape: pl.BlockSpec((1,) + shape, lambda e: (e,) + (0,) * len(shape))
    fixed = pl.BlockSpec((tokens, width), lambda e: (0, 0))
    token_out = jax.ShapeDtypeStruct((tokens, width), bf16)
    got = pl.pallas_call(
        functools.partial(slot_kernel, sources),
        out_shape=(
            jax.ShapeDtypeStruct((experts, held, width), bf16),
            jax.ShapeDtypeStruct((experts, held, FFE), bf16),
            jax.ShapeDtypeStruct((experts, held, width), bf16),
            jax.ShapeDtypeStruct((experts, held, 2 * FFE), bf16),
            jax.ShapeDtypeStruct((experts, sources, tokens), f32),
        )
        + (token_out,) * (2 * sources),
        grid=(experts,),
        in_specs=[fixed] * (2 * sources)
        + [
            each(sources, tokens),
            each(sources, tokens),
            each(width, 2 * FFE),
            each(FFE, width),
        ],
        out_specs=(
            each(held, width),
            each(held, FFE),
            each(held, width),
            each(held, 2 * FFE),
            each(sources, tokens),
        )
        + (fixed,) * (2 * sources),
        scratch_shapes=[
            pltpu.VMEM((sources, tokens, width), f32),
            pltpu.VMEM((sources, tokens, width), f32),
        ],
        compiler_params=pltpu.CompilerParams(vmem_limit_bytes=56 * 2**20),
        cost_estimate=pl.CostEstimate(
            flops=experts * held * width * FFE * 12,
            bytes_accessed=experts * FFE * width * 6 + 8 * held * width * experts,
            transcendentals=0,
        ),
    )(*rows, *cots, ranks, weights, gate_up, down)
    return got[:5], got[5 : 5 + sources], got[5 + sources :]


def grads_kernel(parts, *refs):
    x_refs, dgu_refs = refs[:parts], refs[parts : 2 * parts]
    hid_refs, ds_refs = refs[2 * parts : 3 * parts], refs[3 * parts : 4 * parts]
    gu_ref, down_ref = refs[4 * parts :]
    join = lambda many: jnp.concatenate([r[0] for r in many], axis=0)
    gu_ref[0] = mm(join(x_refs), join(dgu_refs), TN).astype(bf16)
    down_ref[0] = mm(join(hid_refs), join(ds_refs), TN).astype(bf16)


def expert_grads(xs, dgus, hids, dss):
    parts = len(xs)
    experts, _, width = xs[0].shape
    spec = lambda a: pl.BlockSpec((1,) + a.shape[1:], lambda e: (e, 0, 0))
    many = [*xs, *dgus, *hids, *dss]
    return pl.pallas_call(
        functools.partial(grads_kernel, parts),
        out_shape=(
            jax.ShapeDtypeStruct((experts, width, 2 * FFE), bf16),
            jax.ShapeDtypeStruct((experts, FFE, width), bf16),
        ),
        grid=(experts,),
        in_specs=[spec(a) for a in many],
        out_specs=(
            pl.BlockSpec((1, width, 2 * FFE), lambda e: (e, 0, 0)),
            pl.BlockSpec((1, FFE, width), lambda e: (e, 0, 0)),
        ),
        compiler_params=pltpu.CompilerParams(vmem_limit_bytes=56 * 2**20),
        cost_estimate=pl.CostEstimate(
            flops=6 * experts * width * FFE * sum(a.shape[1] for a in xs),
            bytes_accessed=experts * width * FFE * 6 + 30 * 2**20,
            transcendentals=0,
        ),
    )(*many)


def per_device(
    inputs,
    cotangent,
    routes,
    segment_ids,
    parents,
    w_qkv,
    w_out,
    w_router,
    w_gate_up,
    w_down,
    gain_attn,
    gain_moe,
    row_qkv,
    col_qkv,
    row_out,
    col_out,
    row_router,
    col_router,
    row_gate_up,
    col_gate_up,
    row_down,
    col_down,
    second_attn,
    second_moe,
):
    tp_count = lax.axis_size("tp")
    ctx_count = lax.axis_size("ctx")
    fsdp_count = lax.axis_size("fsdp")
    count = tp_count * ctx_count * fsdp_count
    tp_index = lax.axis_index("tp")
    ctx_index = lax.axis_index("ctx")
    fsdp_index = lax.axis_index("fsdp")
    flat_index = fsdp_index * ctx_count + ctx_index
    owner_index = fsdp_index * tp_count + tp_index
    keep_once = (tp_index == 0).astype(f32)
    tok_rows = inputs.shape[0]
    half_rows = tok_rows // tp_count
    tree_len = segment_ids.shape[1]
    tokens_all = tok_rows * fsdp_count * ctx_count
    capacity = half_rows * TOPK * 3 // (2 * EXPERTS)
    groups = fsdp_count * tp_count
    local_experts = EXPERTS // groups
    q_own = HEADS // (tp_count * ctx_count)
    kv_own = KV_HEADS // (tp_count * ctx_count)
    group_size = HEADS // KV_HEADS
    q_cols = q_own * HEAD
    kv_cols = kv_own * HEAD
    own_cols = q_cols + 2 * kv_cols
    dense_rows = w_qkv.shape[0]
    qkv_cols = w_qkv.shape[1]
    dense_parts = fsdp_count * ctx_count
    ctx_rows = w_gate_up.shape[1]
    labels = jnp.arange(EXPERTS, dtype=jnp.int32)

    def by_ctx(columns):
        q_end = ctx_count * q_cols
        k_end = q_end + ctx_count * kv_cols
        lead = columns.shape[:-1]
        return jnp.concatenate(
            [
                columns[..., :q_end].reshape(lead + (ctx_count, q_cols)),
                columns[..., q_end:k_end].reshape(lead + (ctx_count, kv_cols)),
                columns[..., k_end:].reshape(lead + (ctx_count, kv_cols)),
            ],
            axis=-1,
        )

    def from_ctx(columns):
        lead = columns.shape[:-2]
        return jnp.concatenate(
            [
                columns[..., :q_cols].reshape(lead + (-1,)),
                columns[..., q_cols : q_cols + kv_cols].reshape(lead + (-1,)),
                columns[..., q_cols + kv_cols :].reshape(lead + (-1,)),
            ],
            axis=-1,
        )

    w_qkv_low = w_qkv.astype(bf16)
    w_grouped = by_ctx(w_qkv_low)
    extras = jnp.concatenate(
        [gain_attn.astype(bf16)[:, None], gain_moe.astype(bf16)[:, None], w_router.astype(bf16)],
        axis=1,
    )
    w_send = jnp.concatenate(
        [
            jnp.moveaxis(w_grouped, 1, 0),
            jnp.broadcast_to(extras[None], (ctx_count,) + extras.shape),
        ],
        axis=-1,
    )
    w_send = jnp.broadcast_to(w_send[None], (fsdp_count,) + w_send.shape)
    w_got = exchange(w_send.reshape((dense_parts,) + w_send.shape[2:]), ("fsdp", "ctx"))
    w_got = w_got.reshape(D, own_cols + 2 + EXPERTS)
    parts = inputs[None]
    arrived = parts
    bit = ctx_count // 2
    while bit:
        other = partner(parts, "ctx", bit, ctx_count)
        arrived = other if bit == ctx_count // 2 else arrived
        parts = in_order(parts, other, (ctx_index // bit) % 2, 1).reshape((-1,) + inputs.shape)
        bit //= 2
    tree_inputs = parts.reshape(tree_len, D).astype(f32)
    w_own = w_got[:, :own_cols]
    gain_one = w_got[:, own_cols].astype(f32)
    gain_two = w_got[:, own_cols + 1].astype(f32)
    router_full = w_got[:, own_cols + 2 :]

    my_routes = lax.dynamic_slice_in_dim(routes, tp_index * half_rows, half_rows, 0)
    hit = jnp.sum((my_routes[..., None] == labels).astype(f32), axis=1)
    counts = jnp.sum(share(jnp.sum(hit, axis=0), count), axis=0)
    fraction = counts / (tokens_all * TOPK)
    master_sums = jnp.stack(
        [
            jnp.sum(w_qkv * w_qkv),
            jnp.sum(w_out * w_out),
            keep_once * jnp.sum(w_router * w_router),
            jnp.sum(w_gate_up * w_gate_up),
            jnp.sum(w_down * w_down),
            keep_once * jnp.sum(gain_attn * gain_attn),
            keep_once * jnp.sum(gain_moe * gain_moe),
        ]
    )
    before = (
        jnp.arange(half_rows, dtype=jnp.int32)[:, None]
        < jnp.arange(half_rows, dtype=jnp.int32)[None, :]
    ).astype(bf16)
    rank = dot("te,tu->eu", hit.astype(bf16), before)
    rank = jnp.where(hit.T > 0.5, rank, -1.0)
    ranks = exchange(rank.reshape(groups, local_experts, half_rows), ("fsdp", "tp"))
    ranks = ranks.reshape(fsdp_count, tp_count, local_experts, half_rows)

    def relative(values):
        return xor_order(xor_order(values, 0, fsdp_index), 1, tp_index)

    ranks = relative(ranks)

    def spread(block):
        near = [block] + [partner(block, "fsdp", j, fsdp_count) for j in range(1, fsdp_count)]
        return [[b] + [partner(b, "tp", y, tp_count) for y in range(1, tp_count)] for b in near]

    grad_slots = spread(after(cotangent, w_got))
    gate_up_low = after(w_gate_up.astype(bf16), arrived)
    down_low = after(w_down.astype(bf16), arrived)
    gate_up_all = lax.all_gather(gate_up_low, "ctx", axis=1, tiled=True)
    down_all = lax.all_gather(down_low, "ctx", axis=2, tiled=True)
    out_rows = w_out.shape[0]
    out_t = jnp.broadcast_to(w_out.astype(bf16).T, (dense_parts, dense_rows, out_rows))
    out_t = exchange(after(out_t, w_got), ("fsdp", "ctx")).reshape(1, D, out_rows)
    other = partner(out_t, "tp", 1, tp_count)
    out_t = in_order(out_t, other, tp_index, 1).reshape(tp_count, D, out_rows)
    qkv_full = lax.all_gather(
        after(w_grouped, down_all).reshape(dense_rows, qkv_cols), ("tp", "fsdp", "ctx"), axis=0, tiled=True
    ).reshape(tp_count, D, qkv_cols)

    act1 = (tree_inputs * inv_rms(tree_inputs) * gain_one).astype(bf16)
    qkv = dot("td,dc->tc", act1, w_own).astype(bf16)
    query = (qkv[:, :q_cols] * HEAD ** (-0.5)).reshape(tree_len, kv_own, group_size, HEAD)
    query = query.transpose(1, 2, 0, 3)
    keys = qkv[:, q_cols : q_cols + kv_cols].reshape(tree_len, kv_own, HEAD).transpose(1, 0, 2)
    values = qkv[:, q_cols + kv_cols :].reshape(tree_len, kv_own, HEAD).transpose(1, 0, 2)
    seg_hot = (segment_ids[0][:, None] == jnp.arange(NSEG, dtype=jnp.int32)).astype(bf16)
    hidden_from = (1.0 - ancestry(parents[0])) * -1e30
    barred = dot("qs,su->qu", seg_hot, hidden_from.astype(bf16)).astype(bf16)
    lanes = 2 * HEAD
    spare = lanes - HEAD - NSEG
    barred = jnp.pad(barred, ((0, 0), (0, spare)))
    seg_hot = jnp.pad(seg_hot, ((0, 0), (0, spare)))
    query = jnp.concatenate(
        [query, jnp.broadcast_to(barred, query.shape[:2] + barred.shape)], axis=-1
    )
    keys_wide = jnp.concatenate(
        [keys, jnp.broadcast_to(seg_hot, (kv_own,) + seg_hot.shape)], axis=-1
    )
    step_rows = half_rows
    steps = tree_len // step_rows
    outs, logs = [], []
    for h in range(kv_own):
        out_h, log_h = attention_forward(query[h], keys_wide[h], values[h].T, step_rows)
        outs.append(out_h)
        logs.append(log_h)
    attended_heads = jnp.concatenate(outs, axis=0)
    attended_own = attended_heads.transpose(1, 0, 2).reshape(tree_len, q_cols)
    attended = exchange(attended_own, ("ctx", "tp")).reshape(ctx_count, tp_count, half_rows, q_cols)
    attended = attended.transpose(2, 1, 0, 3).reshape(half_rows, tp_count, ctx_count * q_cols)
    inputs_half = lax.dynamic_slice_in_dim(inputs, tp_index * half_rows, half_rows, 0).astype(f32)
    x_one = inputs_half + dot("rtk,tdk->rd", attended, out_t)

    inv_two = inv_rms(x_one)
    act2 = (x_one * inv_two * gain_two).astype(bf16)
    row_slots = spread(act2)
    logits = dot("td,de->te", act2, router_full)
    router_probs = jax.nn.softmax(logits, axis=-1)
    combine = jax.nn.softmax(jnp.where(hit > 0.5, logits, -jnp.inf), axis=-1)
    weights = exchange(combine.T.reshape(groups, local_experts, half_rows), ("fsdp", "tp"))

    weights = weights.reshape(fsdp_count, tp_count, local_experts, half_rows)
    weights = relative(weights)
    kept, d_combines, moe_parts, d_parts = [], [], [], []
    for chunk in [[j] for j in range(fsdp_count)]:
        rows = [r for j in chunk for r in row_slots[j]]
        cots = [c for j in chunk for c in grad_slots[j]]
        pieces = lambda a: a[chunk[0] : chunk[-1] + 1].reshape(-1, local_experts, half_rows)
        held, moe_out, d_out = expert_slot(
            rows,
            cots,
            pieces(ranks).transpose(1, 0, 2),
            pieces(weights).transpose(1, 0, 2),
            gate_up_all,
            down_all,
            capacity,
        )
        kept.append(held[:4])
        d_combines.append(held[4])
        for n, j in enumerate(chunk):
            moe_parts.append(moe_out[n * tp_count : (n + 1) * tp_count])
            d_parts.append(d_out[n * tp_count : (n + 1) * tp_count])

    def collect(parts):
        total = 0.0
        for j in range(fsdp_count):
            block = parts[j][0].astype(f32)
            for y in range(1, tp_count):
                block = block + partner(parts[j][y], "tp", y, tp_count).astype(f32)
            if j:
                block = partner(block.astype(bf16), "fsdp", j, fsdp_count).astype(f32)
            total = total + block
        return total

    d_combine = jnp.concatenate(d_combines, axis=1).transpose(1, 0, 2)
    d_combine = d_combine.reshape(fsdp_count, tp_count, local_experts, half_rows)
    d_combine = relative(d_combine).reshape(groups, local_experts, half_rows)
    d_combine = exchange(d_combine, ("fsdp", "tp")).reshape(EXPERTS, half_rows).T
    d_act2 = collect(d_parts)
    g_gate_up_local, g_down_local = expert_grads(
        [k[0] for k in kept], [k[3] for k in kept], [k[1] for k in kept], [k[2] for k in kept]
    )
    g_gate_up = lax.psum_scatter(
        g_gate_up_local, "ctx", scatter_dimension=1, tiled=True
    ).astype(f32)
    g_down = lax.psum_scatter(
        g_down_local, "ctx", scatter_dimension=2, tiled=True
    ).astype(f32)

    aux_grad = aux_weight * EXPERTS * fraction
    d_logits = combine * (d_combine - jnp.sum(combine * d_combine, axis=-1, keepdims=True))
    d_logits = d_logits + router_probs * (
        aux_grad - jnp.sum(router_probs * aux_grad, axis=-1, keepdims=True)
    )
    d_logits = d_logits.astype(bf16)
    d_act2 = d_act2 + dot("te,de->td", d_logits, router_full)
    d_half, normed_two = norm_backward(x_one, inv_two, gain_two, d_act2)
    d_x1_half = cotangent.astype(f32) + d_half
    d_x1_low = d_x1_half.astype(bf16)
    g_small = jnp.concatenate(
        [dot("te,td->ed", d_logits, act2), jnp.sum(d_act2 * normed_two, axis=0)[None]], axis=0
    )
    g_small = jnp.moveaxis(g_small.reshape(EXPERTS + 1, dense_parts, dense_rows), 1, 0)
    g_small = jnp.broadcast_to(g_small[:, None], (dense_parts, tp_count) + g_small.shape[1:])
    g_small = exchange(g_small.reshape((count,) + g_small.shape[2:]), EVERY)
    g_small = jnp.sum(g_small, axis=0)
    g_router = g_small[:EXPERTS].T
    g_gain2 = g_small[EXPERTS]

    d_attended = dot("rd,tdk->rtk", d_x1_low, out_t).astype(bf16)
    d_attended = d_attended.reshape(half_rows, tp_count, ctx_count, q_cols).transpose(2, 1, 0, 3)
    d_attended = exchange(d_attended.reshape(tree_len, q_cols), ("ctx", "tp"))
    late_parts = [[after(p, d_attended) for p in part] for part in moe_parts]
    d_heads = d_attended.reshape(tree_len, q_own, HEAD).transpose(1, 0, 2)
    delta = jnp.sum(d_heads.astype(f32) * attended_heads.astype(f32), axis=-1)
    delta = delta.reshape(kv_own, group_size, steps, step_rows).transpose(0, 2, 1, 3)
    delta = delta.reshape(kv_own, steps, 1, group_size * step_rows)
    d_heads = d_heads.reshape(kv_own, group_size, tree_len, HEAD)
    d_q, d_k, d_v = [], [], []
    for h in range(kv_own):
        dq_h, dk_h, dv_h = attention_backward(
            query[h], keys_wide[h], keys[h].T, values[h], d_heads[h], logs[h], delta[h]
        )
        d_q.append(dq_h.transpose(1, 0, 2).reshape(tree_len, -1))
        d_k.append(dk_h[:, :HEAD].astype(bf16))
        d_v.append(dv_h.astype(bf16))
    d_qkv = jnp.concatenate(d_q + d_k + d_v, axis=1)
    g_qkv_part = dot("td,tc->dc", act1, d_qkv).astype(bf16)
    g_qkv_got = exchange(g_qkv_part.reshape(dense_parts, dense_rows, own_cols), ("fsdp", "ctx"))
    g_qkv_got = g_qkv_got.reshape(fsdp_count, ctx_count, dense_rows, own_cols).astype(f32)
    g_qkv = from_ctx(jnp.moveaxis(jnp.sum(g_qkv_got, axis=0), 0, 1))
    d_qkv_send = jnp.broadcast_to(
        d_qkv.reshape(ctx_count, 1, tok_rows, own_cols), (ctx_count, tp_count, tok_rows, own_cols)
    )
    d_qkv_all = exchange(d_qkv_send.reshape(-1, tok_rows, own_cols), ("ctx", "tp"))
    d_qkv_all = d_qkv_all.reshape(ctx_count, tp_count, tok_rows, own_cols)
    d_qkv_all = d_qkv_all.transpose(2, 1, 0, 3).reshape(tok_rows, tp_count, qkv_cols)
    d_act1 = dot("rtc,tdc->rd", d_qkv_all, qkv_full)
    own_inputs = inputs.astype(f32)
    d_inputs_attn, _ = norm_backward(own_inputs, inv_rms(own_inputs), gain_one, d_act1)
    d_x1_own = after(d_x1_half, d_attended)[None]
    other = partner(d_x1_own, "tp", 1, tp_count)
    d_x1 = in_order(d_x1_own, other, tp_index, 1).reshape(tok_rows, D)
    layer_out = (x_one + collect(late_parts)).astype(bf16)
    grad_inputs = d_x1 + d_inputs_attn

    attended_t = attended.transpose(1, 0, 2)
    attended_pair = exchange(attended_t, "tp").reshape(tok_rows, -1)
    d_x1_pair = d_x1.astype(bf16)
    g_out_part = dot("td,tq->dq", d_x1_pair, attended_pair).astype(bf16)
    g_out_got = exchange(g_out_part.reshape(dense_parts, dense_rows, -1), ("fsdp", "ctx"))
    g_out = jnp.sum(g_out_got.astype(f32), axis=0).T

    sq_out = g_out * g_out
    sq_router = g_router * g_router
    first = jnp.concatenate(
        [
            jnp.sum(sq_out, axis=1),
            jnp.sum(sq_out, axis=0),
            jnp.sum(sq_router, axis=1),
            jnp.sum(sq_router, axis=0),
            jnp.sum(router_probs, axis=0),
            master_sums,
        ]
    )
    first = share(first, count).reshape(dense_parts, tp_count, -1)
    at = [out_rows, out_rows + dense_rows, out_rows + 2 * dense_rows]
    at.append(at[-1] + EXPERTS)
    tot_row_out = jnp.sum(first[..., : at[0]], axis=0).reshape(-1)
    tot_col_out = jnp.sum(first[..., at[0] : at[1]], axis=1).reshape(-1)
    tot_row_router = first[:, 0, at[1] : at[2]].reshape(-1)
    tot_col_router = jnp.sum(first[:, 0, at[2] : at[3]], axis=0)
    last_totals = jnp.sum(first[..., at[3] :], axis=(0, 1))
    prob_totals = last_totals[:EXPERTS]
    master_totals = last_totals[EXPERTS:]

    sq_gate_up = g_gate_up * g_gate_up
    sq_down = g_down * g_down
    expert_parts = jnp.concatenate(
        [
            jnp.sum(sq_gate_up, axis=2),
            jnp.sum(sq_down, axis=1),
            jnp.sum(sq_gate_up, axis=1),
            jnp.sum(sq_down, axis=2),
        ],
        axis=1,
    )
    expert_got = share(expert_parts, count).reshape(
        fsdp_count, ctx_count, tp_count, local_experts, -1
    )
    split_rows = expert_got[..., : 2 * ctx_rows].transpose(0, 2, 3, 1, 4)
    summed = jnp.sum(expert_got[..., 2 * ctx_rows :], axis=1).reshape(EXPERTS, -1)
    tot_row_gu = split_rows[..., :ctx_rows].reshape(EXPERTS, D)
    tot_col_down = split_rows[..., ctx_rows:].reshape(EXPERTS, D)
    tot_col_gu = summed[:, : 2 * FFE]
    tot_row_down = summed[:, 2 * FFE :]

    sq_qkv = g_qkv * g_qkv
    gain_part = jnp.sum(g_qkv * w_qkv_low.astype(f32), axis=1) / gain_attn.astype(bf16).astype(f32)
    second = jnp.concatenate([jnp.sum(sq_qkv, axis=1), gain_part, jnp.sum(sq_qkv, axis=0)])
    second = share(second, count).reshape(dense_parts, tp_count, -1)
    tot_row_qkv = jnp.sum(second[..., :dense_rows], axis=1).reshape(-1)
    g_gain1_all = jnp.sum(second[..., dense_rows : 2 * dense_rows], axis=1)
    g_gain1 = lax.dynamic_index_in_dim(g_gain1_all, flat_index, 0, keepdims=False)
    tot_col_qkv = jnp.sum(second[..., 2 * dense_rows :], axis=0).reshape(-1)

    qkv_width = (HEADS + 2 * KV_HEADS) * HEAD
    row_qkv_new = decay * row_qkv + (1.0 - decay) * (tot_row_qkv / qkv_width + floor_sq)
    col_qkv_new = decay * col_qkv + (1.0 - decay) * (tot_col_qkv / D + floor_sq)
    row_out_new = decay * row_out + (1.0 - decay) * (tot_row_out / D + floor_sq)
    col_out_new = decay * col_out + (1.0 - decay) * (tot_col_out / (HEADS * HEAD) + floor_sq)
    row_router_new = decay * row_router + (1.0 - decay) * (tot_row_router / EXPERTS + floor_sq)
    col_router_new = decay * col_router + (1.0 - decay) * (tot_col_router / D + floor_sq)
    row_gu_new = decay * row_gate_up + (1.0 - decay) * (tot_row_gu / (2 * FFE) + floor_sq)
    col_gu_new = decay * col_gate_up + (1.0 - decay) * (tot_col_gu / D + floor_sq)
    row_down_new = decay * row_down + (1.0 - decay) * (tot_row_down / D + floor_sq)
    col_down_new = decay * col_down + (1.0 - decay) * (tot_col_down / FFE + floor_sq)
    aux_loss = EXPERTS * jnp.sum(fraction * prob_totals / tokens_all)

    expert_start = owner_index * local_experts
    rows_here = lax.dynamic_slice_in_dim(row_qkv_new, flat_index * dense_rows, dense_rows, 0)
    cols_here = lax.dynamic_slice_in_dim(col_qkv_new, tp_index * qkv_cols, qkv_cols, 0)
    change_qkv = g_qkv * lax.rsqrt(rows_here[:, None] * cols_here[None, :] / jnp.mean(row_qkv_new))
    rows_here = lax.dynamic_slice_in_dim(row_out_new, tp_index * out_rows, out_rows, 0)
    cols_here = lax.dynamic_slice_in_dim(col_out_new, flat_index * dense_rows, dense_rows, 0)
    change_out = g_out * lax.rsqrt(rows_here[:, None] * cols_here[None, :] / jnp.mean(row_out_new))
    rows_here = lax.dynamic_slice_in_dim(row_router_new, flat_index * dense_rows, dense_rows, 0)
    change_router = g_router * lax.rsqrt(
        rows_here[:, None] * col_router_new[None, :] / jnp.mean(row_router_new)
    )
    start_pair = (
        jnp.asarray(expert_start, jnp.int32),
        jnp.asarray(ctx_index * ctx_rows, jnp.int32),
    )
    zero_start = jnp.asarray(0, jnp.int32)
    rows_gu = lax.dynamic_slice(row_gu_new, start_pair, (local_experts, ctx_rows))
    cols_gu = lax.dynamic_slice(col_gu_new, (start_pair[0], zero_start), (local_experts, 2 * FFE))
    mean_gu = lax.dynamic_slice_in_dim(
        jnp.mean(row_gu_new, axis=-1), expert_start, local_experts, 0
    )
    change_gate_up = g_gate_up * lax.rsqrt(
        rows_gu[:, :, None] * cols_gu[:, None, :] / mean_gu[:, None, None]
    )
    rows_dn = lax.dynamic_slice(row_down_new, (start_pair[0], zero_start), (local_experts, FFE))
    cols_dn = lax.dynamic_slice(col_down_new, start_pair, (local_experts, ctx_rows))
    mean_dn = lax.dynamic_slice_in_dim(
        jnp.mean(row_down_new, axis=-1), expert_start, local_experts, 0
    )
    change_down = g_down * lax.rsqrt(
        rows_dn[:, :, None] * cols_dn[:, None, :] / mean_dn[:, None, None]
    )
    second_attn_new = decay * second_attn + (1.0 - decay) * (g_gain1 * g_gain1 + floor_sq)
    second_moe_new = decay * second_moe + (1.0 - decay) * (g_gain2 * g_gain2 + floor_sq)
    change_gain1 = g_gain1 * lax.rsqrt(second_attn_new)
    change_gain2 = g_gain2 * lax.rsqrt(second_moe_new)
    square_sums = jnp.stack(
        [
            jnp.sum(change_qkv * change_qkv),
            jnp.sum(change_out * change_out),
            keep_once * jnp.sum(change_router * change_router),
            jnp.sum(change_gate_up * change_gate_up),
            jnp.sum(change_down * change_down),
            keep_once * jnp.sum(change_gain1 * change_gain1),
            keep_once * jnp.sum(change_gain2 * change_gain2),
        ]
    )
    square_totals = jnp.sum(share(square_sums, count), axis=0)
    entries = jnp.array(
        [
            D * qkv_width,
            HEADS * HEAD * D,
            D * EXPERTS,
            EXPERTS * D * 2 * FFE,
            EXPERTS * FFE * D,
            D,
            D,
        ],
        f32,
    )
    update_rms = jnp.sqrt(square_totals / entries)
    weight_rms = jnp.sqrt(master_totals / entries)
    step_scale = rate * weight_rms / jnp.maximum(clip_rms, update_rms)
    new_qkv = w_qkv - step_scale[0] * change_qkv
    new_out = w_out - step_scale[1] * change_out
    new_router = w_router - step_scale[2] * change_router
    new_gate_up = w_gate_up - step_scale[3] * change_gate_up
    new_down = w_down - step_scale[4] * change_down
    new_gain1 = gain_attn - step_scale[5] * change_gain1
    new_gain2 = gain_moe - step_scale[6] * change_gain2
    return (
        layer_out,
        grad_inputs,
        aux_loss,
        g_qkv,
        g_out,
        g_router,
        g_gate_up,
        g_down,
        g_gain1,
        g_gain2,
        new_qkv,
        new_out,
        new_router,
        new_gate_up,
        new_down,
        new_gain1,
        new_gain2,
        new_qkv.astype(bf16),
        new_out.astype(bf16),
        new_router.astype(bf16),
        new_gate_up.astype(bf16),
        new_down.astype(bf16),
        new_gain1.astype(bf16),
        new_gain2.astype(bf16),
        row_qkv_new,
        col_qkv_new,
        row_out_new,
        col_out_new,
        row_router_new,
        col_router_new,
        row_gu_new,
        col_gu_new,
        row_down_new,
        col_down_new,
        second_attn_new,
        second_moe_new,
        update_rms,
    )


def solution(mesh):
    placed = (
        P(("fsdp", "ctx"), None),
        P(("fsdp", "ctx", "tp"), None),
        P(("fsdp", "ctx"), None),
        P("fsdp", None),
        P("fsdp", None),
        P(("fsdp", "ctx"), "tp"),
        P("tp", ("fsdp", "ctx")),
        P(("fsdp", "ctx"), None),
        P(("fsdp", "tp"), "ctx", None),
        P(("fsdp", "tp"), None, "ctx"),
        P(("fsdp", "ctx")),
        P(("fsdp", "ctx")),
        P(),
        P(),
        P(),
        P(),
        P(),
        P(),
        P(),
        P(),
        P(),
        P(),
        P(("fsdp", "ctx")),
        P(("fsdp", "ctx")),
    )
    return jax.shard_map(
        per_device,
        mesh=mesh,
        in_specs=placed,
        out_specs=(
            P(("fsdp", "ctx", "tp"), None),
            P(("fsdp", "ctx"), None),
            P(),
            P(("fsdp", "ctx"), "tp"),
            P("tp", ("fsdp", "ctx")),
            P(("fsdp", "ctx"), None),
            P(("fsdp", "tp"), "ctx", None),
            P(("fsdp", "tp"), None, "ctx"),
            P(("fsdp", "ctx")),
            P(("fsdp", "ctx")),
            P(("fsdp", "ctx"), "tp"),
            P("tp", ("fsdp", "ctx")),
            P(("fsdp", "ctx"), None),
            P(("fsdp", "tp"), "ctx", None),
            P(("fsdp", "tp"), None, "ctx"),
            P(("fsdp", "ctx")),
            P(("fsdp", "ctx")),
            P(("fsdp", "ctx"), "tp"),
            P("tp", ("fsdp", "ctx")),
            P(("fsdp", "ctx"), None),
            P(("fsdp", "tp"), "ctx", None),
            P(("fsdp", "tp"), None, "ctx"),
            P(("fsdp", "ctx")),
            P(("fsdp", "ctx")),
            P(),
            P(),
            P(),
            P(),
            P(),
            P(),
            P(),
            P(),
            P(),
            P(),
            P(("fsdp", "ctx")),
            P(("fsdp", "ctx")),
            P(),
        ),
        check_vma=False,
    )
```

```python
import functools

import jax
import jax.numpy as jnp
from jax import lax
from jax.experimental import pallas as pl
from jax.experimental.pallas import tpu as pltpu
from jax.sharding import PartitionSpec as P

D = 1536
HEADS = 24
KV_HEADS = 8
HEAD = 64
FFE = 512
TOPK = 8
EXPERTS = 32
NSEG = 13

norm_eps = 1e-05
decay = 0.5
floor_sq = 1e-30
rate = 0.25
clip_rms = 0.05
aux_weight = 1.0
bf16 = jnp.bfloat16
f32 = jnp.float32
EVERY = ("fsdp", "ctx", "tp")
EXTRA = 128

def lasting(microseconds):
    flops = int(microseconds * 1.15e9)
    return pl.CostEstimate(flops=flops, bytes_accessed=1, transcendentals=0)
NT = (((1,), (1,)), ((), ()))
NN = (((1,), (0,)), ((), ()))
TN = (((0,), (0,)), ((), ()))


def dot(spec, left, right):
    return jnp.einsum(spec, left, right, preferred_element_type=f32)


def exchange(values, axes):
    return lax.all_to_all(values, axes, split_axis=0, concat_axis=0, tiled=True)


def share(vector, count):
    return exchange(jnp.broadcast_to(vector[None], (count,) + vector.shape), EVERY)


def inv_rms(values):
    return lax.rsqrt(jnp.mean(values * values, axis=-1, keepdims=True) + norm_eps)


def norm_backward(values, inv, gain, d_out):
    normed = values * inv
    scaled = d_out * gain
    d_values = inv * (scaled - normed * jnp.mean(scaled * normed, axis=-1, keepdims=True))
    return d_values, normed


def ancestry(parent_row):
    seg_labels = jnp.arange(NSEG, dtype=jnp.int32)
    table = jnp.maximum(
        (seg_labels[:, None] == seg_labels[None, :]).astype(f32),
        (parent_row[:, None] == seg_labels[None, :]).astype(f32),
    )
    for sweep in range(NSEG.bit_length()):
        table = jnp.max(table[:, :, None] * table[None, :, :], axis=1)
    return table


def partner(values, axis, bits, count):
    return lax.ppermute(values, axis, [(i, i ^ bits) for i in range(count)])


def after(values, *others):
    return lax.optimization_barrier((values,) + others)[0]


def in_order(mine, other, bit, axis):
    first = jnp.where(bit == 0, mine, other)
    second = jnp.where(bit == 0, other, mine)
    return jnp.stack([first, second], axis=axis)


def mm(left, right, dims):
    return lax.dot_general(left, right, dims, preferred_element_type=f32)


def project_kernel(
    count, index_ref, *refs
):
    block_refs = refs[:count]
    w_ref, gain_ref, barred_ref, seg_ref = refs[count : count + 4]
    act_ref, q_ref, k_ref, kt_ref, v_ref, vt_ref = refs[count + 4 :]
    heads = q_ref.shape[0]
    place = pl.program_id(0) // (pl.num_programs(0) // count) ^ index_ref[0]
    block = block_refs[0][...]
    for j in range(1, count):
        block = jnp.where(place == j, block_refs[j][...], block)
    block = block.astype(f32)
    inv = lax.rsqrt(jnp.mean(block * block, axis=-1, keepdims=True) + norm_eps)
    act = (block * inv * gain_ref[...]).astype(bf16)
    act_ref[...] = act
    qkv = mm(act, w_ref[...], NN).astype(bf16).astype(f32)
    barred = barred_ref[...].astype(f32)
    for h in range(heads):
        query = qkv[:, h * HEAD : (h + 1) * HEAD] * HEAD ** (-0.5)
        q_ref[h] = jnp.concatenate([query, barred], axis=1).astype(bf16)
    key = qkv[:, heads * HEAD : (heads + 1) * HEAD]
    value = qkv[:, (heads + 1) * HEAD : (heads + 2) * HEAD]
    k_ref[...] = jnp.concatenate([key, seg_ref[...].astype(f32)], axis=1).astype(bf16)
    kt_ref[...] = key.T.astype(bf16)
    v_ref[...] = value.astype(bf16)
    vt_ref[...] = value.T.astype(bf16)


def project(blocks, index, weights, gain, barred, seg_hot, heads, rows):
    count = len(blocks)
    tok_rows, width = blocks[0].shape
    per = tok_rows // rows
    length = count * tok_rows
    wide = 2 * HEAD

    def place(j):
        def at(i, s):
            return (jnp.where((i // per ^ s[0]) == j, i % per, 0), 0)

        return at

    whole = lambda a: pl.BlockSpec(a.shape, lambda i, s: (0,) * a.ndim)
    by_rows = lambda columns: pl.BlockSpec((rows, columns), lambda i, s: (i, 0))
    return pl.pallas_call(
        functools.partial(project_kernel, count),
        out_shape=(
            jax.ShapeDtypeStruct((length, width), bf16),
            jax.ShapeDtypeStruct((heads, length, wide), bf16),
            jax.ShapeDtypeStruct((length, wide), bf16),
            jax.ShapeDtypeStruct((HEAD, length), bf16),
            jax.ShapeDtypeStruct((length, HEAD), bf16),
            jax.ShapeDtypeStruct((HEAD, length), bf16),
        ),
        grid_spec=pltpu.PrefetchScalarGridSpec(
            num_scalar_prefetch=1,
            grid=(length // rows,),
            in_specs=[pl.BlockSpec((rows, width), place(j)) for j in range(count)]
            + [whole(weights), whole(gain), by_rows(HEAD), by_rows(HEAD)],
            out_specs=(
                by_rows(width),
                pl.BlockSpec((heads, rows, wide), lambda i, s: (0, i, 0)),
                by_rows(wide),
                pl.BlockSpec((HEAD, rows), lambda i, s: (0, i)),
                by_rows(HEAD),
                pl.BlockSpec((HEAD, rows), lambda i, s: (0, i)),
            ),
        ),
        compiler_params=pltpu.CompilerParams(vmem_limit_bytes=40 * 2**20),
        cost_estimate=lasting(3.3),
    )(index, *blocks, weights, gain, barred, seg_hot)


def forward_kernel(q_ref, k_ref, vt_ref, out_ref, log_ref, acc_ref, top_ref, sum_ref):
    step = pl.program_id(0)
    heads, rows, wide = q_ref.shape
    query = q_ref[...].reshape(heads * rows, wide)
    acc_ref[...] = jnp.zeros_like(acc_ref)
    top_ref[...] = jnp.full(top_ref.shape, -3e38, f32)
    sum_ref[...] = jnp.zeros_like(sum_ref)

    def chunk(j, diagonal):
        at = pl.ds(pl.multiple_of(j * rows, rows), rows)
        scores = mm(k_ref[at, :], query, NT)
        if diagonal:
            key_at = lax.broadcasted_iota(jnp.int32, (rows, rows), 0)
            query_at = lax.broadcasted_iota(jnp.int32, (rows, rows), 1)
            later = jnp.where(key_at > query_at, -1e30, 0.0)
            scores = scores + jnp.concatenate([later] * heads, axis=1)
        top_old = top_ref[...]
        top = jnp.maximum(top_old, jnp.max(scores, axis=0, keepdims=True))
        probs = jnp.exp(scores - top)
        shrink = jnp.exp(top_old - top)
        sum_ref[...] = sum_ref[...] * shrink + jnp.sum(probs, axis=0, keepdims=True)
        acc_ref[...] = acc_ref[...] * shrink + mm(vt_ref[:, at], probs.astype(bf16), NN)
        top_ref[...] = top

    chunk(step, True)

    @pl.loop(0, step)
    def _(j):
        chunk(j, False)

    total = sum_ref[...]
    log_ref[...] = (top_ref[...] + jnp.log(total))[None]
    out = acc_ref[...] / total
    for h in range(heads):
        out_ref[0, h * HEAD : (h + 1) * HEAD, :] = out[:, h * rows : (h + 1) * rows].astype(bf16)


def attention_forward(query, key, value_t, rows):
    heads, length, wide = query.shape
    steps = length // rows
    return pl.pallas_call(
        forward_kernel,
        out_shape=(
            jax.ShapeDtypeStruct((steps, heads * HEAD, rows), bf16),
            jax.ShapeDtypeStruct((steps, 1, heads * rows), f32),
        ),
        grid=(steps,),
        in_specs=[
            pl.BlockSpec((heads, rows, wide), lambda i: (0, i, 0)),
            pl.BlockSpec((length, wide), lambda i: (0, 0)),
            pl.BlockSpec((HEAD, length), lambda i: (0, 0)),
        ],
        out_specs=(
            pl.BlockSpec((1, heads * HEAD, rows), lambda i: (i, 0, 0)),
            pl.BlockSpec((1, 1, heads * rows), lambda i: (i, 0, 0)),
        ),
        scratch_shapes=[
            pltpu.VMEM((HEAD, heads * rows), f32),
            pltpu.VMEM((1, heads * rows), f32),
            pltpu.VMEM((1, heads * rows), f32),
        ],
        compiler_params=pltpu.CompilerParams(vmem_limit_bytes=40 * 2**20),
        cost_estimate=lasting(7.5),
    )(query, key, value_t)


def backward_kernel(
    q_ref, k_ref, kt_ref, v_ref, do_ref, out_ref, log_ref, dq_ref, dkv_ref, acc_ref, dk_ref, dv_ref
):
    step = pl.program_id(0)
    heads, rows, wide = q_ref.shape
    query = q_ref[...].reshape(heads * rows, wide)
    side_by_side = lambda a: jnp.concatenate(
        [a[h * HEAD : (h + 1) * HEAD] for h in range(heads)], axis=1
    )
    d_out = side_by_side(do_ref[0])
    products = side_by_side(do_ref[0].astype(f32) * out_ref[0].astype(f32))
    delta = jnp.sum(products, axis=0, keepdims=True)
    logs = log_ref[0]

    @pl.when(step == 0)
    def _():
        dk_ref[...] = jnp.zeros_like(dk_ref)
        dv_ref[...] = jnp.zeros_like(dv_ref)

    acc_ref[...] = jnp.zeros_like(acc_ref)

    def chunk(j, diagonal):
        at = pl.ds(pl.multiple_of(j * rows, rows), rows)
        scores = mm(k_ref[at, :], query, NT)
        if diagonal:
            key_at = lax.broadcasted_iota(jnp.int32, (rows, rows), 0)
            query_at = lax.broadcasted_iota(jnp.int32, (rows, rows), 1)
            later = jnp.where(key_at > query_at, -1e30, 0.0)
            scores = scores + jnp.concatenate([later] * heads, axis=1)
        probs = jnp.exp(scores - logs)
        d_probs = mm(v_ref[at, :], d_out, NN)
        d_scores = (probs * (d_probs - delta)).astype(bf16)
        dv_ref[at, :] += mm(probs.astype(bf16), d_out, NT)
        dk_ref[at, :] += mm(d_scores, query, NN)
        acc_ref[...] += mm(kt_ref[:, at], d_scores, NN)

    chunk(step, True)

    @pl.loop(0, step)
    def _(j):
        chunk(j, False)

    out = acc_ref[...] * HEAD ** (-0.5)
    out = jnp.concatenate([out[:, h * rows : (h + 1) * rows] for h in range(heads)], axis=0)
    dq_ref[...] = out.T.astype(bf16)

    @pl.when(step == pl.num_programs(0) - 1)
    def _():
        dkv_ref[...] = jnp.concatenate([dk_ref[:, :HEAD], dv_ref[...]], axis=1).astype(bf16)


def attention_backward(query, key, key_t, value, d_out, out, logs):
    heads, length, wide = query.shape
    steps = logs.shape[0]
    rows = length // steps
    by_rows = pl.BlockSpec((rows, heads * HEAD), lambda i: (i, 0))
    return pl.pallas_call(
        backward_kernel,
        out_shape=(
            jax.ShapeDtypeStruct((length, heads * HEAD), bf16),
            jax.ShapeDtypeStruct((length, 2 * HEAD), bf16),
        ),
        grid=(steps,),
        in_specs=[
            pl.BlockSpec((heads, rows, wide), lambda i: (0, i, 0)),
            pl.BlockSpec((length, wide), lambda i: (0, 0)),
            pl.BlockSpec((HEAD, length), lambda i: (0, 0)),
            pl.BlockSpec((length, HEAD), lambda i: (0, 0)),
            pl.BlockSpec((1, heads * HEAD, rows), lambda i: (i, 0, 0)),
            pl.BlockSpec((1, heads * HEAD, rows), lambda i: (i, 0, 0)),
            pl.BlockSpec((1, 1, heads * rows), lambda i: (i, 0, 0)),
        ],
        out_specs=(by_rows, pl.BlockSpec((length, 2 * HEAD), lambda i: (0, 0))),
        scratch_shapes=[
            pltpu.VMEM((HEAD, heads * rows), f32),
            pltpu.VMEM((length, wide), f32),
            pltpu.VMEM((length, HEAD), f32),
        ],
        compiler_params=pltpu.CompilerParams(vmem_limit_bytes=40 * 2**20),
        cost_estimate=lasting(7.5),
    )(query, key, key_t, value, d_out, out, logs)


def slot_kernel(sources, unread, place_in_ref, *refs):
    row_refs, cot_refs = refs[:sources], refs[sources : 2 * sources]
    router_ref, w_ref = refs[2 * sources : 2 * sources + 2]
    refs = refs[2 * sources + 2 + unread :]
    x_ref, hid_ref, ds_ref, dgu_ref, moe_ref = refs[:5]
    dsum_refs = refs[5 : 5 + sources]
    moe_acc, dsum_acc, combine_ref, place_ref = refs[5 + sources :]
    expert = pl.program_id(0)
    tokens, width = row_refs[0].shape
    cap = x_ref.shape[1] // sources
    named = place_in_ref[0] + expert

    @pl.when(expert == 0)
    def _():
        moe_acc[...] = jnp.zeros_like(moe_acc)
        dsum_acc[...] = jnp.zeros_like(dsum_acc)
        for s in range(sources):
            place = cot_refs[s][:, width:].astype(f32).T[:EXPERTS]
            place_ref[s] = place
            hit = place >= 0.0
            logits = mm(router_ref[...], row_refs[s][...], NT)
            top = jnp.max(jnp.where(hit, logits, -3e38), axis=0, keepdims=True)
            grown = jnp.where(hit, jnp.exp(jnp.minimum(logits - top, 0.0)), 0.0)
            combine_ref[s] = grown / jnp.sum(grown, axis=0, keepdims=True)

    slots = lax.broadcasted_iota(jnp.int32, (cap, tokens), 0).astype(f32)
    picks, cots, slot_weights = [], [], []
    for s in range(sources):
        hit = place_ref[s, pl.ds(named, 1), :] == slots
        pick = jnp.where(hit, 1.0, 0.0).astype(bf16)
        picks.append(pick)
        x_ref[0, s * cap : (s + 1) * cap, :] = mm(pick, row_refs[s][...], NN).astype(bf16)
        cots.append(mm(pick, cot_refs[s][:, :width], NN))
        slot_weights.append(
            jnp.sum(
                jnp.where(hit, combine_ref[s, pl.ds(named, 1), :], 0.0), axis=1, keepdims=True
            )
        )
    x_rows = x_ref[0]
    cot = jnp.concatenate(cots, axis=0)
    slot_weight = jnp.concatenate(slot_weights, axis=0)
    gate_up_w = w_ref[0, :, : 2 * FFE]
    down_t = w_ref[0, :, 2 * FFE :]
    gate_up = mm(x_rows, gate_up_w, NN)
    gate = gate_up[:, :FFE]
    up = gate_up[:, FFE:]
    sig = 1.0 / (1.0 + jnp.exp(-gate))
    silu = gate * sig
    hidden = (silu * up).astype(bf16)
    hid_ref[0] = hidden
    expert_out = mm(hidden, down_t, NT).astype(bf16).astype(f32)
    d_slot = (slot_weight * cot).astype(bf16)
    ds_ref[0] = d_slot
    d_comb = jnp.sum(cot * expert_out, axis=1, keepdims=True)
    d_comb_high = d_comb.astype(bf16).astype(f32)
    lane = lax.broadcasted_iota(jnp.int32, (d_comb.shape[0], EXTRA), 1)
    extra = jnp.where(lane == named, d_comb_high, 0.0)
    extra = jnp.where(lane == named + EXPERTS, d_comb - d_comb_high, extra).astype(bf16)
    weighted = (slot_weight * expert_out).astype(bf16)
    d_hidden = mm(d_slot, down_t, NN)
    d_gate = (d_hidden * up * sig * (1.0 + gate * (1.0 - sig))).astype(bf16)
    d_up = (d_hidden * silu).astype(bf16)
    dgu_ref[0, :, :FFE] = d_gate
    dgu_ref[0, :, FFE:] = d_up
    d_row = mm(dgu_ref[0], gate_up_w, NT).astype(bf16)
    for s in range(sources):
        part = slice(s * cap, (s + 1) * cap)
        moe_acc[s] += mm(picks[s], weighted[part], TN)
        dsum_acc[s, :, :width] += mm(picks[s], d_row[part], TN)
        dsum_acc[s, :, width:] += mm(picks[s], extra[part], TN)

    @pl.when(expert == pl.num_programs(0) - 1)
    def _():
        for s in range(sources):
            moe_ref[0, place_in_ref[2] ^ s] = moe_acc[s].astype(bf16)
            dsum_refs[s][...] = dsum_acc[s].astype(bf16)


def expert_slot(place, rows, cots, router_t, weights, cap, slots, moe, needed):
    sources = len(rows)
    tokens, width = rows[0].shape
    experts = weights.shape[0]
    held = sources * cap
    carried = ([] if moe is None else [moe]) + needed
    each = lambda *shape: pl.BlockSpec((1,) + shape, lambda e, s: (e,) + (0,) * len(shape))
    fixed = lambda *shape: pl.BlockSpec(shape, lambda e, s: (0,) * len(shape))
    got = pl.pallas_call(
        functools.partial(slot_kernel, sources, len(carried)),
        out_shape=(
            jax.ShapeDtypeStruct((experts, held, width), bf16),
            jax.ShapeDtypeStruct((experts, held, FFE), bf16),
            jax.ShapeDtypeStruct((experts, held, width), bf16),
            jax.ShapeDtypeStruct((experts, held, 2 * FFE), bf16),
        )
        + (jax.ShapeDtypeStruct((slots, sources, tokens, width), bf16),)
        + (jax.ShapeDtypeStruct((tokens, width + EXTRA), bf16),) * sources,
        grid_spec=pltpu.PrefetchScalarGridSpec(
            num_scalar_prefetch=1,
            grid=(experts,),
            in_specs=[fixed(tokens, width)] * sources
            + [fixed(tokens, width + EXTRA)] * sources
            + [fixed(EXPERTS, width), each(width, 3 * FFE)]
            + [pl.BlockSpec(memory_space=pl.ANY)] * len(carried),
            out_specs=(each(held, width), each(held, FFE), each(held, width), each(held, 2 * FFE))
            + (pl.BlockSpec((1, sources, tokens, width), lambda e, s: (s[1], 0, 0, 0)),)
            + (fixed(tokens, width + EXTRA),) * sources,
            scratch_shapes=[
                pltpu.VMEM((sources, tokens, width), f32),
                pltpu.VMEM((sources, tokens, width + EXTRA), f32),
                pltpu.VMEM((sources, EXPERTS, tokens), f32),
                pltpu.VMEM((sources, EXPERTS, tokens), f32),
            ],
        ),
        compiler_params=pltpu.CompilerParams(vmem_limit_bytes=56 * 2**20),
        cost_estimate=lasting(7.5),
        input_output_aliases={2 * sources + 3: 4} if moe is not None else {},
    )(place, *rows, *cots, router_t, weights, *carried)
    return got[:4], got[4], got[5:]


def middle_kernel(
    tp_ref, got_ref, in_ref, out_ref, gain_ref, router_ref, rank_ref,
    x_ref, act_ref, mine_ref, theirs_ref, combine_ref, probs_ref, total_ref,
):
    tp = tp_ref[0]
    count = got_ref.shape[0] // 2
    gathered = lambda t: jnp.concatenate([got_ref[2 * c + t] for c in range(count)], axis=0)
    mine = gathered(tp).astype(f32).T.astype(bf16)
    theirs = gathered(tp ^ 1).astype(f32).T.astype(bf16)
    mine_ref[...] = mine
    theirs_ref[...] = theirs
    x_one = in_ref[...].astype(f32) + (mm(mine, out_ref[tp], NT) + mm(theirs, out_ref[tp ^ 1], NT))
    x_ref[...] = x_one
    inv = lax.rsqrt(jnp.mean(x_one * x_one, axis=-1, keepdims=True) + norm_eps)
    act = (x_one * inv * gain_ref[...]).astype(bf16)
    act_ref[...] = act
    logits = mm(router_ref[...], act, NT)
    grown = jnp.exp(logits - jnp.max(logits, axis=0, keepdims=True))
    probs = grown / jnp.sum(grown, axis=0, keepdims=True)
    probs_ref[...] = probs
    total_ref[...] = jnp.sum(probs, axis=1, keepdims=True)
    hit = rank_ref[...].astype(f32) >= 0.0
    top = jnp.max(jnp.where(hit, logits, -3e38), axis=0, keepdims=True)
    grown = jnp.where(hit, jnp.exp(jnp.minimum(logits - top, 0.0)), 0.0)
    combine_ref[...] = grown / jnp.sum(grown, axis=0, keepdims=True)


def middle(tp, got, inputs, out_t, gain, router_t, rank):
    rows, width = inputs.shape
    held = got.shape[0] // 2 * got.shape[1]
    shapes = [
        ((rows, width), f32),
        ((rows, width), bf16),
        ((rows, held), bf16),
        ((rows, held), bf16),
        ((EXPERTS, rows), f32),
        ((EXPERTS, rows), f32),
        ((EXPERTS, 1), f32),
    ]
    return pl.pallas_call(
        middle_kernel,
        out_shape=tuple(jax.ShapeDtypeStruct(s, d) for s, d in shapes),
        in_specs=[pl.BlockSpec(memory_space=pltpu.SMEM)]
        + [pl.BlockSpec(memory_space=pltpu.VMEM)] * 6,
        out_specs=(pl.BlockSpec(memory_space=pltpu.VMEM),) * 7,
        compiler_params=pltpu.CompilerParams(vmem_limit_bytes=40 * 2**20),
        cost_estimate=lasting(4),
    )(tp, got, inputs, out_t, gain, router_t, rank)


def return_kernel(slots, tp_ref, *refs):
    part_refs = refs[:slots]
    (
        x_ref, act_ref, combine_ref, probs_ref, aux_ref, cot_ref, gain_ref, router_ref, out_ref,
        low_ref, rest_ref, small_ref, att_ref,
    ) = refs[slots:]
    tp = tp_ref[0]
    width = x_ref.shape[1]
    total = part_refs[0][...].astype(f32)
    for part in part_refs[1:]:
        total = total + part[...].astype(f32)
    extra = total[:, width:].T
    d_combine = extra[:EXPERTS] + extra[EXPERTS : 2 * EXPERTS]
    combine = combine_ref[...]
    probs = probs_ref[...]
    aux = aux_ref[...]
    d_logits = combine * (d_combine - jnp.sum(combine * d_combine, axis=0, keepdims=True))
    d_logits = d_logits + probs * (aux - jnp.sum(probs * aux, axis=0, keepdims=True))
    d_logits = d_logits.astype(bf16)
    d_act = total[:, :width] + mm(d_logits, router_ref[...], TN)
    x_one = x_ref[...]
    inv = lax.rsqrt(jnp.mean(x_one * x_one, axis=-1, keepdims=True) + norm_eps)
    normed = x_one * inv
    scaled = d_act * gain_ref[...]
    d_x = inv * (scaled - normed * jnp.mean(scaled * normed, axis=-1, keepdims=True))
    d_x = d_x + cot_ref[...].astype(f32)
    low = d_x.astype(bf16)
    low_ref[...] = low
    rest_ref[...] = (d_x - low.astype(f32)).astype(bf16)
    mine = mm(low, out_ref[tp], NN).T.astype(bf16)
    theirs = mm(low, out_ref[tp ^ 1], NN).T.astype(bf16)
    cut = att_ref.shape[1]
    for c in range(att_ref.shape[0] // 2):
        att_ref[2 * c + tp] = mine[c * cut : (c + 1) * cut]
        att_ref[2 * c + (tp ^ 1)] = theirs[c * cut : (c + 1) * cut]
    d_router = mm(d_logits, act_ref[...], NN)
    d_gain = jnp.sum(d_act * normed, axis=0, keepdims=True)
    small = jnp.concatenate([d_router, d_gain, jnp.zeros((HEAD - EXPERTS - 1, width), f32)], axis=0)
    small = small.T
    high = small.astype(bf16).astype(f32)
    small_ref[...] = jnp.concatenate([high, small - high], axis=1).astype(bf16)


def expert_return(tp, parts, x_one, act, combine, probs, aux, cot, gain, router_t, out_t, cuts):
    rows, width = x_one.shape
    slots = len(parts)
    shapes = [
        ((rows, width), bf16),
        ((rows, width), bf16),
        ((width, 2 * HEAD), bf16),
        ((cuts, width // cuts, rows), bf16),
    ]
    return pl.pallas_call(
        functools.partial(return_kernel, slots),
        out_shape=tuple(jax.ShapeDtypeStruct(s, d) for s, d in shapes),
        in_specs=[pl.BlockSpec(memory_space=pltpu.SMEM)]
        + [pl.BlockSpec(memory_space=pltpu.VMEM)] * (slots + 9),
        out_specs=(pl.BlockSpec(memory_space=pltpu.VMEM),) * 4,
        compiler_params=pltpu.CompilerParams(vmem_limit_bytes=48 * 2**20),
        cost_estimate=lasting(7),
    )(tp, *parts, x_one, act, combine, probs, aux, cot, gain, router_t, out_t)


def out_grad_kernel(low_ref, other_low_ref, att_ref, other_att_ref, small_ref, other_small_ref, out_ref):
    held = att_ref.shape[1]
    grad = mm(low_ref[...], att_ref[...], TN) + mm(other_low_ref[...], other_att_ref[...], TN)
    out_ref[:, :held] = grad.astype(bf16)
    small = small_ref[...].astype(f32) + other_small_ref[...].astype(f32)
    small = small[:, :HEAD] + small[:, HEAD:]
    high = small.astype(bf16).astype(f32)
    out_ref[:, held:] = jnp.concatenate([high, small - high], axis=1).astype(bf16)


def out_grad(low, other_low, att, other_att, small, other_small):
    rows, width = low.shape
    held = att.shape[1]
    return pl.pallas_call(
        out_grad_kernel,
        out_shape=jax.ShapeDtypeStruct((width, held + small.shape[1]), bf16),
        in_specs=[pl.BlockSpec(memory_space=pltpu.VMEM)] * 6,
        out_specs=pl.BlockSpec(memory_space=pltpu.VMEM),
        compiler_params=pltpu.CompilerParams(vmem_limit_bytes=40 * 2**20),
        cost_estimate=lasting(3),
    )(low, other_low, att, other_att, small, other_small)


def grads_kernel(parts, *refs):
    join = lambda n: jnp.concatenate([r[0] for r in refs[n * parts : (n + 1) * parts]], axis=0)
    out_ref = refs[-1]
    out_ref[0, :, : 2 * FFE] = mm(join(0), join(1), TN).astype(bf16)
    out_ref[0, :, 2 * FFE :] = mm(join(2), join(3), TN).astype(bf16)


def expert_grads(xs, dgus, dss, hids):
    parts = len(xs)
    experts, _, width = xs[0].shape
    spec = lambda a: pl.BlockSpec((1,) + a.shape[1:], lambda e: (e, 0, 0))
    many = [*xs, *dgus, *dss, *hids]
    return pl.pallas_call(
        functools.partial(grads_kernel, parts),
        out_shape=jax.ShapeDtypeStruct((experts, width, 3 * FFE), bf16),
        grid=(experts,),
        in_specs=[spec(a) for a in many],
        out_specs=pl.BlockSpec((1, width, 3 * FFE), lambda e: (e, 0, 0)),
        compiler_params=pltpu.CompilerParams(vmem_limit_bytes=56 * 2**20),
        cost_estimate=lasting(6.6),
    )(*many)


def split_kernel(grad_ref, gu_ref, down_ref, sums_ref):
    wide = gu_ref.shape[2]
    grad = grad_ref[0].astype(f32)
    gate_up = grad[:, :wide]
    down_t = grad[:, wide:]
    gu_ref[0] = gate_up
    down = down_t.T
    down_ref[0] = down
    squares = gate_up * gate_up
    lanes = sum(squares[:, i : i + 128] for i in range(0, wide, 128))
    rows = squares.shape[0]
    sums_ref[0, :, :rows] = jnp.sum(lanes.T, axis=0, keepdims=True)
    sums_ref[0, :, rows : 2 * rows] = jnp.sum(down * down, axis=0, keepdims=True)
    sums_ref[0, :, 2 * rows : 2 * rows + wide] = jnp.sum(squares, axis=0, keepdims=True)
    sums_ref[0, :, 2 * rows + wide :] = jnp.sum(down_t * down_t, axis=0, keepdims=True)


def split(grads):
    experts, rows, wide = grads.shape
    each = lambda *shape: pl.BlockSpec((1,) + shape, lambda e: (e, 0, 0))
    return pl.pallas_call(
        split_kernel,
        out_shape=(
            jax.ShapeDtypeStruct((experts, rows, 2 * FFE), f32),
            jax.ShapeDtypeStruct((experts, FFE, rows), f32),
            jax.ShapeDtypeStruct((experts, 1, 2 * rows + 3 * FFE), f32),
        ),
        grid=(experts,),
        in_specs=[each(rows, wide)],
        out_specs=(each(rows, 2 * FFE), each(FFE, rows), each(1, 2 * rows + 3 * FFE)),
        compiler_params=pltpu.CompilerParams(vmem_limit_bytes=40 * 2**20),
        cost_estimate=lasting(4),
    )(grads)


def half_sum(parts, count):
    total = parts[0].astype(f32)
    for y in range(1, count):
        total = total + partner(parts[y], "tp", y, count).astype(f32)
    return total.astype(bf16)


def per_device(
    inputs,
    cotangent,
    routes,
    segment_ids,
    parents,
    w_qkv,
    w_out,
    w_router,
    w_gate_up,
    w_down,
    gain_attn,
    gain_moe,
    row_qkv,
    col_qkv,
    row_out,
    col_out,
    row_router,
    col_router,
    row_gate_up,
    col_gate_up,
    row_down,
    col_down,
    second_attn,
    second_moe,
):
    tp_count = lax.axis_size("tp")
    ctx_count = lax.axis_size("ctx")
    fsdp_count = lax.axis_size("fsdp")
    count = tp_count * ctx_count * fsdp_count
    tp_index = lax.axis_index("tp")
    ctx_index = lax.axis_index("ctx")
    fsdp_index = lax.axis_index("fsdp")
    flat_index = fsdp_index * ctx_count + ctx_index
    owner_index = fsdp_index * tp_count + tp_index
    keep_once = (tp_index == 0).astype(f32)
    tok_rows = inputs.shape[0]
    half_rows = tok_rows // tp_count
    tree_len = segment_ids.shape[1]
    tokens_all = tok_rows * fsdp_count * ctx_count
    capacity = half_rows * TOPK * 3 // (2 * EXPERTS)
    local_experts = EXPERTS // (fsdp_count * tp_count)
    q_own = HEADS // (tp_count * ctx_count)
    kv_own = KV_HEADS // (tp_count * ctx_count)
    assert kv_own == 1 and tp_count == 2
    q_cols = q_own * HEAD
    kv_cols = kv_own * HEAD
    own_cols = q_cols + 2 * kv_cols
    dense_rows = w_qkv.shape[0]
    qkv_cols = w_qkv.shape[1]
    dense_parts = fsdp_count * ctx_count
    ctx_rows = w_gate_up.shape[1]
    labels = jnp.arange(EXPERTS, dtype=jnp.int32)

    def by_ctx(columns):
        q_end = ctx_count * q_cols
        k_end = q_end + ctx_count * kv_cols
        lead = columns.shape[:-1]
        return jnp.concatenate(
            [
                columns[..., :q_end].reshape(lead + (ctx_count, q_cols)),
                columns[..., q_end:k_end].reshape(lead + (ctx_count, kv_cols)),
                columns[..., k_end:].reshape(lead + (ctx_count, kv_cols)),
            ],
            axis=-1,
        )

    def from_ctx(columns):
        lead = columns.shape[:-2]
        return jnp.concatenate(
            [
                columns[..., :q_cols].reshape(lead + (-1,)),
                columns[..., q_cols : q_cols + kv_cols].reshape(lead + (-1,)),
                columns[..., q_cols + kv_cols :].reshape(lead + (-1,)),
            ],
            axis=-1,
        )

    w_qkv_low = w_qkv.astype(bf16)
    extras = jnp.concatenate(
        [gain_attn.astype(bf16)[:, None], gain_moe.astype(bf16)[:, None], w_router.astype(bf16)],
        axis=1,
    )
    w_send = jnp.concatenate(
        [
            jnp.moveaxis(by_ctx(w_qkv_low), 1, 0),
            jnp.broadcast_to(extras[None], (ctx_count,) + extras.shape),
        ],
        axis=-1,
    )
    w_send = jnp.broadcast_to(w_send[None], (fsdp_count,) + w_send.shape)
    w_got = exchange(w_send.reshape((dense_parts,) + w_send.shape[2:]), ("fsdp", "ctx"))
    w_got = w_got.reshape(D, own_cols + 2 + EXPERTS)
    def spread(block):
        bit = fsdp_count // 2
        blocks = {0: block}
        while bit:
            for j in list(blocks):
                blocks[j ^ bit] = partner(blocks[j], "fsdp", bit, fsdp_count)
            bit //= 2
        near = [blocks[j] for j in range(fsdp_count)]
        return [[b] + [partner(b, "tp", y, tp_count) for y in range(1, tp_count)] for b in near]

    my_routes = lax.dynamic_slice_in_dim(routes, tp_index * half_rows, half_rows, 0)
    hit = jnp.sum((my_routes[..., None] == labels).astype(f32), axis=1)
    before = (
        jnp.arange(half_rows, dtype=jnp.int32)[:, None]
        < jnp.arange(half_rows, dtype=jnp.int32)[None, :]
    ).astype(bf16)
    rank = dot("te,tu->eu", hit.astype(bf16), before)
    rank = jnp.where(hit.T > 0.5, rank, -1.0).astype(bf16)
    riders = jnp.concatenate(
        [rank.T, jnp.broadcast_to(jnp.sum(hit, axis=0).astype(bf16), (half_rows, EXPERTS))], axis=1
    )
    riders = jnp.pad(riders, ((0, 0), (0, EXTRA - 2 * EXPERTS)))
    cot_rows = jnp.concatenate([cotangent, riders], axis=1)
    cot_near = [cot_rows]
    for j in range(1, fsdp_count):
        if fsdp_count == 4 and j == 3:
            cot_near.append(cot_rows)
        else:
            cot_near.append(partner(cot_rows, "fsdp", j, fsdp_count))

    blocks = {0: inputs}
    bit = ctx_count // 2
    while bit:
        for j in list(blocks):
            blocks[j ^ bit] = partner(blocks[j], "ctx", bit, ctx_count)
        if bit == ctx_count // 2:
            arrived = blocks[bit] = after(blocks[bit], w_got)
        bit //= 2
    blocks = [blocks[j] for j in range(ctx_count)]
    gain_one = w_got[:, own_cols].astype(f32)[None]
    gain_two = w_got[:, own_cols + 1].astype(f32)[None]
    router_t = w_got[:, own_cols + 2 :].T
    tp_at = jnp.asarray(tp_index, jnp.int32).reshape(1)

    master_sums = jnp.stack(
        [
            jnp.sum(w_qkv * w_qkv),
            jnp.sum(w_out * w_out),
            keep_once * jnp.sum(w_router * w_router),
            jnp.sum(w_gate_up * w_gate_up),
            jnp.sum(w_down * w_down),
            keep_once * jnp.sum(gain_attn * gain_attn),
            keep_once * jnp.sum(gain_moe * gain_moe),
        ]
    )
    out_rows = w_out.shape[0]
    out_t = lax.all_gather(w_out.astype(bf16).T, ("tp", "fsdp", "ctx"), axis=0, tiled=True)
    out_t = out_t.reshape(tp_count, D, out_rows)
    expert_w = jnp.concatenate(
        [w_gate_up.astype(bf16), w_down.astype(bf16).transpose(0, 2, 1)], axis=2
    )
    expert_w = lax.all_gather(after(expert_w, arrived), "ctx", axis=1, tiled=True)

    seg_hot = (segment_ids[0][:, None] == jnp.arange(HEAD, dtype=jnp.int32)).astype(bf16)
    hidden_from = jnp.pad((1.0 - ancestry(parents[0])) * -1e30, ((0, HEAD - NSEG),) * 2)
    barred = dot("qs,su->qu", seg_hot, hidden_from.astype(bf16)).astype(bf16)
    query_tie = cot_near[1:3]
    act1, query, key, key_t, value, value_t = project(
        blocks,
        jnp.asarray(ctx_index, jnp.int32).reshape(1),
        w_got,
        gain_one,
        barred,
        seg_hot,
        q_own,
        half_rows,
    )
    after_project = [after(c, key) for c in cot_near]
    if fsdp_count == 4:
        after_project[3] = partner(after_project[2], "fsdp", 1, fsdp_count)
    cot_far = [partner(c, "tp", 1, tp_count) for c in after_project]
    grad_slots = [[c, f] for c, f in zip(after_project, cot_far)]
    attended_own, logs = attention_forward(after(query, *query_tie), key, value_t, half_rows)
    counts = sum(
        c[:1, D + EXPERTS : D + 2 * EXPERTS].astype(f32) for pair in grad_slots for c in pair
    )
    bit = 1
    while bit < ctx_count:
        counts = counts + partner(counts, "ctx", bit, ctx_count)
        bit *= 2
    fraction = counts[0] / (tokens_all * TOPK)
    attended_own = after(attended_own, *cot_far[:2], after_project[3])
    attended = exchange(attended_own, ("ctx", "tp"))
    attended = after(attended, *cot_far[2:])
    inputs_half = lax.dynamic_slice_in_dim(inputs, tp_index * half_rows, half_rows, 0)
    x_one, act2, heads_own, heads_other, combine, router_probs, prob_sums = middle(
        tp_at, attended, inputs_half, out_t, gain_two, router_t, rank
    )
    w_tree = lax.all_gather(after(w_got, act2)[:, :own_cols], "ctx", axis=0, tiled=False)
    row_slots = spread(after(act2, *[pair[1] for pair in grad_slots]))

    kept, d_sums, moe_sums = [], [], None
    for j in range(fsdp_count):
        rows = list(row_slots[j])
        if j == 0:
            rows[0] = after(rows[0], row_slots[1][0])
        if j == 1:
            rows[0] = after(rows[0], row_slots[2][0])
        if j >= 2:
            rows[0] = after(rows[0], d_sums[j - 2], *(pair[0] for pair in row_slots[3:]))
        if j == 3:
            rows[0] = after(rows[0], fraction)
        place = jnp.stack([owner_index * local_experts, fsdp_index ^ j, tp_index])
        held, moe_sums, d_out = expert_slot(
            place.astype(jnp.int32),
            rows,
            grad_slots[j],
            router_t,
            expert_w,
            capacity,
            fsdp_count,
            moe_sums,
            [w_tree] if j == fsdp_count - 1 else [],
        )
        kept.append(held)
        d_sums.append(half_sum(d_out, tp_count))
    d_parts = [d_sums[0]] + [partner(d_sums[j], "fsdp", j, fsdp_count) for j in range(1, fsdp_count)]
    other_heads = partner(after(heads_other, d_sums[-1]), "tp", 1, tp_count)
    d_parts[0] = after(d_parts[0], other_heads)
    xs, hids, dss, dgus = (list(part) for part in zip(*kept))
    xs[0] = after(xs[0], *d_sums[-2:])
    g_experts = expert_grads(xs, dgus, dss, hids)
    d_parts[0] = after(d_parts[0], g_experts)
    low, rest, small, d_attended = expert_return(
        tp_at,
        d_parts,
        x_one,
        act2,
        combine,
        router_probs,
        (aux_weight * EXPERTS * fraction)[:, None],
        cotangent,
        gain_two,
        router_t,
        out_t,
        ctx_count * tp_count,
    )
    d_attended = exchange(d_attended, ("ctx", "tp"))
    g_experts = lax.psum_scatter(after(g_experts, low), "ctx", scatter_dimension=1, tiled=True)
    g_gate_up, g_down, expert_sums = split(g_experts)
    expert_sums = expert_sums[:, 0]
    other_low = partner(low, "tp", 1, tp_count)
    other_small = partner(small, "tp", 1, tp_count)
    g_out_part = out_grad(low, other_low, heads_own, other_heads, small, other_small)
    d_attended = after(d_attended, g_out_part)
    g_out_got = exchange(g_out_part.reshape(dense_parts, dense_rows, -1), ("fsdp", "ctx"))
    g_out_got = jnp.sum(g_out_got.astype(f32), axis=0)
    g_out = g_out_got[:, :out_rows].T
    g_small = g_out_got[:, out_rows : out_rows + HEAD] + g_out_got[:, out_rows + HEAD :]
    g_router = g_small[:, :EXPERTS]
    g_gain2 = g_small[:, EXPERTS]

    d_q, d_kv = attention_backward(query, key, key_t, value, d_attended, attended_own, logs)
    moe_sums = after(moe_sums, d_q)
    moe = lax.psum_scatter(
        moe_sums.reshape(-1, D), ("fsdp", "tp"), scatter_dimension=0, tiled=True
    )
    d_qkv = jnp.concatenate([d_q, d_kv], axis=1)
    g_qkv_part = after(dot("td,tc->dc", act1, d_qkv).astype(bf16), g_out_got)
    g_qkv_got = exchange(g_qkv_part.reshape(dense_parts, dense_rows, own_cols), ("fsdp", "ctx"))
    g_qkv_got = g_qkv_got.reshape(fsdp_count, ctx_count, dense_rows, own_cols).astype(f32)
    g_qkv = from_ctx(jnp.moveaxis(jnp.sum(g_qkv_got, axis=0), 0, 1))
    sq_qkv = g_qkv * g_qkv
    sq_out = g_out * g_out
    sq_router = g_router * g_router
    gain_part = jnp.sum(g_qkv * w_qkv_low.astype(f32), axis=1) / gain_attn.astype(bf16).astype(f32)
    d_qkv_send = after(d_qkv, g_qkv_got)
    d_qkv_all = exchange(d_qkv_send.reshape(ctx_count, tok_rows, own_cols), "ctx")
    d_act1_low = dot("crk,cdk->rd", d_qkv_all, w_tree).astype(bf16)
    d_act1_other = partner(d_act1_low, "tp", 1, tp_count)
    pieces = [
        jnp.sum(sq_qkv, axis=0),
        jnp.sum(sq_out, axis=1),
        jnp.sum(sq_qkv, axis=1),
        gain_part,
        jnp.sum(sq_out, axis=0),
        jnp.sum(sq_router, axis=1),
        jnp.concatenate([jnp.sum(sq_router, axis=0), prob_sums[:, 0], master_sums]),
    ]
    sizes = [p.shape[0] for p in pieces]
    padded = [-(-s // 128) * 128 for s in sizes]
    message = jnp.concatenate([jnp.pad(p, (0, n - p.shape[0])) for p, n in zip(pieces, padded)])
    message = after(message, d_qkv_all)
    got = share(message, count).reshape(dense_parts, tp_count, -1)
    shares, at = [], 0
    for size, room in zip(sizes, padded):
        shares.append(got[..., at : at + size])
        at += room
    tot_col_qkv = jnp.sum(shares[0], axis=0).reshape(-1)
    tot_row_out = jnp.sum(shares[1], axis=0).reshape(-1)
    tot_row_qkv = jnp.sum(shares[2], axis=1).reshape(-1)
    g_gain1 = lax.dynamic_index_in_dim(jnp.sum(shares[3], axis=1), flat_index, 0, keepdims=False)
    tot_col_out = jnp.sum(shares[4], axis=1).reshape(-1)
    tot_row_router = shares[5][:, 0].reshape(-1)
    tot_col_router = jnp.sum(shares[6][:, 0, :EXPERTS], axis=0)
    last_totals = jnp.sum(shares[6][..., EXPERTS:], axis=(0, 1))
    prob_totals = last_totals[:EXPERTS]
    master_totals = last_totals[EXPERTS:]

    own_row_gu = expert_sums[:, :ctx_rows]
    start = (owner_index * local_experts, ctx_index * ctx_rows)
    start = tuple(jnp.asarray(s, jnp.int32) for s in start)
    rows_gu = lax.dynamic_slice(row_gate_up, start, (local_experts, ctx_rows))
    rows_gu = decay * rows_gu + (1.0 - decay) * (own_row_gu / (2 * FFE) + floor_sq)
    gu_sum = jnp.pad(jnp.sum(rows_gu, axis=1, keepdims=True), ((0, 0), (0, 127)))
    over_ctx = jnp.concatenate([expert_sums[:, 2 * ctx_rows :], gu_sum], axis=1)
    over_ctx = jnp.broadcast_to(over_ctx[None], (ctx_count,) + over_ctx.shape)
    over_ctx = jnp.sum(exchange(after(over_ctx, got), "ctx"), axis=0)
    mean_gu = over_ctx[:, 3 * FFE] / D
    own_col_gu = over_ctx[:, : 2 * FFE]
    own_row_down = over_ctx[:, 2 * FFE : 3 * FFE]
    own_col_down = expert_sums[:, ctx_rows : 2 * ctx_rows]
    first_row = (start[0], jnp.asarray(0, jnp.int32))
    cols_gu = lax.dynamic_slice(col_gate_up, first_row, (local_experts, 2 * FFE))
    cols_gu = decay * cols_gu + (1.0 - decay) * (own_col_gu / D + floor_sq)
    rows_dn = lax.dynamic_slice(row_down, first_row, (local_experts, FFE))
    rows_dn = decay * rows_dn + (1.0 - decay) * (own_row_down / D + floor_sq)
    cols_dn = lax.dynamic_slice(col_down, start, (local_experts, ctx_rows))
    cols_dn = decay * cols_dn + (1.0 - decay) * (own_col_down / FFE + floor_sq)
    mean_dn = jnp.mean(rows_dn, axis=-1)
    change_gate_up = g_gate_up * lax.rsqrt(
        rows_gu[:, :, None] * cols_gu[:, None, :] / mean_gu[:, None, None]
    )
    change_down = g_down * lax.rsqrt(
        rows_dn[:, :, None] * cols_dn[:, None, :] / mean_dn[:, None, None]
    )
    squares_gu = jnp.sum(change_gate_up * change_gate_up)
    squares_dn = jnp.sum(change_down * change_down)
    d_act1 = d_act1_low.astype(f32) + after(d_act1_other, over_ctx).astype(f32)
    own_inputs = inputs.astype(f32)
    d_inputs_attn, _ = norm_backward(own_inputs, inv_rms(own_inputs), gain_one, d_act1)
    rest = after(rest, d_qkv)
    d_x1 = low.astype(f32) + rest.astype(f32)
    other_x1 = other_low.astype(f32) + partner(rest, "tp", 1, tp_count).astype(f32)
    d_x1 = in_order(d_x1, other_x1, tp_index, 0).reshape(tok_rows, D)
    grad_inputs = d_x1 + d_inputs_attn

    qkv_width = (HEADS + 2 * KV_HEADS) * HEAD
    row_qkv_new = decay * row_qkv + (1.0 - decay) * (tot_row_qkv / qkv_width + floor_sq)
    col_qkv_new = decay * col_qkv + (1.0 - decay) * (tot_col_qkv / D + floor_sq)
    row_out_new = decay * row_out + (1.0 - decay) * (tot_row_out / D + floor_sq)
    col_out_new = decay * col_out + (1.0 - decay) * (tot_col_out / (HEADS * HEAD) + floor_sq)
    row_router_new = decay * row_router + (1.0 - decay) * (tot_row_router / EXPERTS + floor_sq)
    col_router_new = decay * col_router + (1.0 - decay) * (tot_col_router / D + floor_sq)
    aux_loss = EXPERTS * jnp.sum(fraction * prob_totals / tokens_all)

    rows_here = lax.dynamic_slice_in_dim(row_qkv_new, flat_index * dense_rows, dense_rows, 0)
    cols_here = lax.dynamic_slice_in_dim(col_qkv_new, tp_index * qkv_cols, qkv_cols, 0)
    change_qkv = g_qkv * lax.rsqrt(rows_here[:, None] * cols_here[None, :] / jnp.mean(row_qkv_new))
    rows_here = lax.dynamic_slice_in_dim(row_out_new, tp_index * out_rows, out_rows, 0)
    cols_here = lax.dynamic_slice_in_dim(col_out_new, flat_index * dense_rows, dense_rows, 0)
    change_out = g_out * lax.rsqrt(rows_here[:, None] * cols_here[None, :] / jnp.mean(row_out_new))
    rows_here = lax.dynamic_slice_in_dim(row_router_new, flat_index * dense_rows, dense_rows, 0)
    change_router = g_router * lax.rsqrt(
        rows_here[:, None] * col_router_new[None, :] / jnp.mean(row_router_new)
    )
    second_attn_new = decay * second_attn + (1.0 - decay) * (g_gain1 * g_gain1 + floor_sq)
    second_moe_new = decay * second_moe + (1.0 - decay) * (g_gain2 * g_gain2 + floor_sq)
    change_gain1 = g_gain1 * lax.rsqrt(second_attn_new)
    change_gain2 = g_gain2 * lax.rsqrt(second_moe_new)
    square_sums = jnp.stack(
        [
            jnp.sum(change_qkv * change_qkv),
            jnp.sum(change_out * change_out),
            keep_once * jnp.sum(change_router * change_router),
            squares_gu,
            squares_dn,
            keep_once * jnp.sum(change_gain1 * change_gain1),
            keep_once * jnp.sum(change_gain2 * change_gain2),
        ]
    )
    square_totals = jnp.sum(share(square_sums, count), axis=0)
    quarter = lambda a: lax.dynamic_slice_in_dim(
        a, ctx_index * (a.shape[1] // ctx_count), a.shape[1] // ctx_count, 1
    )
    moments = jnp.concatenate([rows_gu, cols_dn, quarter(cols_gu), quarter(rows_dn)], axis=1)
    moments = share(after(moments, square_totals).reshape(-1), count)
    moments = moments.reshape(fsdp_count, ctx_count, tp_count, local_experts, -1)
    moments = moments.transpose(0, 2, 3, 1, 4).reshape(EXPERTS, ctx_count, -1)
    cut_at = (ctx_rows, 2 * ctx_rows, 2 * ctx_rows + 2 * FFE // ctx_count)
    row_gu_new = moments[..., : cut_at[0]].reshape(EXPERTS, D)
    col_down_new = moments[..., cut_at[0] : cut_at[1]].reshape(EXPERTS, D)
    col_gu_new = moments[..., cut_at[1] : cut_at[2]].reshape(EXPERTS, 2 * FFE)
    row_down_new = moments[..., cut_at[2] :].reshape(EXPERTS, FFE)

    entries = jnp.array(
        [
            D * qkv_width,
            HEADS * HEAD * D,
            D * EXPERTS,
            EXPERTS * D * 2 * FFE,
            EXPERTS * FFE * D,
            D,
            D,
        ],
        f32,
    )
    update_rms = jnp.sqrt(square_totals / entries)
    weight_rms = jnp.sqrt(master_totals / entries)
    step_scale = rate * weight_rms / jnp.maximum(clip_rms, update_rms)
    new_qkv = w_qkv - step_scale[0] * change_qkv
    new_out = w_out - step_scale[1] * change_out
    new_router = w_router - step_scale[2] * change_router
    new_gate_up = w_gate_up - step_scale[3] * change_gate_up
    new_down = w_down - step_scale[4] * change_down
    new_gain1 = gain_attn - step_scale[5] * change_gain1
    new_gain2 = gain_moe - step_scale[6] * change_gain2
    layer_out = (x_one + after(moe, update_rms, new_gate_up, grad_inputs).astype(f32)).astype(bf16)
    return (
        layer_out,
        grad_inputs,
        aux_loss,
        g_qkv,
        g_out,
        g_router,
        g_gate_up,
        g_down,
        g_gain1,
        g_gain2,
        new_qkv,
        new_out,
        new_router,
        new_gate_up,
        new_down,
        new_gain1,
        new_gain2,
        new_qkv.astype(bf16),
        new_out.astype(bf16),
        new_router.astype(bf16),
        new_gate_up.astype(bf16),
        new_down.astype(bf16),
        new_gain1.astype(bf16),
        new_gain2.astype(bf16),
        row_qkv_new,
        col_qkv_new,
        row_out_new,
        col_out_new,
        row_router_new,
        col_router_new,
        row_gu_new,
        col_gu_new,
        row_down_new,
        col_down_new,
        second_attn_new,
        second_moe_new,
        update_rms,
    )


def solution(mesh):
    placed = (
        P(("fsdp", "ctx"), None),
        P(("fsdp", "ctx", "tp"), None),
        P(("fsdp", "ctx"), None),
        P("fsdp", None),
        P("fsdp", None),
        P(("fsdp", "ctx"), "tp"),
        P("tp", ("fsdp", "ctx")),
        P(("fsdp", "ctx"), None),
        P(("fsdp", "tp"), "ctx", None),
        P(("fsdp", "tp"), None, "ctx"),
        P(("fsdp", "ctx")),
        P(("fsdp", "ctx")),
        P(),
        P(),
        P(),
        P(),
        P(),
        P(),
        P(),
        P(),
        P(),
        P(),
        P(("fsdp", "ctx")),
        P(("fsdp", "ctx")),
    )
    return jax.shard_map(
        per_device,
        mesh=mesh,
        in_specs=placed,
        out_specs=(
            P(("fsdp", "ctx", "tp"), None),
            P(("fsdp", "ctx"), None),
            P(),
            P(("fsdp", "ctx"), "tp"),
            P("tp", ("fsdp", "ctx")),
            P(("fsdp", "ctx"), None),
            P(("fsdp", "tp"), "ctx", None),
            P(("fsdp", "tp"), None, "ctx"),
            P(("fsdp", "ctx")),
            P(("fsdp", "ctx")),
            P(("fsdp", "ctx"), "tp"),
            P("tp", ("fsdp", "ctx")),
            P(("fsdp", "ctx"), None),
            P(("fsdp", "tp"), "ctx", None),
            P(("fsdp", "tp"), None, "ctx"),
            P(("fsdp", "ctx")),
            P(("fsdp", "ctx")),
            P(("fsdp", "ctx"), "tp"),
            P("tp", ("fsdp", "ctx")),
            P(("fsdp", "ctx"), None),
            P(("fsdp", "tp"), "ctx", None),
            P(("fsdp", "tp"), None, "ctx"),
            P(("fsdp", "ctx")),
            P(("fsdp", "ctx")),
            P(),
            P(),
            P(),
            P(),
            P(),
            P(),
            P(),
            P(),
            P(),
            P(),
            P(("fsdp", "ctx")),
            P(("fsdp", "ctx")),
            P(),
        ),
        check_vma=False,
    )
```

```python
import functools

import jax
import jax.numpy as jnp
from jax import lax
from jax.experimental import pallas as pl
from jax.experimental.pallas import tpu as pltpu
from jax.sharding import PartitionSpec as P

D = 1536
HEADS = 24
KV_HEADS = 8
HEAD = 64
FFE = 512
TOPK = 8
EXPERTS = 32
NSEG = 13

norm_eps = 1e-05
decay = 0.5
floor_sq = 1e-30
rate = 0.25
clip_rms = 0.05
aux_weight = 1.0
bf16 = jnp.bfloat16
f32 = jnp.float32
EVERY = ("fsdp", "ctx", "tp")
EXTRA = 128

def lasting(microseconds):
    flops = int(microseconds * 1.15e9)
    return pl.CostEstimate(flops=flops, bytes_accessed=1, transcendentals=0)
NT = (((1,), (1,)), ((), ()))
NN = (((1,), (0,)), ((), ()))
TN = (((0,), (0,)), ((), ()))


def dot(spec, left, right):
    return jnp.einsum(spec, left, right, preferred_element_type=f32)


def exchange(values, axes):
    return lax.all_to_all(values, axes, split_axis=0, concat_axis=0, tiled=True)


def share(vector, count):
    return exchange(jnp.broadcast_to(vector[None], (count,) + vector.shape), EVERY)


def inv_rms(values):
    return lax.rsqrt(jnp.mean(values * values, axis=-1, keepdims=True) + norm_eps)


def norm_backward(values, inv, gain, d_out):
    normed = values * inv
    scaled = d_out * gain
    d_values = inv * (scaled - normed * jnp.mean(scaled * normed, axis=-1, keepdims=True))
    return d_values, normed


def ancestry(parent_row):
    seg_labels = jnp.arange(NSEG, dtype=jnp.int32)
    table = jnp.maximum(
        (seg_labels[:, None] == seg_labels[None, :]).astype(f32),
        (parent_row[:, None] == seg_labels[None, :]).astype(f32),
    )
    for sweep in range(NSEG.bit_length()):
        table = jnp.max(table[:, :, None] * table[None, :, :], axis=1)
    return table


def partner(values, axis, bits, count):
    return lax.ppermute(values, axis, [(i, i ^ bits) for i in range(count)])


def after(values, *others):
    return lax.optimization_barrier((values,) + others)[0]


def in_order(mine, other, bit, axis):
    first = jnp.where(bit == 0, mine, other)
    second = jnp.where(bit == 0, other, mine)
    return jnp.stack([first, second], axis=axis)


def mm(left, right, dims):
    return lax.dot_general(left, right, dims, preferred_element_type=f32)


def project_kernel(
    count, index_ref, *refs
):
    block_refs = refs[:count]
    w_ref, gain_ref, barred_ref, seg_ref = refs[count : count + 4]
    act_ref, q_ref, k_ref, kt_ref, v_ref, vt_ref = refs[count + 4 :]
    heads = q_ref.shape[0]
    place = pl.program_id(0) // (pl.num_programs(0) // count) ^ index_ref[0]
    block = block_refs[0][...]
    for j in range(1, count):
        block = jnp.where(place == j, block_refs[j][...], block)
    block = block.astype(f32)
    inv = lax.rsqrt(jnp.mean(block * block, axis=-1, keepdims=True) + norm_eps)
    act = (block * inv * gain_ref[...]).astype(bf16)
    act_ref[...] = act
    qkv = mm(act, w_ref[...], NN).astype(bf16).astype(f32)
    barred = barred_ref[...].astype(f32)
    for h in range(heads):
        query = qkv[:, h * HEAD : (h + 1) * HEAD] * HEAD ** (-0.5)
        q_ref[h] = jnp.concatenate([query, barred], axis=1).astype(bf16)
    key = qkv[:, heads * HEAD : (heads + 1) * HEAD]
    value = qkv[:, (heads + 1) * HEAD : (heads + 2) * HEAD]
    k_ref[...] = jnp.concatenate([key, seg_ref[...].astype(f32)], axis=1).astype(bf16)
    kt_ref[...] = key.T.astype(bf16)
    v_ref[...] = value.astype(bf16)
    vt_ref[...] = value.T.astype(bf16)


def project(blocks, index, weights, gain, barred, seg_hot, heads, rows):
    count = len(blocks)
    tok_rows, width = blocks[0].shape
    per = tok_rows // rows
    length = count * tok_rows
    wide = 2 * HEAD

    def place(j):
        def at(i, s):
            return (jnp.where((i // per ^ s[0]) == j, i % per, 0), 0)

        return at

    whole = lambda a: pl.BlockSpec(a.shape, lambda i, s: (0,) * a.ndim)
    by_rows = lambda columns: pl.BlockSpec((rows, columns), lambda i, s: (i, 0))
    return pl.pallas_call(
        functools.partial(project_kernel, count),
        out_shape=(
            jax.ShapeDtypeStruct((length, width), bf16),
            jax.ShapeDtypeStruct((heads, length, wide), bf16),
            jax.ShapeDtypeStruct((length, wide), bf16),
            jax.ShapeDtypeStruct((HEAD, length), bf16),
            jax.ShapeDtypeStruct((length, HEAD), bf16),
            jax.ShapeDtypeStruct((HEAD, length), bf16),
        ),
        grid_spec=pltpu.PrefetchScalarGridSpec(
            num_scalar_prefetch=1,
            grid=(length // rows,),
            in_specs=[pl.BlockSpec((rows, width), place(j)) for j in range(count)]
            + [whole(weights), whole(gain), by_rows(HEAD), by_rows(HEAD)],
            out_specs=(
                by_rows(width),
                pl.BlockSpec((heads, rows, wide), lambda i, s: (0, i, 0)),
                by_rows(wide),
                pl.BlockSpec((HEAD, rows), lambda i, s: (0, i)),
                by_rows(HEAD),
                pl.BlockSpec((HEAD, rows), lambda i, s: (0, i)),
            ),
        ),
        compiler_params=pltpu.CompilerParams(vmem_limit_bytes=40 * 2**20),
        cost_estimate=lasting(3.3),
    )(index, *blocks, weights, gain, barred, seg_hot)


def forward_kernel(q_ref, k_ref, vt_ref, out_ref, log_ref, acc_ref, top_ref, sum_ref):
    step = pl.program_id(0)
    heads, rows, wide = q_ref.shape
    query = q_ref[...].reshape(heads * rows, wide)
    acc_ref[...] = jnp.zeros_like(acc_ref)
    top_ref[...] = jnp.full(top_ref.shape, -3e38, f32)
    sum_ref[...] = jnp.zeros_like(sum_ref)

    def chunk(j, diagonal):
        at = pl.ds(pl.multiple_of(j * rows, rows), rows)
        scores = mm(k_ref[at, :], query, NT)
        if diagonal:
            key_at = lax.broadcasted_iota(jnp.int32, (rows, rows), 0)
            query_at = lax.broadcasted_iota(jnp.int32, (rows, rows), 1)
            later = jnp.where(key_at > query_at, -1e30, 0.0)
            scores = scores + jnp.concatenate([later] * heads, axis=1)
        top_old = top_ref[...]
        top = jnp.maximum(top_old, jnp.max(scores, axis=0, keepdims=True))
        probs = jnp.exp(scores - top)
        shrink = jnp.exp(top_old - top)
        sum_ref[...] = sum_ref[...] * shrink + jnp.sum(probs, axis=0, keepdims=True)
        acc_ref[...] = acc_ref[...] * shrink + mm(vt_ref[:, at], probs.astype(bf16), NN)
        top_ref[...] = top

    chunk(step, True)

    @pl.loop(0, step)
    def _(j):
        chunk(j, False)

    total = sum_ref[...]
    log_ref[...] = (top_ref[...] + jnp.log(total))[None]
    out = acc_ref[...] / total
    for h in range(heads):
        out_ref[0, h * HEAD : (h + 1) * HEAD, :] = out[:, h * rows : (h + 1) * rows].astype(bf16)


def attention_forward(query, key, value_t, rows):
    heads, length, wide = query.shape
    steps = length // rows
    return pl.pallas_call(
        forward_kernel,
        out_shape=(
            jax.ShapeDtypeStruct((steps, heads * HEAD, rows), bf16),
            jax.ShapeDtypeStruct((steps, 1, heads * rows), f32),
        ),
        grid=(steps,),
        in_specs=[
            pl.BlockSpec((heads, rows, wide), lambda i: (0, i, 0)),
            pl.BlockSpec((length, wide), lambda i: (0, 0)),
            pl.BlockSpec((HEAD, length), lambda i: (0, 0)),
        ],
        out_specs=(
            pl.BlockSpec((1, heads * HEAD, rows), lambda i: (i, 0, 0)),
            pl.BlockSpec((1, 1, heads * rows), lambda i: (i, 0, 0)),
        ),
        scratch_shapes=[
            pltpu.VMEM((HEAD, heads * rows), f32),
            pltpu.VMEM((1, heads * rows), f32),
            pltpu.VMEM((1, heads * rows), f32),
        ],
        compiler_params=pltpu.CompilerParams(vmem_limit_bytes=40 * 2**20),
        cost_estimate=lasting(7.5),
    )(query, key, value_t)


def backward_kernel(
    q_ref, k_ref, kt_ref, v_ref, do_ref, out_ref, log_ref, dq_ref, dkv_ref, acc_ref, dk_ref, dv_ref
):
    step = pl.program_id(0)
    heads, rows, wide = q_ref.shape
    query = q_ref[...].reshape(heads * rows, wide)
    side_by_side = lambda a: jnp.concatenate(
        [a[h * HEAD : (h + 1) * HEAD] for h in range(heads)], axis=1
    )
    d_out = side_by_side(do_ref[0])
    products = side_by_side(do_ref[0].astype(f32) * out_ref[0].astype(f32))
    delta = jnp.sum(products, axis=0, keepdims=True)
    logs = log_ref[0]

    @pl.when(step == 0)
    def _():
        dk_ref[...] = jnp.zeros_like(dk_ref)
        dv_ref[...] = jnp.zeros_like(dv_ref)

    acc_ref[...] = jnp.zeros_like(acc_ref)

    def chunk(j, diagonal):
        at = pl.ds(pl.multiple_of(j * rows, rows), rows)
        scores = mm(k_ref[at, :], query, NT)
        if diagonal:
            key_at = lax.broadcasted_iota(jnp.int32, (rows, rows), 0)
            query_at = lax.broadcasted_iota(jnp.int32, (rows, rows), 1)
            later = jnp.where(key_at > query_at, -1e30, 0.0)
            scores = scores + jnp.concatenate([later] * heads, axis=1)
        probs = jnp.exp(scores - logs)
        d_probs = mm(v_ref[at, :], d_out, NN)
        d_scores = (probs * (d_probs - delta)).astype(bf16)
        dv_ref[at, :] += mm(probs.astype(bf16), d_out, NT)
        dk_ref[at, :] += mm(d_scores, query, NN)
        acc_ref[...] += mm(kt_ref[:, at], d_scores, NN)

    chunk(step, True)

    @pl.loop(0, step)
    def _(j):
        chunk(j, False)

    out = acc_ref[...] * HEAD ** (-0.5)
    out = jnp.concatenate([out[:, h * rows : (h + 1) * rows] for h in range(heads)], axis=0)
    dq_ref[...] = out.T.astype(bf16)

    @pl.when(step == pl.num_programs(0) - 1)
    def _():
        dkv_ref[...] = jnp.concatenate([dk_ref[:, :HEAD], dv_ref[...]], axis=1).astype(bf16)


def attention_backward(query, key, key_t, value, d_out, out, logs):
    heads, length, wide = query.shape
    steps = logs.shape[0]
    rows = length // steps
    by_rows = pl.BlockSpec((rows, heads * HEAD), lambda i: (i, 0))
    return pl.pallas_call(
        backward_kernel,
        out_shape=(
            jax.ShapeDtypeStruct((length, heads * HEAD), bf16),
            jax.ShapeDtypeStruct((length, 2 * HEAD), bf16),
        ),
        grid=(steps,),
        in_specs=[
            pl.BlockSpec((heads, rows, wide), lambda i: (0, i, 0)),
            pl.BlockSpec((length, wide), lambda i: (0, 0)),
            pl.BlockSpec((HEAD, length), lambda i: (0, 0)),
            pl.BlockSpec((length, HEAD), lambda i: (0, 0)),
            pl.BlockSpec((1, heads * HEAD, rows), lambda i: (i, 0, 0)),
            pl.BlockSpec((1, heads * HEAD, rows), lambda i: (i, 0, 0)),
            pl.BlockSpec((1, 1, heads * rows), lambda i: (i, 0, 0)),
        ],
        out_specs=(by_rows, pl.BlockSpec((length, 2 * HEAD), lambda i: (0, 0))),
        scratch_shapes=[
            pltpu.VMEM((HEAD, heads * rows), f32),
            pltpu.VMEM((length, wide), f32),
            pltpu.VMEM((length, HEAD), f32),
        ],
        compiler_params=pltpu.CompilerParams(vmem_limit_bytes=40 * 2**20),
        cost_estimate=lasting(7.5),
    )(query, key, key_t, value, d_out, out, logs)


def slot_kernel(sources, unread, place_in_ref, *refs):
    row_refs, cot_refs = refs[:sources], refs[sources : 2 * sources]
    router_ref, w_ref = refs[2 * sources : 2 * sources + 2]
    refs = refs[2 * sources + 2 + unread :]
    x_ref, hid_ref, ds_ref, dgu_ref = refs[:4]
    moe_refs = refs[4 : 4 + sources]
    dsum_refs = refs[4 + sources : 4 + 2 * sources]
    moe_acc, dsum_acc, combine_ref, place_ref = refs[4 + 2 * sources :]
    expert = pl.program_id(0)
    tokens, width = row_refs[0].shape
    cap = x_ref.shape[1] // sources
    named = place_in_ref[0] + expert

    @pl.when(expert == 0)
    def _():
        moe_acc[...] = jnp.zeros_like(moe_acc)
        dsum_acc[...] = jnp.zeros_like(dsum_acc)
        for s in range(sources):
            place = cot_refs[s][:, width:].astype(f32).T[:EXPERTS]
            place_ref[s] = place
            hit = place >= 0.0
            logits = mm(router_ref[...], row_refs[s][...], NT)
            top = jnp.max(jnp.where(hit, logits, -3e38), axis=0, keepdims=True)
            grown = jnp.where(hit, jnp.exp(jnp.minimum(logits - top, 0.0)), 0.0)
            combine_ref[s] = grown / jnp.sum(grown, axis=0, keepdims=True)

    slots = lax.broadcasted_iota(jnp.int32, (cap, tokens), 0).astype(f32)
    picks, cots, slot_weights = [], [], []
    for s in range(sources):
        hit = place_ref[s, pl.ds(named, 1), :] == slots
        pick = jnp.where(hit, 1.0, 0.0).astype(bf16)
        picks.append(pick)
        x_ref[0, s * cap : (s + 1) * cap, :] = mm(pick, row_refs[s][...], NN).astype(bf16)
        cots.append(mm(pick, cot_refs[s][:, :width], NN))
        slot_weights.append(
            jnp.sum(
                jnp.where(hit, combine_ref[s, pl.ds(named, 1), :], 0.0), axis=1, keepdims=True
            )
        )
    x_rows = x_ref[0]
    cot = jnp.concatenate(cots, axis=0)
    slot_weight = jnp.concatenate(slot_weights, axis=0)
    gate_up_w = w_ref[0, :, : 2 * FFE]
    down_t = w_ref[0, :, 2 * FFE :]
    gate_up = mm(x_rows, gate_up_w, NN)
    gate = gate_up[:, :FFE]
    up = gate_up[:, FFE:]
    sig = 1.0 / (1.0 + jnp.exp(-gate))
    silu = gate * sig
    hidden = (silu * up).astype(bf16)
    hid_ref[0] = hidden
    expert_out = mm(hidden, down_t, NT).astype(bf16).astype(f32)
    d_slot = (slot_weight * cot).astype(bf16)
    ds_ref[0] = d_slot
    d_comb = jnp.sum(cot * expert_out, axis=1, keepdims=True)
    d_comb_high = d_comb.astype(bf16).astype(f32)
    lane = lax.broadcasted_iota(jnp.int32, (d_comb.shape[0], EXTRA), 1)
    extra = jnp.where(lane == named, d_comb_high, 0.0)
    extra = jnp.where(lane == named + EXPERTS, d_comb - d_comb_high, extra).astype(bf16)
    weighted = (slot_weight * expert_out).astype(bf16)
    d_hidden = mm(d_slot, down_t, NN)
    d_gate = (d_hidden * up * sig * (1.0 + gate * (1.0 - sig))).astype(bf16)
    d_up = (d_hidden * silu).astype(bf16)
    dgu_ref[0, :, :FFE] = d_gate
    dgu_ref[0, :, FFE:] = d_up
    d_row = mm(dgu_ref[0], gate_up_w, NT).astype(bf16)
    for s in range(sources):
        part = slice(s * cap, (s + 1) * cap)
        moe_acc[s] += mm(picks[s], weighted[part], TN)
        dsum_acc[s, :, :width] += mm(picks[s], d_row[part], TN)
        dsum_acc[s, :, width:] += mm(picks[s], extra[part], TN)

    @pl.when(expert == pl.num_programs(0) - 1)
    def _():
        for s in range(sources):
            moe_refs[s][0] = moe_acc[s].astype(bf16)
            dsum_refs[s][...] = dsum_acc[s].astype(bf16)


def expert_slot(place, rows, cots, router_t, weights, cap, slots, moe, needed):
    sources = len(rows)
    tokens, width = rows[0].shape
    experts = weights.shape[0]
    held = sources * cap
    carried = [*moe, *needed]
    each = lambda *shape: pl.BlockSpec((1,) + shape, lambda e, s: (e,) + (0,) * len(shape))
    fixed = lambda *shape: pl.BlockSpec(shape, lambda e, s: (0,) * len(shape))
    got = pl.pallas_call(
        functools.partial(slot_kernel, sources, len(carried)),
        out_shape=(
            jax.ShapeDtypeStruct((experts, held, width), bf16),
            jax.ShapeDtypeStruct((experts, held, FFE), bf16),
            jax.ShapeDtypeStruct((experts, held, width), bf16),
            jax.ShapeDtypeStruct((experts, held, 2 * FFE), bf16),
        )
        + (jax.ShapeDtypeStruct((slots, tokens, width), bf16),) * sources
        + (jax.ShapeDtypeStruct((tokens, width + EXTRA), bf16),) * sources,
        grid_spec=pltpu.PrefetchScalarGridSpec(
            num_scalar_prefetch=1,
            grid=(experts,),
            in_specs=[fixed(tokens, width)] * sources
            + [fixed(tokens, width + EXTRA)] * sources
            + [fixed(EXPERTS, width), each(width, 3 * FFE)]
            + [pl.BlockSpec(memory_space=pl.ANY)] * len(carried),
            out_specs=(each(held, width), each(held, FFE), each(held, width), each(held, 2 * FFE))
            + (pl.BlockSpec((1, tokens, width), lambda e, s: (s[1], 0, 0)),) * sources
            + (fixed(tokens, width + EXTRA),) * sources,
            scratch_shapes=[
                pltpu.VMEM((sources, tokens, width), f32),
                pltpu.VMEM((sources, tokens, width + EXTRA), f32),
                pltpu.VMEM((sources, EXPERTS, tokens), f32),
                pltpu.VMEM((sources, EXPERTS, tokens), f32),
            ],
        ),
        compiler_params=pltpu.CompilerParams(vmem_limit_bytes=56 * 2**20),
        cost_estimate=lasting(7.5),
        input_output_aliases={2 * sources + 3 + n: 4 + n for n in range(len(moe))},
    )(place, *rows, *cots, router_t, weights, *carried)
    return got[:4], got[4 : 4 + sources], got[4 + sources :]


def middle_kernel(
    tp_ref, got_ref, in_ref, out_ref, gain_ref, router_ref, rank_ref,
    x_ref, act_ref, mine_ref, theirs_ref, combine_ref, probs_ref, total_ref,
):
    tp = tp_ref[0]
    count = got_ref.shape[0] // 2
    gathered = lambda t: jnp.concatenate([got_ref[2 * c + t] for c in range(count)], axis=0)
    mine = gathered(tp).astype(f32).T.astype(bf16)
    theirs = gathered(tp ^ 1).astype(f32).T.astype(bf16)
    mine_ref[...] = mine
    theirs_ref[...] = theirs
    x_one = in_ref[...].astype(f32) + (mm(mine, out_ref[tp], NT) + mm(theirs, out_ref[tp ^ 1], NT))
    x_ref[...] = x_one
    inv = lax.rsqrt(jnp.mean(x_one * x_one, axis=-1, keepdims=True) + norm_eps)
    act = (x_one * inv * gain_ref[...]).astype(bf16)
    act_ref[...] = act
    logits = mm(router_ref[...], act, NT)
    grown = jnp.exp(logits - jnp.max(logits, axis=0, keepdims=True))
    probs = grown / jnp.sum(grown, axis=0, keepdims=True)
    probs_ref[...] = probs
    total_ref[...] = jnp.sum(probs, axis=1, keepdims=True)
    hit = rank_ref[...].astype(f32) >= 0.0
    top = jnp.max(jnp.where(hit, logits, -3e38), axis=0, keepdims=True)
    grown = jnp.where(hit, jnp.exp(jnp.minimum(logits - top, 0.0)), 0.0)
    combine_ref[...] = grown / jnp.sum(grown, axis=0, keepdims=True)


def middle(tp, got, inputs, out_t, gain, router_t, rank):
    rows, width = inputs.shape
    held = got.shape[0] // 2 * got.shape[1]
    shapes = [
        ((rows, width), f32),
        ((rows, width), bf16),
        ((rows, held), bf16),
        ((rows, held), bf16),
        ((EXPERTS, rows), f32),
        ((EXPERTS, rows), f32),
        ((EXPERTS, 1), f32),
    ]
    return pl.pallas_call(
        middle_kernel,
        out_shape=tuple(jax.ShapeDtypeStruct(s, d) for s, d in shapes),
        in_specs=[pl.BlockSpec(memory_space=pltpu.SMEM)]
        + [pl.BlockSpec(memory_space=pltpu.VMEM)] * 6,
        out_specs=(pl.BlockSpec(memory_space=pltpu.VMEM),) * 7,
        compiler_params=pltpu.CompilerParams(vmem_limit_bytes=40 * 2**20),
        cost_estimate=lasting(4),
    )(tp, got, inputs, out_t, gain, router_t, rank)


def return_kernel(slots, tp_ref, *refs):
    part_refs = refs[:slots]
    (
        x_ref, act_ref, combine_ref, probs_ref, aux_ref, cot_ref, gain_ref, router_ref, out_ref,
        low_ref, rest_ref, small_ref, att_ref,
    ) = refs[slots:]
    tp = tp_ref[0]
    width = x_ref.shape[1]
    total = part_refs[0][...].astype(f32)
    for part in part_refs[1:]:
        total = total + part[...].astype(f32)
    extra = total[:, width:].T
    d_combine = extra[:EXPERTS] + extra[EXPERTS : 2 * EXPERTS]
    combine = combine_ref[...]
    probs = probs_ref[...]
    aux = aux_ref[...]
    d_logits = combine * (d_combine - jnp.sum(combine * d_combine, axis=0, keepdims=True))
    d_logits = d_logits + probs * (aux - jnp.sum(probs * aux, axis=0, keepdims=True))
    d_logits = d_logits.astype(bf16)
    d_act = total[:, :width] + mm(d_logits, router_ref[...], TN)
    x_one = x_ref[...]
    inv = lax.rsqrt(jnp.mean(x_one * x_one, axis=-1, keepdims=True) + norm_eps)
    normed = x_one * inv
    scaled = d_act * gain_ref[...]
    d_x = inv * (scaled - normed * jnp.mean(scaled * normed, axis=-1, keepdims=True))
    d_x = d_x + cot_ref[...].astype(f32)
    low = d_x.astype(bf16)
    low_ref[...] = low
    rest_ref[...] = (d_x - low.astype(f32)).astype(bf16)
    mine = mm(low, out_ref[tp], NN).T.astype(bf16)
    theirs = mm(low, out_ref[tp ^ 1], NN).T.astype(bf16)
    cut = att_ref.shape[1]
    for c in range(att_ref.shape[0] // 2):
        att_ref[2 * c + tp] = mine[c * cut : (c + 1) * cut]
        att_ref[2 * c + (tp ^ 1)] = theirs[c * cut : (c + 1) * cut]
    d_router = mm(d_logits, act_ref[...], NN)
    d_gain = jnp.sum(d_act * normed, axis=0, keepdims=True)
    small = jnp.concatenate([d_router, d_gain, jnp.zeros((HEAD - EXPERTS - 1, width), f32)], axis=0)
    small = small.T
    high = small.astype(bf16).astype(f32)
    small_ref[...] = jnp.concatenate([high, small - high], axis=1).astype(bf16)


def expert_return(tp, parts, x_one, act, combine, probs, aux, cot, gain, router_t, out_t, cuts):
    rows, width = x_one.shape
    slots = len(parts)
    shapes = [
        ((rows, width), bf16),
        ((rows, width), bf16),
        ((width, 2 * HEAD), bf16),
        ((cuts, width // cuts, rows), bf16),
    ]
    return pl.pallas_call(
        functools.partial(return_kernel, slots),
        out_shape=tuple(jax.ShapeDtypeStruct(s, d) for s, d in shapes),
        in_specs=[pl.BlockSpec(memory_space=pltpu.SMEM)]
        + [pl.BlockSpec(memory_space=pltpu.VMEM)] * (slots + 9),
        out_specs=(pl.BlockSpec(memory_space=pltpu.VMEM),) * 4,
        compiler_params=pltpu.CompilerParams(vmem_limit_bytes=48 * 2**20),
        cost_estimate=lasting(7),
    )(tp, *parts, x_one, act, combine, probs, aux, cot, gain, router_t, out_t)


def out_grad_kernel(low_ref, other_low_ref, att_ref, other_att_ref, small_ref, other_small_ref, out_ref):
    held = att_ref.shape[1]
    grad = mm(low_ref[...], att_ref[...], TN) + mm(other_low_ref[...], other_att_ref[...], TN)
    out_ref[:, :held] = grad.astype(bf16)
    small = small_ref[...].astype(f32) + other_small_ref[...].astype(f32)
    small = small[:, :HEAD] + small[:, HEAD:]
    high = small.astype(bf16).astype(f32)
    out_ref[:, held:] = jnp.concatenate([high, small - high], axis=1).astype(bf16)


def out_grad(low, other_low, att, other_att, small, other_small):
    rows, width = low.shape
    held = att.shape[1]
    return pl.pallas_call(
        out_grad_kernel,
        out_shape=jax.ShapeDtypeStruct((width, held + small.shape[1]), bf16),
        in_specs=[pl.BlockSpec(memory_space=pltpu.VMEM)] * 6,
        out_specs=pl.BlockSpec(memory_space=pltpu.VMEM),
        compiler_params=pltpu.CompilerParams(vmem_limit_bytes=40 * 2**20),
        cost_estimate=lasting(3),
    )(low, other_low, att, other_att, small, other_small)


def grads_kernel(parts, *refs):
    join = lambda n: jnp.concatenate([r[0] for r in refs[n * parts : (n + 1) * parts]], axis=0)
    out_ref = refs[-1]
    out_ref[0, :, : 2 * FFE] = mm(join(0), join(1), TN).astype(bf16)
    out_ref[0, :, 2 * FFE :] = mm(join(2), join(3), TN).astype(bf16)


def expert_grads(xs, dgus, dss, hids):
    parts = len(xs)
    experts, _, width = xs[0].shape
    spec = lambda a: pl.BlockSpec((1,) + a.shape[1:], lambda e: (e, 0, 0))
    many = [*xs, *dgus, *dss, *hids]
    return pl.pallas_call(
        functools.partial(grads_kernel, parts),
        out_shape=jax.ShapeDtypeStruct((experts, width, 3 * FFE), bf16),
        grid=(experts,),
        in_specs=[spec(a) for a in many],
        out_specs=pl.BlockSpec((1, width, 3 * FFE), lambda e: (e, 0, 0)),
        compiler_params=pltpu.CompilerParams(vmem_limit_bytes=56 * 2**20),
        cost_estimate=lasting(6.6),
    )(*many)


def split_kernel(grad_ref, gu_ref, down_ref, sums_ref):
    wide = gu_ref.shape[2]
    grad = grad_ref[0].astype(f32)
    gate_up = grad[:, :wide]
    down_t = grad[:, wide:]
    gu_ref[0] = gate_up
    down = down_t.T
    down_ref[0] = down
    squares = gate_up * gate_up
    lanes = sum(squares[:, i : i + 128] for i in range(0, wide, 128))
    rows = squares.shape[0]
    sums_ref[0, :, :rows] = jnp.sum(lanes.T, axis=0, keepdims=True)
    sums_ref[0, :, rows : 2 * rows] = jnp.sum(down * down, axis=0, keepdims=True)
    sums_ref[0, :, 2 * rows : 2 * rows + wide] = jnp.sum(squares, axis=0, keepdims=True)
    sums_ref[0, :, 2 * rows + wide :] = jnp.sum(down_t * down_t, axis=0, keepdims=True)


def split(grads):
    experts, rows, wide = grads.shape
    each = lambda *shape: pl.BlockSpec((1,) + shape, lambda e: (e, 0, 0))
    return pl.pallas_call(
        split_kernel,
        out_shape=(
            jax.ShapeDtypeStruct((experts, rows, 2 * FFE), f32),
            jax.ShapeDtypeStruct((experts, FFE, rows), f32),
            jax.ShapeDtypeStruct((experts, 1, 2 * rows + 3 * FFE), f32),
        ),
        grid=(experts,),
        in_specs=[each(rows, wide)],
        out_specs=(each(rows, 2 * FFE), each(FFE, rows), each(1, 2 * rows + 3 * FFE)),
        compiler_params=pltpu.CompilerParams(vmem_limit_bytes=40 * 2**20),
        cost_estimate=lasting(4),
    )(grads)


def dense_kernel(
    at_ref, mean_ref, got_ref, qkv_ref, out_ref, router_ref, gain_ref, old_ref, colq_ref, rowo_ref, colr_ref,
    rows_tot, colq_tot, rowo_tot, last_tot, squares_ref,
):
    flat, tp = at_ref[0], at_ref[1]
    devices = got_ref.shape[0] // 2
    got = got_ref[...]
    even, odd = (
        jnp.concatenate([got[2 * n + t : 2 * n + t + 1] for n in range(devices)], axis=0)
        for t in range(2)
    )
    both = even + odd
    wide_q, wide_o = colq_tot.shape[1], rowo_tot.shape[1]
    start = wide_q + wide_o
    cut = lambda a, n: a[:, start + n * 128 : start + (n + 1) * 128]
    down = lambda a: jnp.sum(a, axis=0, keepdims=True)
    blend = lambda old, total, n: decay * old + (1.0 - decay) * (total / n + floor_sq)
    for row, half in enumerate((even, odd)):
        colq_tot[row : row + 1] = down(half[:, :wide_q])
        rowo_tot[row : row + 1] = down(half[:, wide_q:start])
    rows_tot[...] = jnp.concatenate([cut(both, 0), cut(both, 1), cut(both, 2), cut(even, 3)], axis=1)
    lane = lax.broadcasted_iota(jnp.int32, (1, 128), 1)
    last = jnp.where(lane < EXPERTS, down(cut(even, 4)), down(cut(both, 4)))
    last_tot[...] = last
    own = rows_tot[pl.ds(flat, 1), :]
    high = qkv_ref.shape[0]
    stand = lambda v: jnp.broadcast_to(v, (8, 128)).T[:high, :1]
    old = old_ref[...]
    qkv_width = (HEADS + 2 * KV_HEADS) * HEAD

    row = blend(old[0:1], own[:, :128], qkv_width)
    col = blend(colq_ref[...], colq_tot[pl.ds(tp, 1), :], D)
    mean = blend(mean_ref[0], jnp.sum(cut(both, 0)) / D, qkv_width)
    change = qkv_ref[...] * lax.rsqrt(stand(row) * col / mean)
    square_qkv = jnp.sum(change * change)
    row = blend(rowo_ref[...], rowo_tot[pl.ds(tp, 1), :], D)
    col = blend(old[1:2], own[:, 256:384], HEADS * HEAD)
    mean = blend(mean_ref[1], jnp.sum(rowo_tot[...]) / (HEADS * HEAD), D)
    change = out_ref[...] * lax.rsqrt(stand(col) * row / mean)
    square_out = jnp.sum(change * change)
    row = blend(old[2:3], own[:, 384:], EXPERTS)
    col = blend(colr_ref[...], last[:, :EXPERTS], D)
    mean = blend(mean_ref[2], jnp.sum(cut(even, 3)) / D, EXPERTS)
    change = router_ref[...] * lax.rsqrt(stand(row) * col / mean)
    square_router = jnp.sum(change * change)
    gain = own[:, 128:256]
    change = gain * lax.rsqrt(blend(old[3:4], gain * gain, 1.0))
    square_one = jnp.sum(change * change)
    gain = gain_ref[...]
    change = gain * lax.rsqrt(blend(old[4:5], gain * gain, 1.0))
    square_two = jnp.sum(change * change)
    once = jnp.where(tp == 0, 1.0, 0.0)
    squares = jnp.where(lane == 0, square_qkv, 0.0) + jnp.where(lane == 1, square_out, 0.0)
    for n, square in ((2, square_router), (3, square_one), (4, square_two)):
        squares = squares + jnp.where(lane == n, square * once, 0.0)
    squares_ref[...] = squares


def dense_moments(at, means, got, qkv, out_t, router, gain, old, col_qkv, row_out, col_router):
    devices = got.shape[0] // 2
    shapes = [(devices, 512), (2, col_qkv.shape[1]), (2, row_out.shape[1]), (1, 128), (1, 128)]
    return pl.pallas_call(
        dense_kernel,
        out_shape=tuple(jax.ShapeDtypeStruct(s, f32) for s in shapes),
        in_specs=[pl.BlockSpec(memory_space=pltpu.SMEM)] * 2
        + [pl.BlockSpec(memory_space=pltpu.VMEM)] * 9,
        out_specs=(pl.BlockSpec(memory_space=pltpu.VMEM),) * 5,
        compiler_params=pltpu.CompilerParams(vmem_limit_bytes=24 * 2**20),
        cost_estimate=lasting(4),
    )(at, means, got, qkv, out_t, router, gain, old, col_qkv, row_out, col_router)


def half_sum(parts, count):
    total = parts[0].astype(f32)
    for y in range(1, count):
        total = total + partner(parts[y], "tp", y, count).astype(f32)
    return total.astype(bf16)


def per_device(
    inputs,
    cotangent,
    routes,
    segment_ids,
    parents,
    w_qkv,
    w_out,
    w_router,
    w_gate_up,
    w_down,
    gain_attn,
    gain_moe,
    row_qkv,
    col_qkv,
    row_out,
    col_out,
    row_router,
    col_router,
    row_gate_up,
    col_gate_up,
    row_down,
    col_down,
    second_attn,
    second_moe,
):
    tp_count = lax.axis_size("tp")
    ctx_count = lax.axis_size("ctx")
    fsdp_count = lax.axis_size("fsdp")
    count = tp_count * ctx_count * fsdp_count
    tp_index = lax.axis_index("tp")
    ctx_index = lax.axis_index("ctx")
    fsdp_index = lax.axis_index("fsdp")
    flat_index = fsdp_index * ctx_count + ctx_index
    owner_index = fsdp_index * tp_count + tp_index
    keep_once = (tp_index == 0).astype(f32)
    tok_rows = inputs.shape[0]
    half_rows = tok_rows // tp_count
    tree_len = segment_ids.shape[1]
    tokens_all = tok_rows * fsdp_count * ctx_count
    capacity = half_rows * TOPK * 3 // (2 * EXPERTS)
    local_experts = EXPERTS // (fsdp_count * tp_count)
    q_own = HEADS // (tp_count * ctx_count)
    kv_own = KV_HEADS // (tp_count * ctx_count)
    assert kv_own == 1 and tp_count == 2
    q_cols = q_own * HEAD
    kv_cols = kv_own * HEAD
    own_cols = q_cols + 2 * kv_cols
    dense_rows = w_qkv.shape[0]
    qkv_cols = w_qkv.shape[1]
    dense_parts = fsdp_count * ctx_count
    ctx_rows = w_gate_up.shape[1]
    labels = jnp.arange(EXPERTS, dtype=jnp.int32)

    def by_ctx(columns):
        q_end = ctx_count * q_cols
        k_end = q_end + ctx_count * kv_cols
        lead = columns.shape[:-1]
        return jnp.concatenate(
            [
                columns[..., :q_end].reshape(lead + (ctx_count, q_cols)),
                columns[..., q_end:k_end].reshape(lead + (ctx_count, kv_cols)),
                columns[..., k_end:].reshape(lead + (ctx_count, kv_cols)),
            ],
            axis=-1,
        )

    def from_ctx(columns):
        lead = columns.shape[:-2]
        return jnp.concatenate(
            [
                columns[..., :q_cols].reshape(lead + (-1,)),
                columns[..., q_cols : q_cols + kv_cols].reshape(lead + (-1,)),
                columns[..., q_cols + kv_cols :].reshape(lead + (-1,)),
            ],
            axis=-1,
        )

    w_qkv_low = w_qkv.astype(bf16)
    extras = jnp.concatenate(
        [gain_attn.astype(bf16)[:, None], gain_moe.astype(bf16)[:, None], w_router.astype(bf16)],
        axis=1,
    )
    w_send = jnp.concatenate(
        [
            jnp.moveaxis(by_ctx(w_qkv_low), 1, 0),
            jnp.broadcast_to(extras[None], (ctx_count,) + extras.shape),
        ],
        axis=-1,
    )
    w_send = jnp.broadcast_to(w_send[None], (fsdp_count,) + w_send.shape)
    w_got = exchange(w_send.reshape((dense_parts,) + w_send.shape[2:]), ("fsdp", "ctx"))
    w_got = w_got.reshape(D, own_cols + 2 + EXPERTS)
    def spread(block):
        bit = fsdp_count // 2
        blocks = {0: block}
        while bit:
            for j in list(blocks):
                blocks[j ^ bit] = partner(blocks[j], "fsdp", bit, fsdp_count)
            bit //= 2
        near = [blocks[j] for j in range(fsdp_count)]
        return [[b] + [partner(b, "tp", y, tp_count) for y in range(1, tp_count)] for b in near]

    my_routes = lax.dynamic_slice_in_dim(routes, tp_index * half_rows, half_rows, 0)
    hit = jnp.sum((my_routes[..., None] == labels).astype(f32), axis=1)
    before = (
        jnp.arange(half_rows, dtype=jnp.int32)[:, None]
        < jnp.arange(half_rows, dtype=jnp.int32)[None, :]
    ).astype(bf16)
    rank = dot("te,tu->eu", hit.astype(bf16), before)
    rank = jnp.where(hit.T > 0.5, rank, -1.0).astype(bf16)
    riders = jnp.concatenate(
        [rank.T, jnp.broadcast_to(jnp.sum(hit, axis=0).astype(bf16), (half_rows, EXPERTS))], axis=1
    )
    riders = jnp.pad(riders, ((0, 0), (0, EXTRA - 2 * EXPERTS)))
    cot_rows = jnp.concatenate([cotangent, riders], axis=1)
    cot_near = [cot_rows]
    for j in range(1, fsdp_count):
        if fsdp_count == 4 and j == 3:
            cot_near.append(cot_rows)
        else:
            cot_near.append(partner(cot_rows, "fsdp", j, fsdp_count))

    blocks = {0: inputs}
    bit = ctx_count // 2
    while bit:
        for j in list(blocks):
            blocks[j ^ bit] = partner(blocks[j], "ctx", bit, ctx_count)
        if bit == ctx_count // 2:
            arrived = blocks[bit] = after(blocks[bit], w_got)
        bit //= 2
    blocks = [blocks[j] for j in range(ctx_count)]
    gain_one = w_got[:, own_cols].astype(f32)[None]
    gain_two = w_got[:, own_cols + 1].astype(f32)[None]
    router_t = w_got[:, own_cols + 2 :].T
    tp_at = jnp.asarray(tp_index, jnp.int32).reshape(1)

    master_sums = jnp.stack(
        [
            jnp.sum(w_qkv * w_qkv),
            jnp.sum(w_out * w_out),
            keep_once * jnp.sum(w_router * w_router),
            jnp.sum(w_gate_up * w_gate_up),
            jnp.sum(w_down * w_down),
            keep_once * jnp.sum(gain_attn * gain_attn),
            keep_once * jnp.sum(gain_moe * gain_moe),
        ]
    )
    out_rows = w_out.shape[0]
    out_t = lax.all_gather(w_out.astype(bf16).T, ("tp", "fsdp", "ctx"), axis=0, tiled=True)
    out_t = out_t.reshape(tp_count, D, out_rows)
    expert_w = jnp.concatenate(
        [w_gate_up.astype(bf16), w_down.astype(bf16).transpose(0, 2, 1)], axis=2
    )
    expert_w = lax.all_gather(after(expert_w, arrived), "ctx", axis=1, tiled=True)

    seg_hot = (segment_ids[0][:, None] == jnp.arange(HEAD, dtype=jnp.int32)).astype(bf16)
    hidden_from = jnp.pad((1.0 - ancestry(parents[0])) * -1e30, ((0, HEAD - NSEG),) * 2)
    barred = dot("qs,su->qu", seg_hot, hidden_from.astype(bf16)).astype(bf16)
    query_tie = cot_near[1:3]
    act1, query, key, key_t, value, value_t = project(
        blocks,
        jnp.asarray(ctx_index, jnp.int32).reshape(1),
        w_got,
        gain_one,
        barred,
        seg_hot,
        q_own,
        half_rows,
    )
    after_project = [after(c, key) for c in cot_near]
    if fsdp_count == 4:
        after_project[3] = partner(after_project[2], "fsdp", 1, fsdp_count)
    cot_far = [partner(c, "tp", 1, tp_count) for c in after_project]
    grad_slots = [[c, f] for c, f in zip(after_project, cot_far)]
    attended_own, logs = attention_forward(after(query, *query_tie), key, value_t, half_rows)
    counts = sum(
        c[:1, D + EXPERTS : D + 2 * EXPERTS].astype(f32) for pair in grad_slots for c in pair
    )
    bit = 1
    while bit < ctx_count:
        counts = counts + partner(counts, "ctx", bit, ctx_count)
        bit *= 2
    fraction = counts[0] / (tokens_all * TOPK)
    attended_own = after(attended_own, *cot_far[:2], after_project[3])
    attended = exchange(attended_own, ("ctx", "tp"))
    attended = after(attended, *cot_far[2:])
    inputs_half = lax.dynamic_slice_in_dim(inputs, tp_index * half_rows, half_rows, 0)
    x_one, act2, heads_own, heads_other, combine, router_probs, prob_sums = middle(
        tp_at, attended, inputs_half, out_t, gain_two, router_t, rank
    )
    w_tree = lax.all_gather(after(w_got, act2)[:, :own_cols], "ctx", axis=0, tiled=False)
    row_slots = spread(after(act2, *[pair[1] for pair in grad_slots]))

    kept, d_sums, moe_sums = [], [], []
    for j in range(fsdp_count):
        rows = list(row_slots[j])
        if j == 0:
            rows[0] = after(rows[0], row_slots[1][0])
        if j == 1:
            rows[0] = after(rows[0], row_slots[2][0])
        if j >= 2:
            rows[0] = after(rows[0], d_sums[j - 2], *(pair[0] for pair in row_slots[3:]))
        if j == 3:
            rows[0] = after(rows[0], fraction)
        place = jnp.stack([owner_index * local_experts, fsdp_index ^ j])
        held, moe_sums, d_out = expert_slot(
            place.astype(jnp.int32),
            rows,
            grad_slots[j],
            router_t,
            expert_w,
            capacity,
            fsdp_count,
            moe_sums,
            [w_tree] if j == fsdp_count - 1 else [],
        )
        kept.append(held)
        d_sums.append(half_sum(d_out, tp_count))
    d_parts = [d_sums[0]] + [partner(d_sums[j], "fsdp", j, fsdp_count) for j in range(1, fsdp_count)]
    other_heads = partner(after(heads_other, d_sums[-1]), "tp", 1, tp_count)
    d_parts[0] = after(d_parts[0], other_heads)
    xs, hids, dss, dgus = (list(part) for part in zip(*kept))
    xs[0] = after(xs[0], *d_sums[-2:])
    g_experts = expert_grads(xs, dgus, dss, hids)
    d_parts[0] = after(d_parts[0], g_experts)
    low, rest, small, d_attended = expert_return(
        tp_at,
        d_parts,
        x_one,
        act2,
        combine,
        router_probs,
        (aux_weight * EXPERTS * fraction)[:, None],
        cotangent,
        gain_two,
        router_t,
        out_t,
        ctx_count * tp_count,
    )
    d_attended = exchange(d_attended, ("ctx", "tp"))
    g_experts = lax.psum_scatter(after(g_experts, low), "ctx", scatter_dimension=1, tiled=True)
    g_gate_up, g_down, expert_sums = split(g_experts)
    expert_sums = expert_sums[:, 0]
    other_low = partner(low, "tp", 1, tp_count)
    other_small = partner(small, "tp", 1, tp_count)
    g_out_part = out_grad(low, other_low, heads_own, other_heads, small, other_small)
    d_attended = after(d_attended, g_out_part)
    g_out_got = exchange(g_out_part.reshape(dense_parts, dense_rows, -1), ("fsdp", "ctx"))
    g_out_got = jnp.sum(g_out_got.astype(f32), axis=0)
    g_out_t = g_out_got[:, :out_rows]
    g_out = g_out_t.T
    g_small = g_out_got[:, out_rows : out_rows + HEAD] + g_out_got[:, out_rows + HEAD :]
    g_router = g_small[:, :EXPERTS]
    g_gain2 = g_small[:, EXPERTS]

    moe_theirs = partner(after(moe_sums[1], d_attended), "tp", 1, tp_count)
    d_q, d_kv = attention_backward(query, key, key_t, value, d_attended, attended_own, logs)
    moe = moe_sums[0].astype(f32) + moe_theirs.astype(f32)
    moe = after(moe.astype(bf16), d_q)
    moe_rows = lax.psum_scatter(moe.reshape(-1, D), "fsdp", scatter_dimension=0, tiled=True)
    d_qkv = jnp.concatenate([d_q, d_kv], axis=1)
    g_qkv_part = after(dot("td,tc->dc", act1, d_qkv).astype(bf16), g_out_got)
    g_qkv_got = exchange(g_qkv_part.reshape(dense_parts, dense_rows, own_cols), ("fsdp", "ctx"))
    g_qkv_got = g_qkv_got.reshape(fsdp_count, ctx_count, dense_rows, own_cols).astype(f32)
    g_qkv = from_ctx(jnp.moveaxis(jnp.sum(g_qkv_got, axis=0), 0, 1))
    sq_qkv = g_qkv * g_qkv
    sq_out = g_out * g_out
    sq_router = g_router * g_router
    gain_part = jnp.sum(g_qkv * w_qkv_low.astype(f32), axis=1) / gain_attn.astype(bf16).astype(f32)
    d_qkv_send = after(d_qkv, g_qkv_got)
    d_qkv_all = exchange(d_qkv_send.reshape(ctx_count, tok_rows, own_cols), "ctx")
    d_act1_low = dot("crk,cdk->rd", d_qkv_all, w_tree).astype(bf16)
    d_act1_other = partner(d_act1_low, "tp", 1, tp_count)
    pieces = [
        jnp.sum(sq_qkv, axis=0),
        jnp.sum(sq_out, axis=1),
        jnp.sum(sq_qkv, axis=1),
        gain_part,
        jnp.sum(sq_out, axis=0),
        jnp.sum(sq_router, axis=1),
        jnp.concatenate([jnp.sum(sq_router, axis=0), prob_sums[:, 0], master_sums]),
    ]
    sizes = [p.shape[0] for p in pieces]
    padded = [-(-s // 128) * 128 for s in sizes]
    message = jnp.concatenate([jnp.pad(p, (0, n - p.shape[0])) for p, n in zip(pieces, padded)])
    message = after(message, d_qkv_all, moe)
    got = after(share(message, count), expert_sums)
    own_row_gu = expert_sums[:, :ctx_rows]
    start = (owner_index * local_experts, ctx_index * ctx_rows)
    start = tuple(jnp.asarray(s, jnp.int32) for s in start)
    rows_gu = lax.dynamic_slice(row_gate_up, start, (local_experts, ctx_rows))
    rows_gu = decay * rows_gu + (1.0 - decay) * (own_row_gu / (2 * FFE) + floor_sq)
    gu_sum = jnp.pad(jnp.sum(rows_gu, axis=1, keepdims=True), ((0, 0), (0, 127)))
    over_ctx = jnp.concatenate([expert_sums[:, 2 * ctx_rows :], gu_sum], axis=1)
    over_ctx = jnp.broadcast_to(over_ctx[None], (ctx_count,) + over_ctx.shape)
    over_ctx = jnp.sum(exchange(over_ctx, "ctx"), axis=0)
    mean_gu = over_ctx[:, 3 * FFE] / D
    own_col_gu = over_ctx[:, : 2 * FFE]
    own_row_down = over_ctx[:, 2 * FFE : 3 * FFE]
    own_col_down = expert_sums[:, ctx_rows : 2 * ctx_rows]
    first_row = (start[0], jnp.asarray(0, jnp.int32))
    cols_gu = lax.dynamic_slice(col_gate_up, first_row, (local_experts, 2 * FFE))
    cols_gu = decay * cols_gu + (1.0 - decay) * (own_col_gu / D + floor_sq)
    rows_dn = lax.dynamic_slice(row_down, first_row, (local_experts, FFE))
    rows_dn = decay * rows_dn + (1.0 - decay) * (own_row_down / D + floor_sq)
    cols_dn = lax.dynamic_slice(col_down, start, (local_experts, ctx_rows))
    cols_dn = decay * cols_dn + (1.0 - decay) * (own_col_down / FFE + floor_sq)
    mean_dn = jnp.mean(rows_dn, axis=-1)
    change_gate_up = g_gate_up * lax.rsqrt(
        rows_gu[:, :, None] * cols_gu[:, None, :] / mean_gu[:, None, None]
    )
    change_down = g_down * lax.rsqrt(
        rows_dn[:, :, None] * cols_dn[:, None, :] / mean_dn[:, None, None]
    )
    squares_gu = jnp.sum(change_gate_up * change_gate_up)
    squares_dn = jnp.sum(change_down * change_down)
    at_own = lambda a: lax.dynamic_slice_in_dim(a, flat_index * dense_rows, dense_rows, 0)
    lanes_of = lambda a: jnp.pad(a, (0, 128 - dense_rows))
    old_own = [at_own(row_qkv), at_own(col_out), at_own(row_router), second_attn, second_moe]
    old_own = jnp.pad(jnp.stack([lanes_of(a) for a in old_own]), ((0, 3), (0, 0)))
    tot_rows, tot_colq, tot_rowo, tot_last, dense_squares = dense_moments(
        jnp.stack([flat_index, tp_index]).astype(jnp.int32),
        jnp.stack([jnp.mean(row_qkv), jnp.mean(row_out), jnp.mean(row_router)]),
        got,
        g_qkv,
        g_out_t,
        g_router,
        lanes_of(g_gain2)[None],
        old_own,
        lax.dynamic_slice_in_dim(col_qkv, tp_index * qkv_cols, qkv_cols, 0)[None],
        lax.dynamic_slice_in_dim(row_out, tp_index * out_rows, out_rows, 0)[None],
        col_router[None],
    )
    square_sums = jnp.concatenate(
        [dense_squares[0, :3], squares_gu[None], squares_dn[None], dense_squares[0, 3:5]]
    )
    square_totals = jnp.sum(share(square_sums, count), axis=0)
    tot_rows, tot_colq, tot_rowo, tot_last = (
        after(t, square_totals) for t in (tot_rows, tot_colq, tot_rowo, tot_last)
    )
    piece = lambda n: tot_rows[:, n * 128 : n * 128 + dense_rows].reshape(-1)
    tot_row_qkv, tot_col_out, tot_row_router = piece(0), piece(2), piece(3)
    g_gain1 = lax.dynamic_slice_in_dim(piece(1), flat_index * dense_rows, dense_rows, 0)
    tot_col_qkv = tot_colq.reshape(-1)
    tot_row_out = tot_rowo.reshape(-1)
    tot_col_router = tot_last[0, :EXPERTS]
    last_totals = tot_last[0, EXPERTS : 2 * EXPERTS + 7]
    prob_totals = last_totals[:EXPERTS]
    master_totals = last_totals[EXPERTS:]

    d_act1 = d_act1_low.astype(f32) + after(d_act1_other, over_ctx).astype(f32)
    own_inputs = inputs.astype(f32)
    d_inputs_attn, _ = norm_backward(own_inputs, inv_rms(own_inputs), gain_one, d_act1)
    rest = after(rest, d_qkv_all)
    d_x1 = low.astype(f32) + rest.astype(f32)
    other_rest = after(partner(rest, "tp", 1, tp_count), over_ctx)
    other_x1 = other_low.astype(f32) + other_rest.astype(f32)
    d_x1 = in_order(d_x1, other_x1, tp_index, 0).reshape(tok_rows, D)
    grad_inputs = d_x1 + d_inputs_attn

    qkv_width = (HEADS + 2 * KV_HEADS) * HEAD
    row_qkv_new = decay * row_qkv + (1.0 - decay) * (tot_row_qkv / qkv_width + floor_sq)
    col_qkv_new = decay * col_qkv + (1.0 - decay) * (tot_col_qkv / D + floor_sq)
    row_out_new = decay * row_out + (1.0 - decay) * (tot_row_out / D + floor_sq)
    col_out_new = decay * col_out + (1.0 - decay) * (tot_col_out / (HEADS * HEAD) + floor_sq)
    row_router_new = decay * row_router + (1.0 - decay) * (tot_row_router / EXPERTS + floor_sq)
    col_router_new = decay * col_router + (1.0 - decay) * (tot_col_router / D + floor_sq)
    aux_loss = EXPERTS * jnp.sum(fraction * prob_totals / tokens_all)

    rows_here = lax.dynamic_slice_in_dim(row_qkv_new, flat_index * dense_rows, dense_rows, 0)
    cols_here = lax.dynamic_slice_in_dim(col_qkv_new, tp_index * qkv_cols, qkv_cols, 0)
    change_qkv = g_qkv * lax.rsqrt(rows_here[:, None] * cols_here[None, :] / jnp.mean(row_qkv_new))
    rows_here = lax.dynamic_slice_in_dim(row_out_new, tp_index * out_rows, out_rows, 0)
    cols_here = lax.dynamic_slice_in_dim(col_out_new, flat_index * dense_rows, dense_rows, 0)
    change_out = g_out * lax.rsqrt(rows_here[:, None] * cols_here[None, :] / jnp.mean(row_out_new))
    rows_here = lax.dynamic_slice_in_dim(row_router_new, flat_index * dense_rows, dense_rows, 0)
    change_router = g_router * lax.rsqrt(
        rows_here[:, None] * col_router_new[None, :] / jnp.mean(row_router_new)
    )
    second_attn_new = decay * second_attn + (1.0 - decay) * (g_gain1 * g_gain1 + floor_sq)
    second_moe_new = decay * second_moe + (1.0 - decay) * (g_gain2 * g_gain2 + floor_sq)
    change_gain1 = g_gain1 * lax.rsqrt(second_attn_new)
    change_gain2 = g_gain2 * lax.rsqrt(second_moe_new)
    quarter = lambda a: lax.dynamic_slice_in_dim(
        a, ctx_index * (a.shape[1] // ctx_count), a.shape[1] // ctx_count, 1
    )
    moments = jnp.concatenate([rows_gu, cols_dn, quarter(cols_gu), quarter(rows_dn)], axis=1)
    moments = share(after(moments, square_totals).reshape(-1), count)
    moments = moments.reshape(fsdp_count, ctx_count, tp_count, local_experts, -1)
    moments = moments.transpose(0, 2, 3, 1, 4).reshape(EXPERTS, ctx_count, -1)
    cut_at = (ctx_rows, 2 * ctx_rows, 2 * ctx_rows + 2 * FFE // ctx_count)
    row_gu_new = moments[..., : cut_at[0]].reshape(EXPERTS, D)
    col_down_new = moments[..., cut_at[0] : cut_at[1]].reshape(EXPERTS, D)
    col_gu_new = moments[..., cut_at[1] : cut_at[2]].reshape(EXPERTS, 2 * FFE)
    row_down_new = moments[..., cut_at[2] :].reshape(EXPERTS, FFE)

    entries = jnp.array(
        [
            D * qkv_width,
            HEADS * HEAD * D,
            D * EXPERTS,
            EXPERTS * D * 2 * FFE,
            EXPERTS * FFE * D,
            D,
            D,
        ],
        f32,
    )
    update_rms = jnp.sqrt(square_totals / entries)
    weight_rms = jnp.sqrt(master_totals / entries)
    step_scale = rate * weight_rms / jnp.maximum(clip_rms, update_rms)
    new_qkv = w_qkv - step_scale[0] * change_qkv
    new_out = w_out - step_scale[1] * change_out
    new_router = w_router - step_scale[2] * change_router
    new_gate_up = w_gate_up - step_scale[3] * change_gate_up
    new_down = w_down - step_scale[4] * change_down
    new_gain1 = gain_attn - step_scale[5] * change_gain1
    new_gain2 = gain_moe - step_scale[6] * change_gain2
    layer_out = (x_one + after(moe_rows, update_rms, new_gate_up, grad_inputs).astype(f32)).astype(bf16)
    return (
        layer_out,
        grad_inputs,
        aux_loss,
        g_qkv,
        g_out,
        g_router,
        g_gate_up,
        g_down,
        g_gain1,
        g_gain2,
        new_qkv,
        new_out,
        new_router,
        new_gate_up,
        new_down,
        new_gain1,
        new_gain2,
        new_qkv.astype(bf16),
        new_out.astype(bf16),
        new_router.astype(bf16),
        new_gate_up.astype(bf16),
        new_down.astype(bf16),
        new_gain1.astype(bf16),
        new_gain2.astype(bf16),
        row_qkv_new,
        col_qkv_new,
        row_out_new,
        col_out_new,
        row_router_new,
        col_router_new,
        row_gu_new,
        col_gu_new,
        row_down_new,
        col_down_new,
        second_attn_new,
        second_moe_new,
        update_rms,
    )


def solution(mesh):
    placed = (
        P(("fsdp", "ctx"), None),
        P(("fsdp", "ctx", "tp"), None),
        P(("fsdp", "ctx"), None),
        P("fsdp", None),
        P("fsdp", None),
        P(("fsdp", "ctx"), "tp"),
        P("tp", ("fsdp", "ctx")),
        P(("fsdp", "ctx"), None),
        P(("fsdp", "tp"), "ctx", None),
        P(("fsdp", "tp"), None, "ctx"),
        P(("fsdp", "ctx")),
        P(("fsdp", "ctx")),
        P(),
        P(),
        P(),
        P(),
        P(),
        P(),
        P(),
        P(),
        P(),
        P(),
        P(("fsdp", "ctx")),
        P(("fsdp", "ctx")),
    )
    return jax.shard_map(
        per_device,
        mesh=mesh,
        in_specs=placed,
        out_specs=(
            P(("fsdp", "ctx", "tp"), None),
            P(("fsdp", "ctx"), None),
            P(),
            P(("fsdp", "ctx"), "tp"),
            P("tp", ("fsdp", "ctx")),
            P(("fsdp", "ctx"), None),
            P(("fsdp", "tp"), "ctx", None),
            P(("fsdp", "tp"), None, "ctx"),
            P(("fsdp", "ctx")),
            P(("fsdp", "ctx")),
            P(("fsdp", "ctx"), "tp"),
            P("tp", ("fsdp", "ctx")),
            P(("fsdp", "ctx"), None),
            P(("fsdp", "tp"), "ctx", None),
            P(("fsdp", "tp"), None, "ctx"),
            P(("fsdp", "ctx")),
            P(("fsdp", "ctx")),
            P(("fsdp", "ctx"), "tp"),
            P("tp", ("fsdp", "ctx")),
            P(("fsdp", "ctx"), None),
            P(("fsdp", "tp"), "ctx", None),
            P(("fsdp", "tp"), None, "ctx"),
            P(("fsdp", "ctx")),
            P(("fsdp", "ctx")),
            P(),
            P(),
            P(),
            P(),
            P(),
            P(),
            P(),
            P(),
            P(),
            P(),
            P(("fsdp", "ctx")),
            P(("fsdp", "ctx")),
            P(),
        ),
        check_vma=False,
    )
```

```python
import functools

import jax
import jax.numpy as jnp
from jax import lax
from jax.experimental import pallas as pl
from jax.experimental.pallas import tpu as pltpu
from jax.sharding import PartitionSpec as P

D = 1536
HEADS = 24
KV_HEADS = 8
HEAD = 64
FFE = 512
TOPK = 8
EXPERTS = 32
NSEG = 13

norm_eps = 1e-05
decay = 0.5
floor_sq = 1e-30
rate = 0.25
clip_rms = 0.05
aux_weight = 1.0
bf16 = jnp.bfloat16
f32 = jnp.float32
EVERY = ("fsdp", "ctx", "tp")
EXTRA = 128

def lasting(microseconds):
    flops = int(microseconds * 1.15e9)
    return pl.CostEstimate(flops=flops, bytes_accessed=1, transcendentals=0)
NT = (((1,), (1,)), ((), ()))
NN = (((1,), (0,)), ((), ()))
TN = (((0,), (0,)), ((), ()))


def dot(spec, left, right):
    return jnp.einsum(spec, left, right, preferred_element_type=f32)


def exchange(values, axes):
    return lax.all_to_all(values, axes, split_axis=0, concat_axis=0, tiled=True)


def share(vector, count):
    return exchange(jnp.broadcast_to(vector[None], (count,) + vector.shape), EVERY)


def inv_rms(values):
    return lax.rsqrt(jnp.mean(values * values, axis=-1, keepdims=True) + norm_eps)


def norm_backward(values, inv, gain, d_out):
    normed = values * inv
    scaled = d_out * gain
    d_values = inv * (scaled - normed * jnp.mean(scaled * normed, axis=-1, keepdims=True))
    return d_values, normed


def ancestry(parent_row):
    seg_labels = jnp.arange(NSEG, dtype=jnp.int32)
    table = jnp.maximum(
        (seg_labels[:, None] == seg_labels[None, :]).astype(f32),
        (parent_row[:, None] == seg_labels[None, :]).astype(f32),
    )
    for sweep in range(NSEG.bit_length()):
        table = jnp.max(table[:, :, None] * table[None, :, :], axis=1)
    return table


def partner(values, axis, bits, count):
    return lax.ppermute(values, axis, [(i, i ^ bits) for i in range(count)])


def after(values, *others):
    return lax.optimization_barrier((values,) + others)[0]


def in_order(mine, other, bit, axis):
    first = jnp.where(bit == 0, mine, other)
    second = jnp.where(bit == 0, other, mine)
    return jnp.stack([first, second], axis=axis)


def mm(left, right, dims):
    return lax.dot_general(left, right, dims, preferred_element_type=f32)


def project_kernel(
    count, index_ref, *refs
):
    block_refs = refs[:count]
    w_ref, gain_ref, barred_ref, seg_ref = refs[count : count + 4]
    act_ref, q_ref, k_ref, kt_ref, v_ref, vt_ref = refs[count + 4 :]
    heads = q_ref.shape[0]
    place = pl.program_id(0) // (pl.num_programs(0) // count) ^ index_ref[0]
    block = block_refs[0][...]
    for j in range(1, count):
        block = jnp.where(place == j, block_refs[j][...], block)
    block = block.astype(f32)
    inv = lax.rsqrt(jnp.mean(block * block, axis=-1, keepdims=True) + norm_eps)
    act = (block * inv * gain_ref[...]).astype(bf16)
    act_ref[...] = act
    qkv = mm(act, w_ref[...], NN).astype(bf16).astype(f32)
    barred = barred_ref[...].astype(f32)
    for h in range(heads):
        query = qkv[:, h * HEAD : (h + 1) * HEAD] * HEAD ** (-0.5)
        q_ref[h] = jnp.concatenate([query, barred], axis=1).astype(bf16)
    key = qkv[:, heads * HEAD : (heads + 1) * HEAD]
    value = qkv[:, (heads + 1) * HEAD : (heads + 2) * HEAD]
    k_ref[...] = jnp.concatenate([key, seg_ref[...].astype(f32)], axis=1).astype(bf16)
    kt_ref[...] = key.T.astype(bf16)
    v_ref[...] = value.astype(bf16)
    vt_ref[...] = value.T.astype(bf16)


def project(blocks, index, weights, gain, barred, seg_hot, heads, rows):
    count = len(blocks)
    tok_rows, width = blocks[0].shape
    per = tok_rows // rows
    length = count * tok_rows
    wide = 2 * HEAD

    def place(j):
        def at(i, s):
            return (jnp.where((i // per ^ s[0]) == j, i % per, 0), 0)

        return at

    whole = lambda a: pl.BlockSpec(a.shape, lambda i, s: (0,) * a.ndim)
    by_rows = lambda columns: pl.BlockSpec((rows, columns), lambda i, s: (i, 0))
    return pl.pallas_call(
        functools.partial(project_kernel, count),
        out_shape=(
            jax.ShapeDtypeStruct((length, width), bf16),
            jax.ShapeDtypeStruct((heads, length, wide), bf16),
            jax.ShapeDtypeStruct((length, wide), bf16),
            jax.ShapeDtypeStruct((HEAD, length), bf16),
            jax.ShapeDtypeStruct((length, HEAD), bf16),
            jax.ShapeDtypeStruct((HEAD, length), bf16),
        ),
        grid_spec=pltpu.PrefetchScalarGridSpec(
            num_scalar_prefetch=1,
            grid=(length // rows,),
            in_specs=[pl.BlockSpec((rows, width), place(j)) for j in range(count)]
            + [whole(weights), whole(gain), by_rows(HEAD), by_rows(HEAD)],
            out_specs=(
                by_rows(width),
                pl.BlockSpec((heads, rows, wide), lambda i, s: (0, i, 0)),
                by_rows(wide),
                pl.BlockSpec((HEAD, rows), lambda i, s: (0, i)),
                by_rows(HEAD),
                pl.BlockSpec((HEAD, rows), lambda i, s: (0, i)),
            ),
        ),
        compiler_params=pltpu.CompilerParams(vmem_limit_bytes=40 * 2**20),
        cost_estimate=lasting(3.3),
    )(index, *blocks, weights, gain, barred, seg_hot)


def forward_kernel(q_ref, k_ref, vt_ref, out_ref, log_ref, acc_ref, top_ref, sum_ref):
    step = pl.program_id(0)
    heads, rows, wide = q_ref.shape
    query = q_ref[...].reshape(heads * rows, wide)
    acc_ref[...] = jnp.zeros_like(acc_ref)
    top_ref[...] = jnp.full(top_ref.shape, -3e38, f32)
    sum_ref[...] = jnp.zeros_like(sum_ref)

    def chunk(j, diagonal):
        at = pl.ds(pl.multiple_of(j * rows, rows), rows)
        scores = mm(k_ref[at, :], query, NT)
        if diagonal:
            key_at = lax.broadcasted_iota(jnp.int32, (rows, rows), 0)
            query_at = lax.broadcasted_iota(jnp.int32, (rows, rows), 1)
            later = jnp.where(key_at > query_at, -1e30, 0.0)
            scores = scores + jnp.concatenate([later] * heads, axis=1)
        top_old = top_ref[...]
        top = jnp.maximum(top_old, jnp.max(scores, axis=0, keepdims=True))
        probs = jnp.exp(scores - top)
        shrink = jnp.exp(top_old - top)
        sum_ref[...] = sum_ref[...] * shrink + jnp.sum(probs, axis=0, keepdims=True)
        acc_ref[...] = acc_ref[...] * shrink + mm(vt_ref[:, at], probs.astype(bf16), NN)
        top_ref[...] = top

    chunk(step, True)

    @pl.loop(0, step)
    def _(j):
        chunk(j, False)

    total = sum_ref[...]
    log_ref[...] = (top_ref[...] + jnp.log(total))[None]
    out = acc_ref[...] / total
    for h in range(heads):
        out_ref[0, h * HEAD : (h + 1) * HEAD, :] = out[:, h * rows : (h + 1) * rows].astype(bf16)


def attention_forward(query, key, value_t, rows):
    heads, length, wide = query.shape
    steps = length // rows
    return pl.pallas_call(
        forward_kernel,
        out_shape=(
            jax.ShapeDtypeStruct((steps, heads * HEAD, rows), bf16),
            jax.ShapeDtypeStruct((steps, 1, heads * rows), f32),
        ),
        grid=(steps,),
        in_specs=[
            pl.BlockSpec((heads, rows, wide), lambda i: (0, i, 0)),
            pl.BlockSpec((length, wide), lambda i: (0, 0)),
            pl.BlockSpec((HEAD, length), lambda i: (0, 0)),
        ],
        out_specs=(
            pl.BlockSpec((1, heads * HEAD, rows), lambda i: (i, 0, 0)),
            pl.BlockSpec((1, 1, heads * rows), lambda i: (i, 0, 0)),
        ),
        scratch_shapes=[
            pltpu.VMEM((HEAD, heads * rows), f32),
            pltpu.VMEM((1, heads * rows), f32),
            pltpu.VMEM((1, heads * rows), f32),
        ],
        compiler_params=pltpu.CompilerParams(vmem_limit_bytes=40 * 2**20),
        cost_estimate=lasting(7.5),
    )(query, key, value_t)


def backward_kernel(
    q_ref, k_ref, kt_ref, v_ref, do_ref, out_ref, log_ref, dq_ref, dkv_ref, acc_ref, dk_ref, dv_ref
):
    step = pl.program_id(0)
    heads, rows, wide = q_ref.shape
    query = q_ref[...].reshape(heads * rows, wide)
    side_by_side = lambda a: jnp.concatenate(
        [a[h * HEAD : (h + 1) * HEAD] for h in range(heads)], axis=1
    )
    d_out = side_by_side(do_ref[0])
    products = side_by_side(do_ref[0].astype(f32) * out_ref[0].astype(f32))
    delta = jnp.sum(products, axis=0, keepdims=True)
    logs = log_ref[0]

    @pl.when(step == 0)
    def _():
        dk_ref[...] = jnp.zeros_like(dk_ref)
        dv_ref[...] = jnp.zeros_like(dv_ref)

    acc_ref[...] = jnp.zeros_like(acc_ref)

    def chunk(j, diagonal):
        at = pl.ds(pl.multiple_of(j * rows, rows), rows)
        scores = mm(k_ref[at, :], query, NT)
        if diagonal:
            key_at = lax.broadcasted_iota(jnp.int32, (rows, rows), 0)
            query_at = lax.broadcasted_iota(jnp.int32, (rows, rows), 1)
            later = jnp.where(key_at > query_at, -1e30, 0.0)
            scores = scores + jnp.concatenate([later] * heads, axis=1)
        probs = jnp.exp(scores - logs)
        d_probs = mm(v_ref[at, :], d_out, NN)
        d_scores = (probs * (d_probs - delta)).astype(bf16)
        dv_ref[at, :] += mm(probs.astype(bf16), d_out, NT)
        dk_ref[at, :] += mm(d_scores, query, NN)
        acc_ref[...] += mm(kt_ref[:, at], d_scores, NN)

    chunk(step, True)

    @pl.loop(0, step)
    def _(j):
        chunk(j, False)

    out = acc_ref[...] * HEAD ** (-0.5)
    out = jnp.concatenate([out[:, h * rows : (h + 1) * rows] for h in range(heads)], axis=0)
    dq_ref[...] = out.T.astype(bf16)

    @pl.when(step == pl.num_programs(0) - 1)
    def _():
        dkv_ref[...] = jnp.concatenate([dk_ref[:, :HEAD], dv_ref[...]], axis=1).astype(bf16)


def attention_backward(query, key, key_t, value, d_out, out, logs):
    heads, length, wide = query.shape
    steps = logs.shape[0]
    rows = length // steps
    by_rows = pl.BlockSpec((rows, heads * HEAD), lambda i: (i, 0))
    return pl.pallas_call(
        backward_kernel,
        out_shape=(
            jax.ShapeDtypeStruct((length, heads * HEAD), bf16),
            jax.ShapeDtypeStruct((length, 2 * HEAD), bf16),
        ),
        grid=(steps,),
        in_specs=[
            pl.BlockSpec((heads, rows, wide), lambda i: (0, i, 0)),
            pl.BlockSpec((length, wide), lambda i: (0, 0)),
            pl.BlockSpec((HEAD, length), lambda i: (0, 0)),
            pl.BlockSpec((length, HEAD), lambda i: (0, 0)),
            pl.BlockSpec((1, heads * HEAD, rows), lambda i: (i, 0, 0)),
            pl.BlockSpec((1, heads * HEAD, rows), lambda i: (i, 0, 0)),
            pl.BlockSpec((1, 1, heads * rows), lambda i: (i, 0, 0)),
        ],
        out_specs=(by_rows, pl.BlockSpec((length, 2 * HEAD), lambda i: (0, 0))),
        scratch_shapes=[
            pltpu.VMEM((HEAD, heads * rows), f32),
            pltpu.VMEM((length, wide), f32),
            pltpu.VMEM((length, HEAD), f32),
        ],
        compiler_params=pltpu.CompilerParams(vmem_limit_bytes=40 * 2**20),
        cost_estimate=lasting(7.5),
    )(query, key, key_t, value, d_out, out, logs)


def slot_kernel(sources, unread, place_in_ref, *refs):
    row_refs, cot_refs = refs[:sources], refs[sources : 2 * sources]
    router_ref, w_ref = refs[2 * sources : 2 * sources + 2]
    refs = refs[2 * sources + 2 + unread :]
    x_ref, hid_ref, ds_ref, dgu_ref = refs[:4]
    moe_refs = refs[4 : 4 + sources]
    dsum_refs = refs[4 + sources : 4 + 2 * sources]
    moe_acc, dsum_acc, combine_ref, place_ref = refs[4 + 2 * sources :]
    expert = pl.program_id(0)
    tokens, width = row_refs[0].shape
    cap = x_ref.shape[1] // sources
    named = place_in_ref[0] + expert

    @pl.when(expert == 0)
    def _():
        moe_acc[...] = jnp.zeros_like(moe_acc)
        dsum_acc[...] = jnp.zeros_like(dsum_acc)
        for s in range(sources):
            place = cot_refs[s][:, width:].astype(f32).T[:EXPERTS]
            place_ref[s] = place
            hit = place >= 0.0
            logits = mm(router_ref[...], row_refs[s][...], NT)
            top = jnp.max(jnp.where(hit, logits, -3e38), axis=0, keepdims=True)
            grown = jnp.where(hit, jnp.exp(jnp.minimum(logits - top, 0.0)), 0.0)
            combine_ref[s] = grown / jnp.sum(grown, axis=0, keepdims=True)

    slots = lax.broadcasted_iota(jnp.int32, (cap, tokens), 0).astype(f32)
    picks, cots, slot_weights = [], [], []
    for s in range(sources):
        hit = place_ref[s, pl.ds(named, 1), :] == slots
        pick = jnp.where(hit, 1.0, 0.0).astype(bf16)
        picks.append(pick)
        x_ref[0, s * cap : (s + 1) * cap, :] = mm(pick, row_refs[s][...], NN).astype(bf16)
        cots.append(mm(pick, cot_refs[s][:, :width], NN))
        slot_weights.append(
            jnp.sum(
                jnp.where(hit, combine_ref[s, pl.ds(named, 1), :], 0.0), axis=1, keepdims=True
            )
        )
    x_rows = x_ref[0]
    cot = jnp.concatenate(cots, axis=0)
    slot_weight = jnp.concatenate(slot_weights, axis=0)
    gate_up_w = w_ref[0, :, : 2 * FFE]
    down_t = w_ref[0, :, 2 * FFE :]
    gate_up = mm(x_rows, gate_up_w, NN)
    gate = gate_up[:, :FFE]
    up = gate_up[:, FFE:]
    sig = 1.0 / (1.0 + jnp.exp(-gate))
    silu = gate * sig
    hidden = (silu * up).astype(bf16)
    hid_ref[0] = hidden
    expert_out = mm(hidden, down_t, NT).astype(bf16).astype(f32)
    d_slot = (slot_weight * cot).astype(bf16)
    ds_ref[0] = d_slot
    d_comb = jnp.sum(cot * expert_out, axis=1, keepdims=True)
    d_comb_high = d_comb.astype(bf16).astype(f32)
    lane = lax.broadcasted_iota(jnp.int32, (d_comb.shape[0], EXTRA), 1)
    extra = jnp.where(lane == named, d_comb_high, 0.0)
    extra = jnp.where(lane == named + EXPERTS, d_comb - d_comb_high, extra).astype(bf16)
    weighted = (slot_weight * expert_out).astype(bf16)
    d_hidden = mm(d_slot, down_t, NN)
    d_gate = (d_hidden * up * sig * (1.0 + gate * (1.0 - sig))).astype(bf16)
    d_up = (d_hidden * silu).astype(bf16)
    dgu_ref[0, :, :FFE] = d_gate
    dgu_ref[0, :, FFE:] = d_up
    d_row = mm(dgu_ref[0], gate_up_w, NT).astype(bf16)
    for s in range(sources):
        part = slice(s * cap, (s + 1) * cap)
        moe_acc[s] += mm(picks[s], weighted[part], TN)
        dsum_acc[s, :, :width] += mm(picks[s], d_row[part], TN)
        dsum_acc[s, :, width:] += mm(picks[s], extra[part], TN)

    @pl.when(expert == pl.num_programs(0) - 1)
    def _():
        for s in range(sources):
            moe_refs[s][0] = moe_acc[s].astype(bf16)
            dsum_refs[s][...] = dsum_acc[s].astype(bf16)


def expert_slot(place, rows, cots, router_t, weights, cap, slots, moe, needed):
    sources = len(rows)
    tokens, width = rows[0].shape
    experts = weights.shape[0]
    held = sources * cap
    carried = [*moe, *needed]
    each = lambda *shape: pl.BlockSpec((1,) + shape, lambda e, s: (e,) + (0,) * len(shape))
    fixed = lambda *shape: pl.BlockSpec(shape, lambda e, s: (0,) * len(shape))
    got = pl.pallas_call(
        functools.partial(slot_kernel, sources, len(carried)),
        out_shape=(
            jax.ShapeDtypeStruct((experts, held, width), bf16),
            jax.ShapeDtypeStruct((experts, held, FFE), bf16),
            jax.ShapeDtypeStruct((experts, held, width), bf16),
            jax.ShapeDtypeStruct((experts, held, 2 * FFE), bf16),
        )
        + (jax.ShapeDtypeStruct((slots, tokens, width), bf16),) * sources
        + (jax.ShapeDtypeStruct((tokens, width + EXTRA), bf16),) * sources,
        grid_spec=pltpu.PrefetchScalarGridSpec(
            num_scalar_prefetch=1,
            grid=(experts,),
            in_specs=[fixed(tokens, width)] * sources
            + [fixed(tokens, width + EXTRA)] * sources
            + [fixed(EXPERTS, width), each(width, 3 * FFE)]
            + [pl.BlockSpec(memory_space=pl.ANY)] * len(carried),
            out_specs=(each(held, width), each(held, FFE), each(held, width), each(held, 2 * FFE))
            + (pl.BlockSpec((1, tokens, width), lambda e, s: (s[1], 0, 0)),) * sources
            + (fixed(tokens, width + EXTRA),) * sources,
            scratch_shapes=[
                pltpu.VMEM((sources, tokens, width), f32),
                pltpu.VMEM((sources, tokens, width + EXTRA), f32),
                pltpu.VMEM((sources, EXPERTS, tokens), f32),
                pltpu.VMEM((sources, EXPERTS, tokens), f32),
            ],
        ),
        compiler_params=pltpu.CompilerParams(vmem_limit_bytes=56 * 2**20),
        cost_estimate=lasting(7.5),
        input_output_aliases={2 * sources + 3 + n: 4 + n for n in range(len(moe))},
    )(place, *rows, *cots, router_t, weights, *carried)
    return got[:4], got[4 : 4 + sources], got[4 + sources :]


def middle_kernel(
    tp_ref, got_ref, in_ref, out_ref, gain_ref, router_ref, rank_ref,
    x_ref, act_ref, mine_ref, theirs_ref, combine_ref, probs_ref, total_ref,
):
    tp = tp_ref[0]
    count = got_ref.shape[0] // 2
    gathered = lambda t: jnp.concatenate([got_ref[2 * c + t] for c in range(count)], axis=0)
    mine = gathered(tp).astype(f32).T.astype(bf16)
    theirs = gathered(tp ^ 1).astype(f32).T.astype(bf16)
    mine_ref[...] = mine
    theirs_ref[...] = theirs
    x_one = in_ref[...].astype(f32) + (mm(mine, out_ref[tp], NT) + mm(theirs, out_ref[tp ^ 1], NT))
    x_ref[...] = x_one
    inv = lax.rsqrt(jnp.mean(x_one * x_one, axis=-1, keepdims=True) + norm_eps)
    act = (x_one * inv * gain_ref[...]).astype(bf16)
    act_ref[...] = act
    logits = mm(router_ref[...], act, NT)
    grown = jnp.exp(logits - jnp.max(logits, axis=0, keepdims=True))
    probs = grown / jnp.sum(grown, axis=0, keepdims=True)
    probs_ref[...] = probs
    total_ref[...] = jnp.sum(probs, axis=1, keepdims=True)
    hit = rank_ref[...].astype(f32) >= 0.0
    top = jnp.max(jnp.where(hit, logits, -3e38), axis=0, keepdims=True)
    grown = jnp.where(hit, jnp.exp(jnp.minimum(logits - top, 0.0)), 0.0)
    combine_ref[...] = grown / jnp.sum(grown, axis=0, keepdims=True)


def middle(tp, got, inputs, out_t, gain, router_t, rank):
    rows, width = inputs.shape
    held = got.shape[0] // 2 * got.shape[1]
    shapes = [
        ((rows, width), f32),
        ((rows, width), bf16),
        ((rows, held), bf16),
        ((rows, held), bf16),
        ((EXPERTS, rows), f32),
        ((EXPERTS, rows), f32),
        ((EXPERTS, 1), f32),
    ]
    return pl.pallas_call(
        middle_kernel,
        out_shape=tuple(jax.ShapeDtypeStruct(s, d) for s, d in shapes),
        in_specs=[pl.BlockSpec(memory_space=pltpu.SMEM)]
        + [pl.BlockSpec(memory_space=pltpu.VMEM)] * 6,
        out_specs=(pl.BlockSpec(memory_space=pltpu.VMEM),) * 7,
        compiler_params=pltpu.CompilerParams(vmem_limit_bytes=40 * 2**20),
        cost_estimate=lasting(4),
    )(tp, got, inputs, out_t, gain, router_t, rank)


def return_kernel(slots, tp_ref, *refs):
    part_refs = refs[:slots]
    (
        x_ref, act_ref, combine_ref, probs_ref, aux_ref, cot_ref, gain_ref, router_ref, out_ref,
        low_ref, rest_ref, small_ref, att_ref,
    ) = refs[slots:]
    tp = tp_ref[0]
    width = x_ref.shape[1]
    total = part_refs[0][...].astype(f32)
    for part in part_refs[1:]:
        total = total + part[...].astype(f32)
    extra = total[:, width:].T
    d_combine = extra[:EXPERTS] + extra[EXPERTS : 2 * EXPERTS]
    combine = combine_ref[...]
    probs = probs_ref[...]
    aux = aux_ref[...]
    d_logits = combine * (d_combine - jnp.sum(combine * d_combine, axis=0, keepdims=True))
    d_logits = d_logits + probs * (aux - jnp.sum(probs * aux, axis=0, keepdims=True))
    d_logits = d_logits.astype(bf16)
    d_act = total[:, :width] + mm(d_logits, router_ref[...], TN)
    x_one = x_ref[...]
    inv = lax.rsqrt(jnp.mean(x_one * x_one, axis=-1, keepdims=True) + norm_eps)
    normed = x_one * inv
    scaled = d_act * gain_ref[...]
    d_x = inv * (scaled - normed * jnp.mean(scaled * normed, axis=-1, keepdims=True))
    d_x = d_x + cot_ref[...].astype(f32)
    low = d_x.astype(bf16)
    low_ref[...] = low
    rest_ref[...] = (d_x - low.astype(f32)).astype(bf16)
    mine = mm(low, out_ref[tp], NN).T.astype(bf16)
    theirs = mm(low, out_ref[tp ^ 1], NN).T.astype(bf16)
    cut = att_ref.shape[1]
    for c in range(att_ref.shape[0] // 2):
        att_ref[2 * c + tp] = mine[c * cut : (c + 1) * cut]
        att_ref[2 * c + (tp ^ 1)] = theirs[c * cut : (c + 1) * cut]
    d_router = mm(d_logits, act_ref[...], NN)
    d_gain = jnp.sum(d_act * normed, axis=0, keepdims=True)
    small = jnp.concatenate([d_router, d_gain, jnp.zeros((HEAD - EXPERTS - 1, width), f32)], axis=0)
    small = small.T
    high = small.astype(bf16).astype(f32)
    small_ref[...] = jnp.concatenate([high, small - high], axis=1).astype(bf16)


def expert_return(tp, parts, x_one, act, combine, probs, aux, cot, gain, router_t, out_t, cuts):
    rows, width = x_one.shape
    slots = len(parts)
    shapes = [
        ((rows, width), bf16),
        ((rows, width), bf16),
        ((width, 2 * HEAD), bf16),
        ((cuts, width // cuts, rows), bf16),
    ]
    return pl.pallas_call(
        functools.partial(return_kernel, slots),
        out_shape=tuple(jax.ShapeDtypeStruct(s, d) for s, d in shapes),
        in_specs=[pl.BlockSpec(memory_space=pltpu.SMEM)]
        + [pl.BlockSpec(memory_space=pltpu.VMEM)] * (slots + 9),
        out_specs=(pl.BlockSpec(memory_space=pltpu.VMEM),) * 4,
        compiler_params=pltpu.CompilerParams(vmem_limit_bytes=48 * 2**20),
        cost_estimate=lasting(7),
    )(tp, *parts, x_one, act, combine, probs, aux, cot, gain, router_t, out_t)


def out_grad_kernel(low_ref, other_low_ref, att_ref, other_att_ref, small_ref, other_small_ref, out_ref):
    held = att_ref.shape[1]
    grad = mm(low_ref[...], att_ref[...], TN) + mm(other_low_ref[...], other_att_ref[...], TN)
    out_ref[:, :held] = grad.astype(bf16)
    small = small_ref[...].astype(f32) + other_small_ref[...].astype(f32)
    small = small[:, :HEAD] + small[:, HEAD:]
    high = small.astype(bf16).astype(f32)
    out_ref[:, held:] = jnp.concatenate([high, small - high], axis=1).astype(bf16)


def out_grad(low, other_low, att, other_att, small, other_small):
    rows, width = low.shape
    held = att.shape[1]
    return pl.pallas_call(
        out_grad_kernel,
        out_shape=jax.ShapeDtypeStruct((width, held + small.shape[1]), bf16),
        in_specs=[pl.BlockSpec(memory_space=pltpu.VMEM)] * 6,
        out_specs=pl.BlockSpec(memory_space=pltpu.VMEM),
        compiler_params=pltpu.CompilerParams(vmem_limit_bytes=40 * 2**20),
        cost_estimate=lasting(3),
    )(low, other_low, att, other_att, small, other_small)


def grads_kernel(parts, *refs):
    join = lambda n: jnp.concatenate([r[0] for r in refs[n * parts : (n + 1) * parts]], axis=0)
    out_ref = refs[-1]
    out_ref[0, :, : 2 * FFE] = mm(join(0), join(1), TN).astype(bf16)
    out_ref[0, :, 2 * FFE :] = mm(join(2), join(3), TN).astype(bf16)


def expert_grads(xs, dgus, dss, hids):
    parts = len(xs)
    experts, _, width = xs[0].shape
    spec = lambda a: pl.BlockSpec((1,) + a.shape[1:], lambda e: (e, 0, 0))
    many = [*xs, *dgus, *dss, *hids]
    return pl.pallas_call(
        functools.partial(grads_kernel, parts),
        out_shape=jax.ShapeDtypeStruct((experts, width, 3 * FFE), bf16),
        grid=(experts,),
        in_specs=[spec(a) for a in many],
        out_specs=pl.BlockSpec((1, width, 3 * FFE), lambda e: (e, 0, 0)),
        compiler_params=pltpu.CompilerParams(vmem_limit_bytes=56 * 2**20),
        cost_estimate=lasting(6.6),
    )(*many)


def split_kernel(grad_ref, gu_ref, down_ref, sums_ref):
    wide = gu_ref.shape[2]
    grad = grad_ref[0].astype(f32)
    gate_up = grad[:, :wide]
    down_t = grad[:, wide:]
    gu_ref[0] = gate_up
    down = down_t.T
    down_ref[0] = down
    squares = gate_up * gate_up
    lanes = sum(squares[:, i : i + 128] for i in range(0, wide, 128))
    rows = squares.shape[0]
    sums_ref[0, :, :rows] = jnp.sum(lanes.T, axis=0, keepdims=True)
    sums_ref[0, :, rows : 2 * rows] = jnp.sum(down * down, axis=0, keepdims=True)
    sums_ref[0, :, 2 * rows : 2 * rows + wide] = jnp.sum(squares, axis=0, keepdims=True)
    sums_ref[0, :, 2 * rows + wide :] = jnp.sum(down_t * down_t, axis=0, keepdims=True)


def split(grads):
    experts, rows, wide = grads.shape
    each = lambda *shape: pl.BlockSpec((1,) + shape, lambda e: (e, 0, 0))
    return pl.pallas_call(
        split_kernel,
        out_shape=(
            jax.ShapeDtypeStruct((experts, rows, 2 * FFE), f32),
            jax.ShapeDtypeStruct((experts, FFE, rows), f32),
            jax.ShapeDtypeStruct((experts, 1, 2 * rows + 3 * FFE), f32),
        ),
        grid=(experts,),
        in_specs=[each(rows, wide)],
        out_specs=(each(rows, 2 * FFE), each(FFE, rows), each(1, 2 * rows + 3 * FFE)),
        compiler_params=pltpu.CompilerParams(vmem_limit_bytes=40 * 2**20),
        cost_estimate=lasting(4),
    )(grads)


def dense_kernel(
    at_ref, mean_ref, got_ref, qkv_ref, out_ref, router_ref, gain_ref, old_ref, colq_ref, rowo_ref, colr_ref,
    rows_tot, colq_tot, rowo_tot, last_tot, squares_ref,
):
    flat, tp = at_ref[0], at_ref[1]
    devices = got_ref.shape[0] // 2
    got = got_ref[...]
    even, odd = (
        jnp.concatenate([got[2 * n + t : 2 * n + t + 1] for n in range(devices)], axis=0)
        for t in range(2)
    )
    both = even + odd
    wide_q, wide_o = colq_tot.shape[1], rowo_tot.shape[1]
    start = wide_q + wide_o
    cut = lambda a, n: a[:, start + n * 128 : start + (n + 1) * 128]
    down = lambda a: jnp.sum(a, axis=0, keepdims=True)
    blend = lambda old, total, n: decay * old + (1.0 - decay) * (total / n + floor_sq)
    for row, half in enumerate((even, odd)):
        colq_tot[row : row + 1] = down(half[:, :wide_q])
        rowo_tot[row : row + 1] = down(half[:, wide_q:start])
    rows_tot[...] = jnp.concatenate([cut(both, 0), cut(both, 1), cut(both, 2), cut(even, 3)], axis=1)
    lane = lax.broadcasted_iota(jnp.int32, (1, 128), 1)
    last = jnp.where(lane < EXPERTS, down(cut(even, 4)), down(cut(both, 4)))
    last_tot[...] = last
    own = rows_tot[pl.ds(flat, 1), :]
    high = qkv_ref.shape[0]
    stand = lambda v: jnp.broadcast_to(v, (8, 128)).T[:high, :1]
    old = old_ref[...]
    qkv_width = (HEADS + 2 * KV_HEADS) * HEAD

    row = blend(old[0:1], own[:, :128], qkv_width)
    col = blend(colq_ref[...], colq_tot[pl.ds(tp, 1), :], D)
    mean = blend(mean_ref[0], jnp.sum(cut(both, 0)) / D, qkv_width)
    change = qkv_ref[...] * lax.rsqrt(stand(row) * col / mean)
    square_qkv = jnp.sum(change * change)
    row = blend(rowo_ref[...], rowo_tot[pl.ds(tp, 1), :], D)
    col = blend(old[1:2], own[:, 256:384], HEADS * HEAD)
    mean = blend(mean_ref[1], jnp.sum(rowo_tot[...]) / (HEADS * HEAD), D)
    change = out_ref[...] * lax.rsqrt(stand(col) * row / mean)
    square_out = jnp.sum(change * change)
    row = blend(old[2:3], own[:, 384:], EXPERTS)
    col = blend(colr_ref[...], last[:, :EXPERTS], D)
    mean = blend(mean_ref[2], jnp.sum(cut(even, 3)) / D, EXPERTS)
    change = router_ref[...] * lax.rsqrt(stand(row) * col / mean)
    square_router = jnp.sum(change * change)
    gain = own[:, 128:256]
    change = gain * lax.rsqrt(blend(old[3:4], gain * gain, 1.0))
    square_one = jnp.sum(change * change)
    gain = gain_ref[...]
    change = gain * lax.rsqrt(blend(old[4:5], gain * gain, 1.0))
    square_two = jnp.sum(change * change)
    once = jnp.where(tp == 0, 1.0, 0.0)
    squares = jnp.where(lane == 0, square_qkv, 0.0) + jnp.where(lane == 1, square_out, 0.0)
    for n, square in ((2, square_router), (3, square_one), (4, square_two)):
        squares = squares + jnp.where(lane == n, square * once, 0.0)
    squares_ref[...] = squares


def dense_moments(at, means, got, qkv, out_t, router, gain, old, col_qkv, row_out, col_router):
    devices = got.shape[0] // 2
    shapes = [(devices, 512), (2, col_qkv.shape[1]), (2, row_out.shape[1]), (1, 128), (1, 128)]
    return pl.pallas_call(
        dense_kernel,
        out_shape=tuple(jax.ShapeDtypeStruct(s, f32) for s in shapes),
        in_specs=[pl.BlockSpec(memory_space=pltpu.SMEM)] * 2
        + [pl.BlockSpec(memory_space=pltpu.VMEM)] * 9,
        out_specs=(pl.BlockSpec(memory_space=pltpu.VMEM),) * 5,
        compiler_params=pltpu.CompilerParams(vmem_limit_bytes=24 * 2**20),
        cost_estimate=lasting(4),
    )(at, means, got, qkv, out_t, router, gain, old, col_qkv, row_out, col_router)


def half_sum(parts, count):
    total = parts[0].astype(f32)
    for y in range(1, count):
        total = total + partner(parts[y], "tp", y, count).astype(f32)
    return total.astype(bf16)


def per_device(
    inputs,
    cotangent,
    routes,
    segment_ids,
    parents,
    w_qkv,
    w_out,
    w_router,
    w_gate_up,
    w_down,
    gain_attn,
    gain_moe,
    row_qkv,
    col_qkv,
    row_out,
    col_out,
    row_router,
    col_router,
    row_gate_up,
    col_gate_up,
    row_down,
    col_down,
    second_attn,
    second_moe,
):
    tp_count = lax.axis_size("tp")
    ctx_count = lax.axis_size("ctx")
    fsdp_count = lax.axis_size("fsdp")
    count = tp_count * ctx_count * fsdp_count
    tp_index = lax.axis_index("tp")
    ctx_index = lax.axis_index("ctx")
    fsdp_index = lax.axis_index("fsdp")
    flat_index = fsdp_index * ctx_count + ctx_index
    owner_index = fsdp_index * tp_count + tp_index
    keep_once = (tp_index == 0).astype(f32)
    tok_rows = inputs.shape[0]
    half_rows = tok_rows // tp_count
    tree_len = segment_ids.shape[1]
    tokens_all = tok_rows * fsdp_count * ctx_count
    capacity = half_rows * TOPK * 3 // (2 * EXPERTS)
    local_experts = EXPERTS // (fsdp_count * tp_count)
    q_own = HEADS // (tp_count * ctx_count)
    kv_own = KV_HEADS // (tp_count * ctx_count)
    assert kv_own == 1 and tp_count == 2
    q_cols = q_own * HEAD
    kv_cols = kv_own * HEAD
    own_cols = q_cols + 2 * kv_cols
    dense_rows = w_qkv.shape[0]
    qkv_cols = w_qkv.shape[1]
    dense_parts = fsdp_count * ctx_count
    ctx_rows = w_gate_up.shape[1]
    labels = jnp.arange(EXPERTS, dtype=jnp.int32)

    def by_ctx(columns):
        q_end = ctx_count * q_cols
        k_end = q_end + ctx_count * kv_cols
        lead = columns.shape[:-1]
        return jnp.concatenate(
            [
                columns[..., :q_end].reshape(lead + (ctx_count, q_cols)),
                columns[..., q_end:k_end].reshape(lead + (ctx_count, kv_cols)),
                columns[..., k_end:].reshape(lead + (ctx_count, kv_cols)),
            ],
            axis=-1,
        )

    def from_ctx(columns):
        lead = columns.shape[:-2]
        return jnp.concatenate(
            [
                columns[..., :q_cols].reshape(lead + (-1,)),
                columns[..., q_cols : q_cols + kv_cols].reshape(lead + (-1,)),
                columns[..., q_cols + kv_cols :].reshape(lead + (-1,)),
            ],
            axis=-1,
        )

    w_qkv_low = w_qkv.astype(bf16)
    extras = jnp.concatenate(
        [gain_attn.astype(bf16)[:, None], gain_moe.astype(bf16)[:, None], w_router.astype(bf16)],
        axis=1,
    )
    w_send = jnp.concatenate(
        [
            jnp.moveaxis(by_ctx(w_qkv_low), 1, 0),
            jnp.broadcast_to(extras[None], (ctx_count,) + extras.shape),
        ],
        axis=-1,
    )
    w_send = jnp.broadcast_to(w_send[None], (fsdp_count,) + w_send.shape)
    w_got = exchange(w_send.reshape((dense_parts,) + w_send.shape[2:]), ("fsdp", "ctx"))
    w_got = w_got.reshape(D, own_cols + 2 + EXPERTS)
    def spread(block):
        bit = fsdp_count // 2
        blocks = {0: block}
        while bit:
            for j in list(blocks):
                blocks[j ^ bit] = partner(blocks[j], "fsdp", bit, fsdp_count)
            bit //= 2
        near = [blocks[j] for j in range(fsdp_count)]
        return [[b] + [partner(b, "tp", y, tp_count) for y in range(1, tp_count)] for b in near]

    my_routes = lax.dynamic_slice_in_dim(routes, tp_index * half_rows, half_rows, 0)
    hit = jnp.sum((my_routes[..., None] == labels).astype(f32), axis=1)
    before = (
        jnp.arange(half_rows, dtype=jnp.int32)[:, None]
        < jnp.arange(half_rows, dtype=jnp.int32)[None, :]
    ).astype(bf16)
    rank = dot("te,tu->eu", hit.astype(bf16), before)
    rank = jnp.where(hit.T > 0.5, rank, -1.0).astype(bf16)
    riders = jnp.concatenate(
        [rank.T, jnp.broadcast_to(jnp.sum(hit, axis=0).astype(bf16), (half_rows, EXPERTS))], axis=1
    )
    riders = jnp.pad(riders, ((0, 0), (0, EXTRA - 2 * EXPERTS)))
    cot_rows = jnp.concatenate([cotangent, riders], axis=1)
    cot_near = [cot_rows]
    for j in range(1, fsdp_count):
        if fsdp_count == 4 and j == 3:
            cot_near.append(cot_rows)
        else:
            cot_near.append(partner(cot_rows, "fsdp", j, fsdp_count))

    blocks = {0: inputs}
    bit = ctx_count // 2
    while bit:
        for j in list(blocks):
            blocks[j ^ bit] = partner(blocks[j], "ctx", bit, ctx_count)
        if bit == ctx_count // 2:
            arrived = blocks[bit] = after(blocks[bit], w_got)
        bit //= 2
    blocks = [blocks[j] for j in range(ctx_count)]
    gain_one = w_got[:, own_cols].astype(f32)[None]
    gain_two = w_got[:, own_cols + 1].astype(f32)[None]
    router_t = w_got[:, own_cols + 2 :].T
    tp_at = jnp.asarray(tp_index, jnp.int32).reshape(1)

    master_sums = jnp.stack(
        [
            jnp.sum(w_qkv * w_qkv),
            jnp.sum(w_out * w_out),
            keep_once * jnp.sum(w_router * w_router),
            jnp.sum(w_gate_up * w_gate_up),
            jnp.sum(w_down * w_down),
            keep_once * jnp.sum(gain_attn * gain_attn),
            keep_once * jnp.sum(gain_moe * gain_moe),
        ]
    )
    out_rows = w_out.shape[0]
    out_t = lax.all_gather(w_out.astype(bf16).T, ("tp", "fsdp", "ctx"), axis=0, tiled=True)
    out_t = out_t.reshape(tp_count, D, out_rows)
    expert_w = jnp.concatenate(
        [w_gate_up.astype(bf16), w_down.astype(bf16).transpose(0, 2, 1)], axis=2
    )
    expert_w = lax.all_gather(after(expert_w, arrived), "ctx", axis=1, tiled=True)

    seg_hot = (segment_ids[0][:, None] == jnp.arange(HEAD, dtype=jnp.int32)).astype(bf16)
    hidden_from = jnp.pad((1.0 - ancestry(parents[0])) * -1e30, ((0, HEAD - NSEG),) * 2)
    barred = dot("qs,su->qu", seg_hot, hidden_from.astype(bf16)).astype(bf16)
    query_tie = cot_near[1:3]
    act1, query, key, key_t, value, value_t = project(
        blocks,
        jnp.asarray(ctx_index, jnp.int32).reshape(1),
        w_got,
        gain_one,
        barred,
        seg_hot,
        q_own,
        half_rows,
    )
    after_project = [after(c, key) for c in cot_near]
    if fsdp_count == 4:
        after_project[3] = partner(after_project[2], "fsdp", 1, fsdp_count)
    cot_far = [partner(c, "tp", 1, tp_count) for c in after_project]
    grad_slots = [[c, f] for c, f in zip(after_project, cot_far)]
    attended_own, logs = attention_forward(after(query, *query_tie), key, value_t, half_rows)
    counts = sum(
        c[:1, D + EXPERTS : D + 2 * EXPERTS].astype(f32) for pair in grad_slots for c in pair
    )
    bit = 1
    while bit < ctx_count:
        counts = counts + partner(counts, "ctx", bit, ctx_count)
        bit *= 2
    fraction = counts[0] / (tokens_all * TOPK)
    attended_own = after(attended_own, *cot_far[:2], after_project[3])
    attended = exchange(attended_own, ("ctx", "tp"))
    attended = after(attended, *cot_far[2:])
    inputs_half = lax.dynamic_slice_in_dim(inputs, tp_index * half_rows, half_rows, 0)
    x_one, act2, heads_own, heads_other, combine, router_probs, prob_sums = middle(
        tp_at, attended, inputs_half, out_t, gain_two, router_t, rank
    )
    w_tree = lax.all_gather(after(w_got, act2)[:, :own_cols], "ctx", axis=0, tiled=False)
    row_slots = spread(after(act2, *[pair[1] for pair in grad_slots]))

    kept, d_sums, moe_sums = [], [], []
    for j in range(fsdp_count):
        rows = list(row_slots[j])
        if j == 0:
            rows[0] = after(rows[0], row_slots[1][0])
        if j == 1:
            rows[0] = after(rows[0], row_slots[2][0])
        if j >= 2:
            rows[0] = after(rows[0], d_sums[j - 2], *(pair[0] for pair in row_slots[3:]))
        if j == 3:
            rows[0] = after(rows[0], fraction)
        place = jnp.stack([owner_index * local_experts, fsdp_index ^ j])
        held, moe_sums, d_out = expert_slot(
            place.astype(jnp.int32),
            rows,
            grad_slots[j],
            router_t,
            expert_w,
            capacity,
            fsdp_count,
            moe_sums,
            [w_tree] if j == fsdp_count - 1 else [],
        )
        kept.append(held)
        d_sums.append(half_sum(d_out, tp_count))
    d_parts = [d_sums[0]] + [partner(d_sums[j], "fsdp", j, fsdp_count) for j in range(1, fsdp_count)]
    other_heads = partner(after(heads_other, d_sums[-1]), "tp", 1, tp_count)
    d_parts[0] = after(d_parts[0], other_heads)
    xs, hids, dss, dgus = (list(part) for part in zip(*kept))
    xs[0] = after(xs[0], *d_sums[-2:])
    g_experts = expert_grads(xs, dgus, dss, hids)
    d_parts[0] = after(d_parts[0], g_experts)
    low, rest, small, d_attended = expert_return(
        tp_at,
        d_parts,
        x_one,
        act2,
        combine,
        router_probs,
        (aux_weight * EXPERTS * fraction)[:, None],
        cotangent,
        gain_two,
        router_t,
        out_t,
        ctx_count * tp_count,
    )
    d_attended = exchange(d_attended, ("ctx", "tp"))
    g_experts = lax.psum_scatter(after(g_experts, d_parts[2]), "ctx", scatter_dimension=1, tiled=True)
    g_gate_up, g_down, expert_sums = split(g_experts)
    expert_sums = expert_sums[:, 0]
    other_low = partner(low, "tp", 1, tp_count)
    other_small = partner(small, "tp", 1, tp_count)
    g_out_part = out_grad(low, other_low, heads_own, other_heads, small, other_small)
    g_out_got = exchange(g_out_part.reshape(dense_parts, dense_rows, -1), ("fsdp", "ctx"))
    g_out_got = jnp.sum(g_out_got.astype(f32), axis=0)
    g_out_t = g_out_got[:, :out_rows]
    g_out = g_out_t.T
    g_small = g_out_got[:, out_rows : out_rows + HEAD] + g_out_got[:, out_rows + HEAD :]
    g_router = g_small[:, :EXPERTS]
    g_gain2 = g_small[:, EXPERTS]

    moe_theirs = partner(after(moe_sums[1], d_attended), "tp", 1, tp_count)
    d_q, d_kv = attention_backward(query, key, key_t, value, d_attended, attended_own, logs)
    moe = moe_sums[0].astype(f32) + moe_theirs.astype(f32)
    moe = after(moe.astype(bf16), d_q)
    moe_rows = lax.psum_scatter(moe.reshape(-1, D), "fsdp", scatter_dimension=0, tiled=True)
    d_qkv = jnp.concatenate([d_q, d_kv], axis=1)
    g_qkv_part = after(dot("td,tc->dc", act1, d_qkv).astype(bf16), g_out_got)
    g_qkv_got = exchange(g_qkv_part.reshape(dense_parts, dense_rows, own_cols), ("fsdp", "ctx"))
    g_qkv_got = g_qkv_got.reshape(fsdp_count, ctx_count, dense_rows, own_cols).astype(f32)
    g_qkv = from_ctx(jnp.moveaxis(jnp.sum(g_qkv_got, axis=0), 0, 1))
    sq_qkv = g_qkv * g_qkv
    sq_out = g_out * g_out
    sq_router = g_router * g_router
    gain_part = jnp.sum(g_qkv * w_qkv_low.astype(f32), axis=1) / gain_attn.astype(bf16).astype(f32)
    d_qkv_send = after(d_qkv, g_qkv_got)
    d_qkv_all = exchange(d_qkv_send.reshape(ctx_count, tok_rows, own_cols), "ctx")
    d_act1_low = dot("crk,cdk->rd", d_qkv_all, w_tree).astype(bf16)
    d_act1_other = partner(d_act1_low, "tp", 1, tp_count)
    pieces = [
        jnp.sum(sq_qkv, axis=0),
        jnp.sum(sq_out, axis=1),
        jnp.sum(sq_qkv, axis=1),
        gain_part,
        jnp.sum(sq_out, axis=0),
        jnp.sum(sq_router, axis=1),
        jnp.concatenate([jnp.sum(sq_router, axis=0), prob_sums[:, 0], master_sums]),
    ]
    sizes = [p.shape[0] for p in pieces]
    padded = [-(-s // 128) * 128 for s in sizes]
    message = jnp.concatenate([jnp.pad(p, (0, n - p.shape[0])) for p, n in zip(pieces, padded)])
    message = after(message, d_qkv_all, moe)
    got = after(share(message, count), expert_sums)
    own_row_gu = expert_sums[:, :ctx_rows]
    start = (owner_index * local_experts, ctx_index * ctx_rows)
    start = tuple(jnp.asarray(s, jnp.int32) for s in start)
    rows_gu = lax.dynamic_slice(row_gate_up, start, (local_experts, ctx_rows))
    rows_gu = decay * rows_gu + (1.0 - decay) * (own_row_gu / (2 * FFE) + floor_sq)
    gu_sum = jnp.pad(jnp.sum(rows_gu, axis=1, keepdims=True), ((0, 0), (0, 127)))
    over_ctx = jnp.concatenate([expert_sums[:, 2 * ctx_rows :], gu_sum], axis=1)
    over_ctx = jnp.broadcast_to(over_ctx[None], (ctx_count,) + over_ctx.shape)
    over_ctx = jnp.sum(exchange(over_ctx, "ctx"), axis=0)
    mean_gu = over_ctx[:, 3 * FFE] / D
    own_col_gu = over_ctx[:, : 2 * FFE]
    own_row_down = over_ctx[:, 2 * FFE : 3 * FFE]
    own_col_down = expert_sums[:, ctx_rows : 2 * ctx_rows]
    first_row = (start[0], jnp.asarray(0, jnp.int32))
    cols_gu = lax.dynamic_slice(col_gate_up, first_row, (local_experts, 2 * FFE))
    cols_gu = decay * cols_gu + (1.0 - decay) * (own_col_gu / D + floor_sq)
    rows_dn = lax.dynamic_slice(row_down, first_row, (local_experts, FFE))
    rows_dn = decay * rows_dn + (1.0 - decay) * (own_row_down / D + floor_sq)
    cols_dn = lax.dynamic_slice(col_down, start, (local_experts, ctx_rows))
    cols_dn = decay * cols_dn + (1.0 - decay) * (own_col_down / FFE + floor_sq)
    mean_dn = jnp.mean(rows_dn, axis=-1)
    change_gate_up = g_gate_up * lax.rsqrt(
        rows_gu[:, :, None] * cols_gu[:, None, :] / mean_gu[:, None, None]
    )
    change_down = g_down * lax.rsqrt(
        rows_dn[:, :, None] * cols_dn[:, None, :] / mean_dn[:, None, None]
    )
    squares_gu = jnp.sum(change_gate_up * change_gate_up)
    squares_dn = jnp.sum(change_down * change_down)
    at_own = lambda a: lax.dynamic_slice_in_dim(a, flat_index * dense_rows, dense_rows, 0)
    lanes_of = lambda a: jnp.pad(a, (0, 128 - dense_rows))
    old_own = [at_own(row_qkv), at_own(col_out), at_own(row_router), second_attn, second_moe]
    old_own = jnp.pad(jnp.stack([lanes_of(a) for a in old_own]), ((0, 3), (0, 0)))
    tot_rows, tot_colq, tot_rowo, tot_last, dense_squares = dense_moments(
        jnp.stack([flat_index, tp_index]).astype(jnp.int32),
        jnp.stack([jnp.mean(row_qkv), jnp.mean(row_out), jnp.mean(row_router)]),
        got,
        g_qkv,
        g_out_t,
        g_router,
        lanes_of(g_gain2)[None],
        old_own,
        lax.dynamic_slice_in_dim(col_qkv, tp_index * qkv_cols, qkv_cols, 0)[None],
        lax.dynamic_slice_in_dim(row_out, tp_index * out_rows, out_rows, 0)[None],
        col_router[None],
    )
    square_sums = jnp.concatenate(
        [dense_squares[0, :3], squares_gu[None], squares_dn[None], dense_squares[0, 3:5]]
    )
    square_totals = jnp.sum(share(square_sums, count), axis=0)
    tot_rows, tot_colq, tot_rowo, tot_last = (
        after(t, square_totals) for t in (tot_rows, tot_colq, tot_rowo, tot_last)
    )
    piece = lambda n: tot_rows[:, n * 128 : n * 128 + dense_rows].reshape(-1)
    tot_row_qkv, tot_col_out, tot_row_router = piece(0), piece(2), piece(3)
    g_gain1 = lax.dynamic_slice_in_dim(piece(1), flat_index * dense_rows, dense_rows, 0)
    tot_col_qkv = tot_colq.reshape(-1)
    tot_row_out = tot_rowo.reshape(-1)
    tot_col_router = tot_last[0, :EXPERTS]
    last_totals = tot_last[0, EXPERTS : 2 * EXPERTS + 7]
    prob_totals = last_totals[:EXPERTS]
    master_totals = last_totals[EXPERTS:]

    d_act1 = d_act1_low.astype(f32) + after(d_act1_other, over_ctx).astype(f32)
    own_inputs = inputs.astype(f32)
    d_inputs_attn, _ = norm_backward(own_inputs, inv_rms(own_inputs), gain_one, d_act1)
    rest = after(rest, d_qkv_all)
    d_x1 = low.astype(f32) + rest.astype(f32)
    other_rest = after(partner(rest, "tp", 1, tp_count), over_ctx)
    other_x1 = other_low.astype(f32) + other_rest.astype(f32)
    d_x1 = in_order(d_x1, other_x1, tp_index, 0).reshape(tok_rows, D)
    grad_inputs = d_x1 + d_inputs_attn

    qkv_width = (HEADS + 2 * KV_HEADS) * HEAD
    row_qkv_new = decay * row_qkv + (1.0 - decay) * (tot_row_qkv / qkv_width + floor_sq)
    col_qkv_new = decay * col_qkv + (1.0 - decay) * (tot_col_qkv / D + floor_sq)
    row_out_new = decay * row_out + (1.0 - decay) * (tot_row_out / D + floor_sq)
    col_out_new = decay * col_out + (1.0 - decay) * (tot_col_out / (HEADS * HEAD) + floor_sq)
    row_router_new = decay * row_router + (1.0 - decay) * (tot_row_router / EXPERTS + floor_sq)
    col_router_new = decay * col_router + (1.0 - decay) * (tot_col_router / D + floor_sq)
    aux_loss = EXPERTS * jnp.sum(fraction * prob_totals / tokens_all)

    rows_here = lax.dynamic_slice_in_dim(row_qkv_new, flat_index * dense_rows, dense_rows, 0)
    cols_here = lax.dynamic_slice_in_dim(col_qkv_new, tp_index * qkv_cols, qkv_cols, 0)
    change_qkv = g_qkv * lax.rsqrt(rows_here[:, None] * cols_here[None, :] / jnp.mean(row_qkv_new))
    rows_here = lax.dynamic_slice_in_dim(row_out_new, tp_index * out_rows, out_rows, 0)
    cols_here = lax.dynamic_slice_in_dim(col_out_new, flat_index * dense_rows, dense_rows, 0)
    change_out = g_out * lax.rsqrt(rows_here[:, None] * cols_here[None, :] / jnp.mean(row_out_new))
    rows_here = lax.dynamic_slice_in_dim(row_router_new, flat_index * dense_rows, dense_rows, 0)
    change_router = g_router * lax.rsqrt(
        rows_here[:, None] * col_router_new[None, :] / jnp.mean(row_router_new)
    )
    second_attn_new = decay * second_attn + (1.0 - decay) * (g_gain1 * g_gain1 + floor_sq)
    second_moe_new = decay * second_moe + (1.0 - decay) * (g_gain2 * g_gain2 + floor_sq)
    change_gain1 = g_gain1 * lax.rsqrt(second_attn_new)
    change_gain2 = g_gain2 * lax.rsqrt(second_moe_new)
    quarter = lambda a: lax.dynamic_slice_in_dim(
        a, ctx_index * (a.shape[1] // ctx_count), a.shape[1] // ctx_count, 1
    )
    moments = jnp.concatenate([rows_gu, cols_dn, quarter(cols_gu), quarter(rows_dn)], axis=1)
    moments = share(after(moments, square_totals).reshape(-1), count)
    moments = moments.reshape(fsdp_count, ctx_count, tp_count, local_experts, -1)
    moments = moments.transpose(0, 2, 3, 1, 4).reshape(EXPERTS, ctx_count, -1)
    cut_at = (ctx_rows, 2 * ctx_rows, 2 * ctx_rows + 2 * FFE // ctx_count)
    row_gu_new = moments[..., : cut_at[0]].reshape(EXPERTS, D)
    col_down_new = moments[..., cut_at[0] : cut_at[1]].reshape(EXPERTS, D)
    col_gu_new = moments[..., cut_at[1] : cut_at[2]].reshape(EXPERTS, 2 * FFE)
    row_down_new = moments[..., cut_at[2] :].reshape(EXPERTS, FFE)

    entries = jnp.array(
        [
            D * qkv_width,
            HEADS * HEAD * D,
            D * EXPERTS,
            EXPERTS * D * 2 * FFE,
            EXPERTS * FFE * D,
            D,
            D,
        ],
        f32,
    )
    update_rms = jnp.sqrt(square_totals / entries)
    weight_rms = jnp.sqrt(master_totals / entries)
    step_scale = rate * weight_rms / jnp.maximum(clip_rms, update_rms)
    new_qkv = w_qkv - step_scale[0] * change_qkv
    new_out = w_out - step_scale[1] * change_out
    new_router = w_router - step_scale[2] * change_router
    new_gate_up = w_gate_up - step_scale[3] * change_gate_up
    new_down = w_down - step_scale[4] * change_down
    new_gain1 = gain_attn - step_scale[5] * change_gain1
    new_gain2 = gain_moe - step_scale[6] * change_gain2
    layer_out = (x_one + after(moe_rows, update_rms, new_gate_up, grad_inputs).astype(f32)).astype(bf16)
    return (
        layer_out,
        grad_inputs,
        aux_loss,
        g_qkv,
        g_out,
        g_router,
        g_gate_up,
        g_down,
        g_gain1,
        g_gain2,
        new_qkv,
        new_out,
        new_router,
        new_gate_up,
        new_down,
        new_gain1,
        new_gain2,
        new_qkv.astype(bf16),
        new_out.astype(bf16),
        new_router.astype(bf16),
        new_gate_up.astype(bf16),
        new_down.astype(bf16),
        new_gain1.astype(bf16),
        new_gain2.astype(bf16),
        row_qkv_new,
        col_qkv_new,
        row_out_new,
        col_out_new,
        row_router_new,
        col_router_new,
        row_gu_new,
        col_gu_new,
        row_down_new,
        col_down_new,
        second_attn_new,
        second_moe_new,
        update_rms,
    )


def solution(mesh):
    placed = (
        P(("fsdp", "ctx"), None),
        P(("fsdp", "ctx", "tp"), None),
        P(("fsdp", "ctx"), None),
        P("fsdp", None),
        P("fsdp", None),
        P(("fsdp", "ctx"), "tp"),
        P("tp", ("fsdp", "ctx")),
        P(("fsdp", "ctx"), None),
        P(("fsdp", "tp"), "ctx", None),
        P(("fsdp", "tp"), None, "ctx"),
        P(("fsdp", "ctx")),
        P(("fsdp", "ctx")),
        P(),
        P(),
        P(),
        P(),
        P(),
        P(),
        P(),
        P(),
        P(),
        P(),
        P(("fsdp", "ctx")),
        P(("fsdp", "ctx")),
    )
    return jax.shard_map(
        per_device,
        mesh=mesh,
        in_specs=placed,
        out_specs=(
            P(("fsdp", "ctx", "tp"), None),
            P(("fsdp", "ctx"), None),
            P(),
            P(("fsdp", "ctx"), "tp"),
            P("tp", ("fsdp", "ctx")),
            P(("fsdp", "ctx"), None),
            P(("fsdp", "tp"), "ctx", None),
            P(("fsdp", "tp"), None, "ctx"),
            P(("fsdp", "ctx")),
            P(("fsdp", "ctx")),
            P(("fsdp", "ctx"), "tp"),
            P("tp", ("fsdp", "ctx")),
            P(("fsdp", "ctx"), None),
            P(("fsdp", "tp"), "ctx", None),
            P(("fsdp", "tp"), None, "ctx"),
            P(("fsdp", "ctx")),
            P(("fsdp", "ctx")),
            P(("fsdp", "ctx"), "tp"),
            P("tp", ("fsdp", "ctx")),
            P(("fsdp", "ctx"), None),
            P(("fsdp", "tp"), "ctx", None),
            P(("fsdp", "tp"), None, "ctx"),
            P(("fsdp", "ctx")),
            P(("fsdp", "ctx")),
            P(),
            P(),
            P(),
            P(),
            P(),
            P(),
            P(),
            P(),
            P(),
            P(),
            P(("fsdp", "ctx")),
            P(("fsdp", "ctx")),
            P(),
        ),
        check_vma=False,
    )
```
